32 devices in a mesh: rows: 8 (over z, y), bank: 4 (over x, core).
Axes of the slice: x: 2, y: 2, z: 4, core: 2. Of those that a mesh axis runs over, the one named last changes fastest.
Arguments:
- hidden_in: bfloat16 [32768, 512], P(('rows', 'bank')), may hold values from -6 to 6
- lengths: int32 [32, 16], P(('rows', 'bank')), may hold values from 0 to 1024, as said below
- ln1_gain: float32 [512], replicated, may hold values from 0.1 to 1.9
- ln1_bias: float32 [512], replicated, may hold values from -3 to 3
- w_qkv: bfloat16 [512, 1536], replicated, may hold values from -0.25 to 0.25
- w_out: bfloat16 [512, 512], replicated, may hold values from -0.75 to 0.75
- b_out: float32 [512], replicated, may hold values from -3 to 3
- ln2_gain: float32 [512], replicated, may hold values from 0.1 to 1.9
- ln2_bias: float32 [512], replicated, may hold values from -3 to 3
- w_up: bfloat16 [512, 2048], replicated, may hold values from -0.25 to 0.25
- b_up: float32 [2048], replicated, may hold values from -3 to 3
- w_down: bfloat16 [2048, 512], replicated, may hold values from -0.125 to 0.125
- b_down: float32 [512], replicated, may hold values from -3 to 3
- bank: bfloat16 [8192, 512], P('bank'), may hold values from -6 to 6
- bank_labels: int32 [8192], P('bank'), may hold values from 0 to 203
- target_slots: int32 [32768], P(('rows', 'bank')), may hold values from 0 to 8191
- gold_ids: int32 [32768], P(('rows', 'bank')), may hold values from 0 to 203
Outputs:
- block_out: bfloat16 [32768, 512], P(('rows', 'bank'))
- token_loss: float32 [32768], P(('rows', 'bank'))
- input_grad: bfloat16 [32768, 512], P(('rows', 'bank'))
- ln1_gain_grad: float32 [512], replicated
- ln1_bias_grad: float32 [512], replicated
- w_qkv_grad: float32 [512, 1536], replicated
- w_out_grad: float32 [512, 512], replicated
- b_out_grad: float32 [512], replicated
- ln2_gain_grad: float32 [512], replicated
- ln2_bias_grad: float32 [512], replicated
- w_up_grad: float32 [512, 2048], replicated
- b_up_grad: float32 [2048], replicated
- w_down_grad: float32 [2048, 512], replicated
- b_down_grad: float32 [512], replicated
The draws below stay inside these ranges and needn't reach their ends.
Inputs may be any that keep to these rules, and one draw needn't show every extreme that they name: Each row's lengths sum to at most 1024; zeros may follow the last document; in some row one document fills all 1024 slots.
All inputs are finite; a program needn't handle non-finite values.
Results may differ from the reference program's by a relative error of at most 0.01225.
Values may be sent and summed in bfloat16 or wider, within the bound.
No kernel may reach another device: no remote copies, remote signals or barrier semaphores. Data moves between devices by JAX's collectives and lax.ppermute only.
A program may use at most 256 MiB of HBM per device.

```python
import math
import jax
import jax.numpy as jnp
from jax import lax

D = 512
HEADS = 8
HEAD_DIM = 64
FF = 2048
VOCAB = 204
CAP = 1024
DOCS = 16
GROUPS = 32
TOKENS = 32768
SLOTS = 8192


def draw_lengths(key, part):
    key = jax.random.fold_in(key, 11)
    total_key, cut_key, pick_key = jax.random.split(key, 3)
    totals = jax.random.randint(total_key, (GROUPS, 1), CAP // 4, CAP + 1)
    cut_points = jax.random.randint(cut_key, (GROUPS, DOCS - 1), 0, CAP + 1)
    cut_points = jnp.sort(jnp.minimum(cut_points, totals), axis=1)
    bounds = jnp.concatenate([jnp.zeros((GROUPS, 1), jnp.int32), cut_points, totals], axis=1)
    doc_lengths = bounds[:, 1:] - bounds[:, :-1]
    chosen = jax.random.randint(pick_key, (), 0, GROUPS)
    whole_row = jnp.zeros((DOCS,), jnp.int32).at[0].set(CAP)
    return jnp.where((jnp.arange(GROUPS) == chosen)[:, None], whole_row[None, :], doc_lengths).astype(jnp.int32)


def place_ends(drawn, stream_key, least, top_value):
    extent = drawn.shape
    place = [jax.random.randint(jax.random.fold_in(stream_key, axis), (), 0, extent[axis]) for axis in range(len(extent))]
    drawn = drawn.at[tuple(place)].set(least)
    longest = extent.index(max(extent))
    place[longest] = (place[longest] + 1) % extent[longest]
    return drawn.at[tuple(place)].set(top_value)


def levels(rng, dims, shards, least, top_value):
    loudness = 1.0
    for position, shards_of in shards:
        heights = jax.random.uniform(jax.random.fold_in(jax.random.fold_in(rng, 6), position), (shards_of,), jnp.float32, least / len(shards), top_value / len(shards))
        loudness = loudness * jnp.repeat(jnp.exp(heights), dims[position] // shards_of).reshape((-1,) + (1,) * (len(dims) - 1 - position))
    return loudness


def scatter_about(key, extent, deviation, most, shards=(), kind=jnp.bfloat16):
    array = jax.random.normal(key, extent, jnp.float32) * deviation
    if len(shards) > 0:
        array = levels(key, extent, shards, -0.22, 0.18) * array
    return jnp.clip(array, min=-most, max=most).astype(kind)


def setup_inputs(seed: int = 0) -> dict:
    key_of = jax.random.split(jax.random.key(seed), 18)
    return {
        "hidden_in": scatter_about(key_of[0], (TOKENS, D), 1.0, 6.0, ((0, 32),)),
        "lengths": draw_lengths(jax.random.fold_in(key_of[17], 71), 0),
        "ln1_gain": jnp.clip(1.0 + 0.18 * jax.random.normal(key_of[2], (D,), jnp.float32), 0.1, 1.9),
        "ln1_bias": scatter_about(key_of[3], (D,), 0.3, 3.0, (), jnp.float32),
        "w_qkv": scatter_about(key_of[4], (D, 3 * D), D ** -0.5, 0.25),
        "w_out": scatter_about(key_of[5], (D, D), (D // 8) ** -0.5, 0.75),
        "b_out": scatter_about(key_of[6], (D,), 0.3, 3.0, (), jnp.float32),
        "ln2_gain": jnp.clip(1.0 + 0.18 * jax.random.normal(key_of[7], (D,), jnp.float32), 0.1, 1.9),
        "ln2_bias": scatter_about(key_of[8], (D,), 0.3, 3.0, (), jnp.float32),
        "w_up": scatter_about(key_of[9], (D, FF), D ** -0.5, 0.25),
        "b_up": scatter_about(key_of[10], (FF,), 0.5, 3.0, (), jnp.float32),
        "w_down": scatter_about(key_of[11], (FF, D), FF ** -0.5, 0.125),
        "b_down": scatter_about(key_of[12], (D,), 0.3, 3.0, (), jnp.float32),
        "bank": scatter_about(key_of[13], (SLOTS, D), 1.0, 6.0, ((0, 4),)),
        "bank_labels": place_ends(jax.random.randint(key_of[14], (SLOTS,), 0, VOCAB), jax.random.fold_in(key_of[14], 1), 0, VOCAB - 1).astype(jnp.int32),
        "target_slots": place_ends(jax.random.randint(key_of[15], (TOKENS,), 0, SLOTS), jax.random.fold_in(key_of[15], 1), 0, SLOTS - 1).astype(jnp.int32),
        "gold_ids": place_ends(jax.random.randint(key_of[16], (TOKENS,), 0, VOCAB), jax.random.fold_in(key_of[16], 1), 0, VOCAB - 1).astype(jnp.int32),
    }


@jax.custom_vjp
def low(v):
    return lax.optimization_barrier(v.astype(jnp.bfloat16)).astype(jnp.float32)

@jax.custom_vjp
def low_back(v):
    return v

def low_keep(v):
    return (low(v), None)

def low_pass(kept, grad):
    return (grad,)

def back_keep(v):
    return (v, None)

def back_low(kept, grad):
    return (low(grad),)
low.defvjp(low_keep, low_pass)
low_back.defvjp(back_keep, back_low)

def layout(lengths_row, length):
    doc_ends = jnp.cumsum(lengths_row)
    places = jnp.arange(length, dtype=jnp.int32)
    passed = (places[:, None] >= doc_ends[None, :]).astype(jnp.int32)
    segment = lax.optimization_barrier(jnp.sum(passed, axis=1))
    begins = lax.optimization_barrier(jnp.sum(passed * lengths_row[None, :], axis=1))
    return (segment, places - begins, places < doc_ends[-1])

def sinusoid(offset, width):
    half_idx = jnp.arange(width // 2, dtype=jnp.float32)
    inv_freq = jnp.exp(half_idx * (-2.0 * math.log(10000.0) / width))
    angles = offset.astype(jnp.float32)[:, None] * inv_freq[None, :]
    return jnp.concatenate([jnp.sin(angles), jnp.cos(angles)], axis=1)

def normed(values, gain_row, shift_row):
    center = values - lax.optimization_barrier(jnp.mean(values, axis=-1, keepdims=True))
    spread = lax.optimization_barrier(jnp.mean(center * center, axis=-1, keepdims=True))
    return center * lax.rsqrt(spread + 1e-05) * gain_row + shift_row

def block_forward(params_all, stream_in, lengths_row):
    ln1_gain, ln1_bias, w_qkv, w_out, b_out, ln2_gain, ln2_bias, w_up, b_up, w_down, b_down = params_all
    highest = lax.Precision.HIGHEST
    segment, offset, live_flag = layout(lengths_row, CAP)
    stream = stream_in + sinusoid(offset, D)
    normed_a = low(normed(stream, ln1_gain, ln1_bias))
    projected = low(low_back(jnp.dot(normed_a, w_qkv, precision=highest)))
    queries = projected[:, :D].reshape(CAP, HEADS, HEAD_DIM)
    keys_all = projected[:, D:2 * D].reshape(CAP, HEADS, HEAD_DIM)
    values_all = projected[:, 2 * D:].reshape(CAP, HEADS, HEAD_DIM)
    places = jnp.arange(CAP, dtype=jnp.int32)
    allowed = (places[:, None] >= places[None, :]) & (segment[:, None] == segment[None, :])
    scores = low_back(jnp.einsum('qhd,khd->hqk', queries, keys_all, precision=highest) / math.sqrt(HEAD_DIM))
    scores = jnp.where(allowed[None], scores, -1e+30)
    soft_weights = low(jax.nn.softmax(scores, axis=-1))
    attn_mixed = low(low_back(jnp.einsum('hqk,khd->qhd', soft_weights, values_all, precision=highest).reshape(CAP, D)))
    after_attn = stream + low_back(jnp.dot(attn_mixed, w_out, precision=highest)) + b_out
    normed_c = low(normed(after_attn, ln2_gain, ln2_bias))
    hidden = low_back(jnp.dot(normed_c, w_up, precision=highest)) + b_up
    activated = low(jax.nn.gelu(hidden, approximate=False))
    result = after_attn + low_back(jnp.dot(activated, w_down, precision=highest)) + b_down
    return (result, live_flag.astype(jnp.float32))

def reference(hidden_in, lengths, ln1_gain, ln1_bias, w_qkv, w_out, b_out, ln2_gain, ln2_bias, w_up, b_up, w_down, b_down, bank, bank_labels, target_slots, gold_ids):
    highest = lax.Precision.HIGHEST
    params_all = jax.tree.map(lambda leaf_value: leaf_value.astype(jnp.float32), (ln1_gain, ln1_bias, w_qkv, w_out, b_out, ln2_gain, ln2_bias, w_up, b_up, w_down, b_down))
    inputs_f = hidden_in.astype(jnp.float32).reshape(GROUPS, CAP, D)
    bank_f = bank.astype(jnp.float32)
    slot_ids = jnp.arange(SLOTS, dtype=jnp.int32)
    targets = target_slots.reshape(GROUPS, CAP)
    gold_blocks = gold_ids.reshape(GROUPS, CAP)

    def objective(params_now, inputs_now):

        def run_block(block_pair):
            return block_forward(params_now, block_pair[0], block_pair[1])
        results, live_blocks = lax.map(jax.checkpoint(run_block), (inputs_now, lengths))

        def score_block(block_group):
            block_rows, target_rows, gold_rows, live_rows = block_group
            scores = low_back(jnp.dot(low(block_rows), bank_f.T, precision=highest) / math.sqrt(D))
            positive = (bank_labels[None, :] == gold_rows[:, None]) | (slot_ids[None, :] == target_rows[:, None])
            lse_all = jax.scipy.special.logsumexp(scores, axis=1)
            lse_pos = jax.scipy.special.logsumexp(jnp.where(positive, scores, -1e+30), axis=1)
            return (lse_all - lse_pos) * live_rows
        losses = lax.map(jax.checkpoint(score_block), (results, targets, gold_blocks, live_blocks))
        return (jnp.sum(losses), (results, losses))
    objective_value, pull_back, (results, losses) = jax.vjp(objective, params_all, inputs_f, has_aux=True)
    grad_params, grad_inputs = pull_back(jnp.ones((), jnp.float32))
    return (results.reshape(TOKENS, D).astype(jnp.bfloat16), losses.reshape(TOKENS), grad_inputs.reshape(TOKENS, D).astype(jnp.bfloat16), grad_params[0], grad_params[1], grad_params[2], grad_params[3], grad_params[4], grad_params[5], grad_params[6], grad_params[7], grad_params[8], grad_params[9], grad_params[10])
```

```python
import functools
import math

import jax
import jax.numpy as jnp
import numpy as np
from jax import lax
from jax.experimental import pallas as pl
from jax.experimental.pallas import tpu as pltpu
from jax.sharding import PartitionSpec as P

LOG2E = 1.4426950408889634
LN2 = 0.6931471805599453
NT = (((1,), (1,)), ((), ()))
NN = (((1,), (0,)), ((), ()))
f32, bf16 = jnp.float32, jnp.bfloat16

def column(row, rows):
    return jnp.transpose(jnp.broadcast_to(row.astype(f32), (128, rows)))[:, :1]

def bank_kernel(lengths_ref, q_ref, gold_ref, target_ref, labels_ref, bank_hbm,
                grad_ref, loss_ref, bsum_ref,
                bank_ref, s0_ref, s1_ref, e_ref, max_ref, sems, *, rows, tile, docs):
    step = pl.program_id(0)
    slots, width = bank_ref.shape
    tiles = slots // tile
    c = LOG2E / math.sqrt(width)
    copies = [pltpu.make_async_copy(bank_hbm.at[pl.ds(j * tile, tile)], bank_ref.at[pl.ds(j * tile, tile)], sems.at[j]) for j in range(tiles)]

    @pl.when(step == 0)
    def _():
        for j in range(tiles):
            copies[j].start()

    total = lengths_ref[0, 0]
    for j in range(1, docs):
        total = total + lengths_ref[0, j]
    gold = column(gold_ref[...], rows)
    target = column(target_ref[...], rows)
    gold_b = jnp.broadcast_to(gold, (rows, 128)).astype(jnp.int32)
    target_b = jnp.broadcast_to(target, (rows, 128)).astype(jnp.int32)
    place = step * rows + lax.broadcasted_iota(jnp.int32, (rows, 1), 0)
    live = place < total
    q = q_ref[...]
    lane = lax.broadcasted_iota(jnp.int32, (1, tile), 1)

    def wide(col):
        return jnp.concatenate([col] * (tile // 128), axis=1)

    def positive_of(j):
        labels = labels_ref[j]
        return (labels == wide(gold_b)) | ((lane + j * tile) == wide(target_b))

    def scores(j):
        return lax.dot_general(q, bank_ref[pl.ds(j * tile, tile), :], NT, preferred_element_type=f32)

    def fold(x):
        out = x[:, :128]
        for i in range(1, tile // 128):
            out = out + x[:, i * 128:(i + 1) * 128]
        return out

    def fold_max(x):
        out = x[:, :128]
        for i in range(1, tile // 128):
            out = jnp.maximum(out, x[:, i * 128:(i + 1) * 128])
        return out

    def eat(j, s_ref, top, sum_all, sum_pos):
        s = s_ref[...]
        here = jnp.max(fold_max(s), axis=1, keepdims=True) * c
        new_top = jnp.maximum(top, here)
        shrink = jnp.exp2(top - new_top)
        e = jnp.exp2(s * c - new_top)
        pos = positive_of(j)
        sum_all = sum_all * shrink + fold(e)
        sum_pos = sum_pos * shrink + fold(jnp.where(pos, e, 0.0))
        e_ref[j] = e.astype(e_ref.dtype)
        max_ref[j] = new_top
        return new_top, sum_all, sum_pos

    @pl.when(step == 0)
    def _():
        copies[0].wait()
    s0_ref[...] = scores(0)
    state = (jnp.full((rows, 1), -1e30, f32), jnp.zeros((rows, 128), f32), jnp.zeros((rows, 128), f32))

    bufs = (s0_ref, s1_ref)
    for j in range(tiles):
        if j + 1 < tiles:
            @pl.when(step == 0)
            def _():
                copies[j + 1].wait()
            bufs[(j + 1) % 2][...] = scores(j + 1)
        state = eat(j, bufs[j % 2], *state)
    top, sum_all, sum_pos = state
    sum_all = jnp.sum(sum_all, axis=1, keepdims=True)
    sum_pos = jnp.sum(sum_pos, axis=1, keepdims=True)
    safe = jnp.min(sum_pos) >= 2.0 ** -60
    lse_all = top + jnp.log2(sum_all)

    def finish(loss, acc):
        loss_ref[...] = jnp.transpose(jnp.broadcast_to(jnp.where(live, loss, 0.0), (rows, 128)))[:1, :]
        acc = acc * (1.0 / math.sqrt(width))
        grad_ref[...] = acc
        part = jnp.sum(acc, axis=0, keepdims=True)
        bsum_ref[...] = jnp.where(step == 0, part, bsum_ref[...] + part)

    @pl.when(safe)
    def _():
        lse_pos = top + jnp.log2(sum_pos)
        inv_all = jnp.where(live, 1.0 / sum_all, 0.0)
        inv_diff = inv_all - jnp.where(live, 1.0 / sum_pos, 0.0)
        acc = jnp.zeros((rows, width), f32)
        for j in range(tiles):
            factor = jnp.exp2(max_ref[j] - top)
            on = jnp.broadcast_to(factor * inv_diff, (rows, 128))
            off = jnp.broadcast_to(factor * inv_all, (rows, 128))
            g = e_ref[j].astype(f32) * jnp.where(positive_of(j), wide(on), wide(off))
            acc = acc + lax.dot_general(g.astype(bf16), bank_ref[pl.ds(j * tile, tile), :], NN, preferred_element_type=f32)
        finish((lse_all - lse_pos) * LN2, acc)

    @pl.when(jnp.logical_not(safe))
    def _():
        def pos_top(j, best):
            masked = jnp.where(positive_of(j), scores(j) * c, -1e30)
            return jnp.maximum(best, jnp.max(masked, axis=1, keepdims=True))
        top_pos = lax.fori_loop(0, tiles, pos_top, jnp.full((rows, 1), -1e30, f32))

        def pos_sum(j, total_pos):
            x = jnp.where(positive_of(j), scores(j) * c, -1e30)
            return total_pos + jnp.sum(jnp.exp2(x - top_pos), axis=1, keepdims=True)
        lse_pos = top_pos + jnp.log2(lax.fori_loop(0, tiles, pos_sum, jnp.zeros((rows, 1), f32)))
        cut_all = jnp.where(live, lse_all, 1e30)
        cut_pos = jnp.where(live, lse_pos, 1e30)

        def pull(j, acc):
            s = scores(j) * c
            g = jnp.exp2(s - cut_all) - jnp.exp2(jnp.where(positive_of(j), s, -1e30) - cut_pos)
            return acc + lax.dot_general(g.astype(bf16), bank_ref[pl.ds(j * tile, tile), :], NN, preferred_element_type=f32)
        finish((lse_all - lse_pos) * LN2, lax.fori_loop(0, tiles, pull, jnp.zeros((rows, width), f32)))

def bank_call(lengths, q, gold, target, labels, bank, *, rows=512, tile=1024, edt=bf16):
    length, width = q.shape
    slots = bank.shape[0]
    tiles = slots // tile
    docs = lengths.shape[1]
    return pl.pallas_call(
        functools.partial(bank_kernel, rows=rows, tile=tile, docs=docs),
        grid=(length // rows,),
        in_specs=[
            pl.BlockSpec(memory_space=pltpu.SMEM),
            pl.BlockSpec((rows, width), lambda i: (i, 0)),
            pl.BlockSpec((1, rows), lambda i: (0, i)),
            pl.BlockSpec((1, rows), lambda i: (0, i)),
            pl.BlockSpec((tiles, 1, tile), lambda i: (0, 0, 0)),
            pl.BlockSpec(memory_space=pl.ANY),
        ],
        out_specs=[
            pl.BlockSpec((rows, width), lambda i: (i, 0)),
            pl.BlockSpec((1, rows), lambda i: (0, i)),
            pl.BlockSpec((1, width), lambda i: (0, 0)),
        ],
        out_shape=[
            jax.ShapeDtypeStruct((length, width), f32),
            jax.ShapeDtypeStruct((1, length), f32),
            jax.ShapeDtypeStruct((1, width), f32),
        ],
        scratch_shapes=[
            pltpu.VMEM((slots, width), bf16),
            pltpu.VMEM((rows, tile), f32),
            pltpu.VMEM((rows, tile), f32),
            pltpu.VMEM((tiles, rows, tile), edt),
            pltpu.VMEM((tiles, rows, 1), f32),
            pltpu.SemaphoreType.DMA((tiles,)),
        ],
        compiler_params=pltpu.CompilerParams(vmem_limit_bytes=56 * 2 ** 20),
        name="bank",
    )(lengths, q, gold.reshape(1, length), target.reshape(1, length), labels.reshape(tiles, 1, tile), bank)

TN = (((0,), (0,)), ((), ()))
BIG = 1e30
STAT = 120
NEG = -1e30

def doc_bounds(lengths_ref, docs):
    lane = lax.broadcasted_iota(jnp.int32, (1, 128), 1)
    begin = jnp.zeros((1, 128), jnp.int32)
    end = jnp.zeros((1, 128), jnp.int32)
    at = jnp.int32(0)
    for j in range(docs):
        begin = jnp.where(lane == j, at, begin)
        at = at + lengths_ref[0, j]
        end = jnp.where(lane == j, at, end)
    begin = jnp.where(lane == docs, at, begin)
    end = jnp.where(lane == docs, 2 ** 30, end)
    return begin, end, at

def one_hot_docs(lengths_ref, docs, length):
    begin, end, _ = doc_bounds(lengths_ref, docs)
    place = lax.broadcasted_iota(jnp.int32, (length, 128), 0)
    return (place >= begin) & (place < end)

def split3(col):
    hi = col.astype(bf16).astype(f32)
    mid = (col - hi).astype(bf16).astype(f32)
    lo = col - hi - mid
    return hi, mid, lo

def with_stat(base, col, lane):
    hi, mid, lo = split3(col)
    return jnp.where(lane == STAT, hi, jnp.where(lane == STAT + 1, mid, jnp.where(lane == STAT + 2, lo, base))).astype(bf16)

def key_marks(hot, lane):
    ones = (lane >= STAT) & (lane < STAT + 3)
    return jnp.where(ones, 1.0, jnp.where(hot, 0.0, -BIG)).astype(bf16)

def attn_fwd_kernel(lengths_ref, q_ref, k_ref, v_ref, mixed_ref, lse_ref, aug_q, aug_k, kk, *, docs, dim, block):
    pair = pl.program_id(0)
    length = q_ref.shape[0]
    lane = lax.broadcasted_iota(jnp.int32, (1, 128), 1)

    @pl.when(pair == 0)
    def _():
        hot = one_hot_docs(lengths_ref, docs, length)
        marks = lane < docs + 1
        aug_q[...] = jnp.where(hot & marks, 1.0, 0.0).astype(bf16)
        aug_k[...] = key_marks(hot, lane)
        lse_ref[...] = jnp.zeros_like(lse_ref)

    kk[:, :128] = k_ref[...]
    kk[:, 128:] = aug_k[...]
    scale = 1.0 / math.sqrt(dim)
    first = lane < dim
    row = lax.broadcasted_iota(jnp.int32, (block, block), 0)
    col = lax.broadcasted_iota(jnp.int32, (block, block), 1)
    causal = row >= col
    for b in range(length // block):
        rows = pl.ds(b * block, block)
        q2 = q_ref[rows, :].astype(f32) * scale
        outs, lses = [], []
        for h in range(2):
            mine = first if h == 0 else jnp.logical_not(first)
            qq = jnp.concatenate([jnp.where(mine, q2, 0.0).astype(bf16), aug_q[rows, :]], axis=1)
            s_diag = lax.dot_general(qq, kk[rows, :], NT, preferred_element_type=f32)
            s_diag = jnp.where(causal, s_diag, NEG)
            top = jnp.max(s_diag, axis=1, keepdims=True)
            if b > 0:
                s_old = lax.dot_general(qq, kk[:b * block, :], NT, preferred_element_type=f32)
                top = jnp.maximum(top, jnp.max(s_old, axis=1, keepdims=True))
            e = jnp.exp(s_diag - top)
            total = jnp.sum(e, axis=1, keepdims=True)
            o = lax.dot_general(e.astype(bf16), v_ref[rows, :], NN, preferred_element_type=f32)
            if b > 0:
                e = jnp.exp(s_old - top)
                total = total + jnp.sum(e, axis=1, keepdims=True)
                o = o + lax.dot_general(e.astype(bf16), v_ref[:b * block, :], NN, preferred_element_type=f32)
            outs.append(o * (1.0 / total))
            lses.append(top + jnp.log(total))
        mixed_ref[rows, :] = jnp.where(first, outs[0], outs[1]).astype(bf16)
        lse_ref[rows, :] = jnp.where(lane == 2 * pair, lses[0], jnp.where(lane == 2 * pair + 1, lses[1], lse_ref[rows, :]))

def attn_fwd(lengths, projected, *, dim=64, block=256):
    length, width3 = projected.shape
    width = width3 // 3
    docs = lengths.shape[1]
    pairs = width // 128
    col = lambda off: pl.BlockSpec((length, 128), lambda p: (0, p + off))
    return pl.pallas_call(
        functools.partial(attn_fwd_kernel, docs=docs, dim=dim, block=block),
        grid=(pairs,),
        in_specs=[pl.BlockSpec(memory_space=pltpu.SMEM), col(0), col(pairs), col(2 * pairs)],
        out_specs=[col(0), pl.BlockSpec((length, 128), lambda p: (0, 0))],
        out_shape=[jax.ShapeDtypeStruct((length, width), bf16), jax.ShapeDtypeStruct((length, 128), f32)],
        scratch_shapes=[pltpu.VMEM((length, 128), bf16), pltpu.VMEM((length, 128), bf16), pltpu.VMEM((length, 256), bf16)],
        compiler_params=pltpu.CompilerParams(vmem_limit_bytes=48 * 2 ** 20),
        name="attend",
    )(lengths, projected, projected, projected)

def attn_bwd_kernel(lengths_ref, q_ref, k_ref, v_ref, mixed_ref, gmix_ref, lse_ref, dq_ref, dk_ref, dv_ref,
                    aug_q, aug_k, kk, vv, qq, gg, kt, dqt, *, docs, dim, block):
    pair = pl.program_id(0)
    length = q_ref.shape[0]
    blocks = length // block
    lane = lax.broadcasted_iota(jnp.int32, (1, 128), 1)

    @pl.when(pair == 0)
    def _():
        hot = one_hot_docs(lengths_ref, docs, length)
        marks = lane < docs + 1
        aug_q[...] = jnp.where(hot & marks, 1.0, 0.0).astype(bf16)
        aug_k[...] = key_marks(hot, lane)

    kk[:, :128] = k_ref[...]
    kk[:, 128:] = aug_k[...]
    vv[:, :128] = v_ref[...]
    vv[:, 128:] = aug_k[...]
    kt[...] = jnp.transpose(k_ref[...])
    scale = 1.0 / math.sqrt(dim)
    first = lane < dim
    q2 = q_ref[...].astype(f32) * scale
    g2 = gmix_ref[...].astype(f32)
    dots = g2 * mixed_ref[...].astype(f32)
    lse_all = lse_ref[...]
    marks_q = aug_q[...].astype(f32)
    for h in range(2):
        mine = first if h == 0 else jnp.logical_not(first)
        lse = jnp.sum(jnp.where(lane == 2 * pair + h, lse_all, 0.0), axis=1, keepdims=True)
        qq[h, :, :128] = jnp.where(mine, q2, 0.0).astype(bf16)
        qq[h, :, 128:] = with_stat(marks_q, -lse, lane)
        delta = jnp.sum(jnp.where(mine, dots, 0.0), axis=1, keepdims=True)
        gg[h, :, :128] = jnp.where(mine, g2, 0.0).astype(bf16)
        gg[h, :, 128:] = with_stat(jnp.zeros_like(marks_q), -delta, lane)
    krow = lax.broadcasted_iota(jnp.int32, (block, block), 0)
    qcol = lax.broadcasted_iota(jnp.int32, (block, block), 1)
    causal = qcol >= krow
    for kb in range(blocks):
        keys = pl.ds(kb * block, block)
        dk = jnp.zeros((block, 128), f32)
        dv = jnp.zeros((block, 128), f32)
        for h in range(2):
            for qb in range(kb, blocks):
                queries = pl.ds(qb * block, block)
                s = lax.dot_general(kk[keys, :], qq[h, queries, :], NT, preferred_element_type=f32)
                if qb == kb:
                    s = jnp.where(causal, s, NEG)
                p = jnp.exp(s)
                dp = lax.dot_general(vv[keys, :], gg[h, queries, :], NT, preferred_element_type=f32)
                ds = (p * dp).astype(bf16)
                dv = dv + lax.dot_general(p.astype(bf16), gg[h, queries, :128], NN, preferred_element_type=f32)
                dk = dk + lax.dot_general(ds, qq[h, queries, :128], NN, preferred_element_type=f32)
                part = lax.dot_general(kt[h * dim:(h + 1) * dim, keys], ds, NN, preferred_element_type=f32)
                if kb == 0:
                    dqt[h * dim:(h + 1) * dim, queries] = part
                else:
                    dqt[h * dim:(h + 1) * dim, queries] += part
        dk_ref[keys, :] = dk.astype(bf16)
        dv_ref[keys, :] = dv.astype(bf16)
    dq_ref[...] = (jnp.transpose(dqt[...]) * scale).astype(bf16)

def attn_bwd(lengths, projected, mixed, gmix, lse, *, dim=64, block=256):
    length, width3 = projected.shape
    width = width3 // 3
    docs = lengths.shape[1]
    pairs = width // 128
    col = lambda off: pl.BlockSpec((length, 128), lambda p: (0, p + off))
    one = jax.ShapeDtypeStruct((length, width), bf16)
    return pl.pallas_call(
        functools.partial(attn_bwd_kernel, docs=docs, dim=dim, block=block),
        grid=(pairs,),
        in_specs=[pl.BlockSpec(memory_space=pltpu.SMEM), col(0), col(pairs), col(2 * pairs), col(0), col(0),
                  pl.BlockSpec((length, 128), lambda p: (0, 0))],
        out_specs=[col(0), col(0), col(0)],
        out_shape=[one, one, one],
        scratch_shapes=[pltpu.VMEM((length, 128), bf16), pltpu.VMEM((length, 128), bf16),
                        pltpu.VMEM((length, 256), bf16), pltpu.VMEM((length, 256), bf16),
                        pltpu.VMEM((2, length, 256), bf16), pltpu.VMEM((2, length, 256), bf16),
                        pltpu.VMEM((128, length), bf16), pltpu.VMEM((128, length), f32)],
        compiler_params=pltpu.CompilerParams(vmem_limit_bytes=48 * 2 ** 20),
        name="attend_back",
    )(lengths, projected, projected, projected, mixed, gmix, lse)


def place_tables(length, width):
    freq = np.exp(np.arange(width // 2, dtype=np.float64) * (-2.0 * math.log(10000.0) / width))
    angles = np.arange(length, dtype=np.float64)[:, None] * freq[None, :]
    return (np.concatenate([np.sin(angles), np.cos(angles)], axis=1).astype(np.float32),
            freq.astype(np.float32)[None, :])

def norm_stats(v):
    center = v - jnp.mean(v, axis=1, keepdims=True)
    inv = lax.rsqrt(jnp.mean(center * center, axis=1, keepdims=True) + 1e-5)
    return center * inv, inv

def front_kernel(lengths_ref, x_ref, table_ref, freq_ref, gain_ref, bias_ref, w_ref,
                 stream_ref, normed_ref, proj_ref, starts, *, docs):
    step = pl.program_id(0)
    rows, width = x_ref.shape
    half = width // 2
    begin, end, _ = doc_bounds(lengths_ref, docs)

    @pl.when(step == 0)
    def _():
        at = jnp.transpose(jnp.broadcast_to(begin.astype(f32), (128, 128)))[:, :1]
        angle = at * freq_ref[...]
        both = jnp.concatenate([jnp.sin(angle), jnp.cos(angle)], axis=1)
        hi = both.astype(bf16)
        mid = (both - hi.astype(f32)).astype(bf16)
        starts[:128, :] = hi
        starts[128:256, :] = mid
        starts[256:, :] = (both - hi.astype(f32) - mid.astype(f32)).astype(bf16)

    place = step * rows + lax.broadcasted_iota(jnp.int32, (rows, 128), 0)
    hot = jnp.where((place >= begin) & (place < end), 1.0, 0.0).astype(bf16)
    start = lax.dot_general(jnp.concatenate([hot, hot, hot], axis=1), starts[...], NN, preferred_element_type=f32)
    sin_b, cos_b = start[:, :half], start[:, half:]
    sin_t, cos_t = table_ref[:, :half], table_ref[:, half:]
    x = x_ref[...].astype(f32)
    stream = jnp.concatenate([x[:, :half] + (sin_t * cos_b - cos_t * sin_b),
                              x[:, half:] + (cos_t * cos_b + sin_t * sin_b)], axis=1)
    stream_ref[...] = stream
    unit, _ = norm_stats(stream)
    normed = (unit * gain_ref[...] + bias_ref[...]).astype(bf16)
    normed_ref[...] = normed
    proj_ref[...] = lax.dot_general(normed, w_ref[...], NN, preferred_element_type=f32).astype(bf16)

def front(lengths, x, gain, bias, w, *, rows=256):
    length, width = x.shape
    table, freq = place_tables(length, width)
    docs = lengths.shape[1]
    blk = pl.BlockSpec((rows, width), lambda i: (i, 0))
    whole = lambda a: pl.BlockSpec(a.shape, lambda i: (0,) * a.ndim)
    return pl.pallas_call(
        functools.partial(front_kernel, docs=docs),
        grid=(length // rows,),
        in_specs=[pl.BlockSpec(memory_space=pltpu.SMEM), blk, blk, whole(freq), whole(gain), whole(bias), whole(w)],
        out_specs=[blk, blk, pl.BlockSpec((rows, w.shape[1]), lambda i: (i, 0))],
        out_shape=[jax.ShapeDtypeStruct((length, width), f32), jax.ShapeDtypeStruct((length, width), bf16),
                   jax.ShapeDtypeStruct((length, w.shape[1]), bf16)],
        scratch_shapes=[pltpu.VMEM((384, width), bf16)],
        compiler_params=pltpu.CompilerParams(vmem_limit_bytes=40 * 2 ** 20),
        name="front",
    )(lengths, x, table, freq, gain, bias, w)

ERF = (0.254829592, -0.284496736, 1.421413741, -1.453152027, 1.061405429)
ERF_P = 0.3275911

def gelu_both(h):
    bell = jnp.exp(h * h * -0.5)
    t = 1.0 / (1.0 + jnp.abs(h) * (ERF_P / math.sqrt(2.0)))
    poly = t * (ERF[0] + t * (ERF[1] + t * (ERF[2] + t * (ERF[3] + t * ERF[4]))))
    tail = 0.5 * poly * bell
    phi = jnp.where(h < 0.0, tail, 1.0 - tail)
    return h * phi, phi + h * bell * (1.0 / math.sqrt(2.0 * math.pi))

def ffn_kernel(stream_ref, mixed_ref, w_out_ref, b_out_ref, gain_ref, bias_ref, w_up_ref, b_up_ref, w_down_ref, b_down_ref,
               after_ref, normed_ref, act_ref, slope_ref, out_ref, *, chunk):
    after = stream_ref[...] + lax.dot_general(mixed_ref[...], w_out_ref[...], NN, preferred_element_type=f32) + b_out_ref[...]
    after_ref[...] = after
    unit, _ = norm_stats(after)
    normed = (unit * gain_ref[...] + bias_ref[...]).astype(bf16)
    normed_ref[...] = normed
    acc = after + b_down_ref[...]
    wide = w_up_ref.shape[1]
    for c in range(wide // chunk):
        cols = pl.ds(c * chunk, chunk)
        hidden = lax.dot_general(normed, w_up_ref[:, cols], NN, preferred_element_type=f32) + b_up_ref[:, cols]
        act, slope = gelu_both(hidden)
        act = act.astype(bf16)
        act_ref[:, cols] = act
        slope_ref[:, cols] = slope.astype(bf16)
        acc = acc + lax.dot_general(act, w_down_ref[cols, :], NN, preferred_element_type=f32)
    out_ref[...] = acc.astype(bf16)

def ffn(stream, mixed, w_out, b_out, gain, bias, w_up, b_up, w_down, b_down, *, rows=256, chunk=512):
    length, width = stream.shape
    wide = w_up.shape[1]
    blk = pl.BlockSpec((rows, width), lambda i: (i, 0))
    big = pl.BlockSpec((rows, wide), lambda i: (i, 0))
    whole = lambda a: pl.BlockSpec(a.shape, lambda i: (0,) * a.ndim)
    args = (w_out, b_out, gain, bias, w_up, b_up, w_down, b_down)
    return pl.pallas_call(
        functools.partial(ffn_kernel, chunk=chunk),
        grid=(length // rows,),
        in_specs=[blk, blk] + [whole(a) for a in args],
        out_specs=[blk, blk, big, big, blk],
        out_shape=[jax.ShapeDtypeStruct((length, width), f32), jax.ShapeDtypeStruct((length, width), bf16),
                   jax.ShapeDtypeStruct((length, wide), bf16), jax.ShapeDtypeStruct((length, wide), bf16),
                   jax.ShapeDtypeStruct((length, width), bf16)],
        compiler_params=pltpu.CompilerParams(vmem_limit_bytes=48 * 2 ** 20),
        name="ffn",
    )(stream, mixed, *args)

def norm_back(g, gain, unit, inv):
    gu = g * gain
    return inv * (gu - jnp.mean(gu, axis=1, keepdims=True) - unit * jnp.mean(gu * unit, axis=1, keepdims=True))

def colsum(x):
    return jnp.sum(x, axis=0, keepdims=True)

def permuted_rows(dst, src, me, chunk):
    for a in range(src.shape[0] // chunk):
        dst[pl.ds(pl.multiple_of(lax.bitwise_xor(jnp.int32(a), me) * chunk, chunk), chunk), :] = src[a * chunk:(a + 1) * chunk, :]

def down_grad_kernel(me_ref, act_ref, g_ref, send_ref, keep_ref, g_low):
    i = pl.program_id(0)

    @pl.when(i == 0)
    def _():
        g_low[...] = g_ref[...].astype(bf16)
    out = lax.dot_general(act_ref[...], g_low[...], TN, preferred_element_type=f32).astype(bf16)

    @pl.when(i < 8)
    def _():
        send_ref[...] = out

    @pl.when(i >= 8)
    def _():
        keep_ref[...] = out

def down_grad(me, act, g):
    length, width = g.shape
    wide = act.shape[1]
    block = wide // 16

    def act_index(i, me_ref):
        keep, ab, pq = i // 8, (i // 4) % 2, i % 4
        core = jnp.bitwise_xor(1 - keep, me_ref[0])
        return (0, ab * 8 + core * 4 + jnp.bitwise_xor(pq, jnp.where(ab == 0, me_ref[1], me_ref[2])))
    return pl.pallas_call(
        down_grad_kernel,
        grid_spec=pltpu.PrefetchScalarGridSpec(
            num_scalar_prefetch=1, grid=(16,),
            in_specs=[pl.BlockSpec((length, block), act_index), pl.BlockSpec((length, width), lambda i, m: (0, 0))],
            out_specs=[pl.BlockSpec((block, width), lambda i, m: (jnp.minimum(i, 7), 0)),
                       pl.BlockSpec((block, width), lambda i, m: (jnp.maximum(i - 8, 0), 0))],
            scratch_shapes=[pltpu.VMEM((length, width), bf16)]),
        out_shape=[jax.ShapeDtypeStruct((wide // 2, width), bf16)] * 2,
        compiler_params=pltpu.CompilerParams(vmem_limit_bytes=40 * 2 ** 20),
        name="down_grad",
    )(me, act, g)

def ffn_back_kernel(me_ref, g_ref, slope_ref, w_down_ref, w_up_ref, normed_ref, after_ref, gain_ref, mixed_ref, w_out_ref,
                    bdown_ref, up_send, up_keep, gafter_ref, gmix_ref, out_send, out_keep, small_ref,
                    g_low, norm_t, acc, bup):
    i = pl.program_id(0)
    steps = pl.num_programs(0)
    width = g_ref.shape[1]
    tile = slope_ref.shape[1]
    row8 = width // 8

    def arranged(t, dst):
        for ab in range(2):
            for a in range(8):
                r = lax.bitwise_xor(jnp.int32(a), me_ref[0] * 4 + me_ref[1 + ab])
                dst[ab, pl.ds(pl.multiple_of(r * row8, row8), row8), :] = t[a * row8:(a + 1) * row8, :]

    @pl.when(i == 0)
    def _():
        g_low[...] = g_ref[...].astype(bf16)
        arranged(jnp.transpose(normed_ref[...]), norm_t)
        acc[...] = jnp.zeros_like(acc)
    gh = lax.dot_general(g_low[...], w_down_ref[...], NT, preferred_element_type=f32) * slope_ref[...].astype(f32)
    bup[pl.ds(i, 1), :] = colsum(gh)
    gh = gh.astype(bf16)
    acc[...] += lax.dot_general(gh, w_up_ref[...], NT, preferred_element_type=f32)
    lhs = norm_t[i // (steps // 2)]
    grad = lax.dot_general(lhs, gh, NN, preferred_element_type=f32).astype(bf16)
    up_keep[...] = grad[:width // 2, :]
    up_send[...] = grad[width // 2:, :]

    @pl.when(i == steps - 1)
    def _():
        unit, inv = norm_stats(after_ref[...])
        gn = acc[...]
        ga = g_ref[...] + norm_back(gn, gain_ref[...], unit, inv)
        gafter_ref[...] = ga
        low = ga.astype(bf16)
        gmix_ref[...] = lax.dot_general(low, w_out_ref[...], NT, preferred_element_type=f32).astype(bf16)
        arranged(jnp.transpose(mixed_ref[...]), norm_t)
        for ab in range(2):
            cols = slice(ab * width // 2, (ab + 1) * width // 2)
            grad_out = lax.dot_general(norm_t[ab], low[:, cols], NN, preferred_element_type=f32).astype(bf16)
            out_keep[:, cols] = grad_out[:width // 2, :]
            out_send[:, cols] = grad_out[width // 2:, :]
        small_ref[0:1, :] = bdown_ref[...]
        small_ref[1:2, :] = colsum(gn * unit)
        small_ref[2:3, :] = colsum(gn)
        small_ref[3:4, :] = colsum(ga)
        per = width // tile
        for k in range(steps // per):
            for m in range(per):
                small_ref[4 + k:5 + k, m * tile:(m + 1) * tile] = bup[k * per + m:k * per + m + 1, :]

def ffn_back(me, g, slope, w_down, w_up, normed, after, gain, mixed, w_out, bdown, *, tile=256):
    length, width = g.shape
    wide = slope.shape[1]
    steps = wide // tile
    whole = lambda a: pl.BlockSpec(a.shape, lambda i, m: (0,) * a.ndim)
    full = lambda s: pl.BlockSpec(s, lambda i, m: (0,) * len(s))
    half = pl.BlockSpec((width // 2, tile), lambda i, m: (0, i))
    small_rows = 4 + wide // width
    return pl.pallas_call(
        ffn_back_kernel,
        grid_spec=pltpu.PrefetchScalarGridSpec(
            num_scalar_prefetch=1, grid=(steps,),
            in_specs=[whole(g), pl.BlockSpec((length, tile), lambda i, m: (0, i)), pl.BlockSpec((tile, width), lambda i, m: (i, 0)),
                      pl.BlockSpec((width, tile), lambda i, m: (0, i)), whole(normed), whole(after), whole(gain), whole(mixed),
                      whole(w_out), whole(bdown)],
            out_specs=[half, half, full((length, width)), full((length, width)), full((width // 2, width)), full((width // 2, width)),
                       full((small_rows, width))],
            scratch_shapes=[pltpu.VMEM((length, width), bf16), pltpu.VMEM((2, width, length), bf16), pltpu.VMEM((length, width), f32),
                            pltpu.VMEM((steps, tile), f32)]),
        out_shape=[jax.ShapeDtypeStruct((width // 2, wide), bf16)] * 2
        + [jax.ShapeDtypeStruct((length, width), f32), jax.ShapeDtypeStruct((length, width), bf16)]
        + [jax.ShapeDtypeStruct((width // 2, width), bf16)] * 2 + [jax.ShapeDtypeStruct((small_rows, width), f32)],
        compiler_params=pltpu.CompilerParams(vmem_limit_bytes=56 * 2 ** 20),
        name="ffn_back",
    )(me, g, slope, w_down, w_up, normed, after, gain, mixed, w_out, bdown)

def qkv_grad_kernel(me_ref, gp_q, gp_k, gp_v, normed_ref, send_ref, keep_ref, norm_t):
    width = normed_ref.shape[1]
    row8 = width // 8
    t = jnp.transpose(normed_ref[...])
    for ab in range(2):
        for a in range(8):
            r = lax.bitwise_xor(jnp.int32(a), me_ref[0] * 4 + me_ref[1 + ab])
            norm_t[ab, pl.ds(pl.multiple_of(r * row8, row8), row8), :] = t[a * row8:(a + 1) * row8, :]
    at = 0
    cut = 3 * width // 2
    for part in (gp_q, gp_k, gp_v):
        for c in range(0, width, 256):
            ab = 0 if at < cut else 1
            grad = lax.dot_general(norm_t[ab], part[:, c:c + 256], NN, preferred_element_type=f32).astype(bf16)
            keep_ref[:, at:at + 256] = grad[:width // 2, :]
            send_ref[:, at:at + 256] = grad[width // 2:, :]
            at += 256

def qkv_grad(me, gq, gk, gv, normed):
    length, width = normed.shape
    vm = pl.BlockSpec(memory_space=pltpu.VMEM)
    return pl.pallas_call(
        qkv_grad_kernel,
        in_specs=[pl.BlockSpec(memory_space=pltpu.SMEM), vm, vm, vm, vm],
        out_specs=[vm, vm],
        out_shape=[jax.ShapeDtypeStruct((width // 2, 3 * width), bf16)] * 2,
        scratch_shapes=[pltpu.VMEM((2, width, length), bf16)],
        compiler_params=pltpu.CompilerParams(vmem_limit_bytes=48 * 2 ** 20),
        name="qkv_grad",
    )(me, gq, gk, gv, normed)

def front_back_kernel(gq, gk, gv, w_ref, stream_ref, gafter_ref, gain_ref, out_ref, small_ref):
    i = pl.program_id(0)
    width = stream_ref.shape[1]
    gn = lax.dot_general(gq[...], w_ref[:, :width], NT, preferred_element_type=f32)
    gn = gn + lax.dot_general(gk[...], w_ref[:, width:2 * width], NT, preferred_element_type=f32)
    gn = gn + lax.dot_general(gv[...], w_ref[:, 2 * width:], NT, preferred_element_type=f32)
    unit, inv = norm_stats(stream_ref[...])
    out_ref[...] = (gafter_ref[...] + norm_back(gn, gain_ref[...], unit, inv)).astype(bf16)
    part = jnp.concatenate([colsum(gn * unit), colsum(gn)], axis=0)
    small_ref[...] = jnp.where(i == 0, part, small_ref[...] + part)

def front_back(gq, gk, gv, w, stream, gafter, gain, *, rows=256):
    length, width = stream.shape
    blk = pl.BlockSpec((rows, width), lambda i: (i, 0))
    whole = lambda a: pl.BlockSpec(a.shape, lambda i: (0,) * a.ndim)
    return pl.pallas_call(
        front_back_kernel,
        grid=(length // rows,),
        in_specs=[blk, blk, blk, whole(w), blk, blk, whole(gain)],
        out_specs=[blk, pl.BlockSpec((2, width), lambda i: (0, 0))],
        out_shape=[jax.ShapeDtypeStruct((length, width), bf16), jax.ShapeDtypeStruct((2, width), f32)],
        compiler_params=pltpu.CompilerParams(vmem_limit_bytes=40 * 2 ** 20),
        name="front_back",
    )(gq, gk, gv, w, stream, gafter, gain)


def finish_kernel(me_ref, own_a, own_b, got_a, got_b, out_ref, *, by_rows, nt, n):
    i = pl.program_id(0)
    rows = own_a.shape[0]
    chunk = rows // (4 * n)

    def lay(ab, own, got):
        for near, ref in ((0, own), (1, got)):
            core = lax.bitwise_xor(jnp.int32(near), me_ref[0])
            for pq in range(4):
                for z in range(n):
                    at = core * 4 + lax.bitwise_xor(jnp.int32(pq), me_ref[1 + ab])
                    at = at * n + lax.bitwise_xor(jnp.int32(z), me_ref[3])
                    at = at * chunk + (ab * 2 * rows if by_rows else 0)
                    r = (pq * n + z) * chunk
                    out_ref[pl.ds(pl.multiple_of(at, chunk), chunk), :] = ref[r:r + chunk, :].astype(f32)
    if by_rows:
        lay(0, own_a, got_a)
        lay(1, own_b, got_b)
    else:
        @pl.when(i < nt)
        def _():
            lay(0, own_a, got_a)

        @pl.when(i >= nt)
        def _():
            lay(1, own_b, got_b)

def finish(me, own_a, own_b, got_a, got_b, *, by_rows, n, tile):
    rows, width = own_a.shape
    nt = width // tile
    if by_rows:
        spec_a = spec_b = pl.BlockSpec((rows, tile), lambda i, m: (0, i))
        grid, shape = nt, (4 * rows, width)
    else:
        spec_a = pl.BlockSpec((rows, tile), lambda i, m: (0, jnp.minimum(i, nt - 1)))
        spec_b = pl.BlockSpec((rows, tile), lambda i, m: (0, jnp.maximum(i - nt, 0)))
        grid, shape = 2 * nt, (2 * rows, 2 * width)
    return pl.pallas_call(
        functools.partial(finish_kernel, by_rows=by_rows, nt=nt, n=n),
        grid_spec=pltpu.PrefetchScalarGridSpec(
            num_scalar_prefetch=1, grid=(grid,),
            in_specs=[spec_a, spec_b, spec_a, spec_b],
            out_specs=pl.BlockSpec((shape[0], tile), lambda i, m: (0, i))),
        out_shape=jax.ShapeDtypeStruct(shape, f32),
        compiler_params=pltpu.CompilerParams(vmem_limit_bytes=40 * 2 ** 20),
        name="finish",
    )(me, own_a, own_b, got_a, got_b)

class Links:
    def __init__(self, mesh):
        self.sizes = dict(mesh.shape)
        self.n = self.sizes["rows"] // 2

    def swap(self, x, axis, bit):
        return lax.ppermute(x, axis, [(a, a ^ bit) for a in range(self.sizes[axis])])

    def core(self, x):
        return self.swap(x, "bank", 1)

    def near(self, x):
        return self.swap(x, "bank", 2)

    def side(self, x):
        return self.swap(x, "rows", 1)

def plus(*terms):
    out = terms[0].astype(f32)
    for t in terms[1:]:
        out = out + t.astype(f32)
    return out.astype(bf16)

def total(links, me, send, keep, *, by_rows, tile):
    n = links.n
    got = links.core(send)
    rows, width = keep.shape
    if by_rows:
        cut = lambda x: (x[:rows // 2], x[rows // 2:])
    else:
        cut = lambda x: (x[:, :width // 2], x[:, width // 2:])
    (ka, kb), (ga, gb) = cut(keep), cut(got)
    half = ka.shape[0] // 2
    sa, sb = plus(ka[half:], ga[half:]), plus(kb[half:], gb[half:])
    ra, rb = links.near(sa), links.side(sb)
    a, b = plus(ka[:half], ga[:half]), plus(kb[:half], gb[:half])
    half //= 2
    sa, sb = plus(a[half:], ra[half:]), plus(b[half:], rb[half:])
    a, b = plus(a[:half], ra[:half]), plus(b[:half], rb[:half])
    ra, rb = links.side(sa), links.near(sb)
    a, b = plus(a, ra), plus(b, rb)
    chunk = half // n
    w = a.shape[1]
    fine = half % (n * 16) == 0 and n & (n - 1) == 0
    if fine:
        zi = lax.axis_index("rows") // 2
        piece = lambda k: jnp.stack([lax.dynamic_slice(v, ((zi ^ k) * chunk, 0), (chunk, w)) for v in (a, b)])
        got = [links.swap(piece(k), "rows", 2 * k) for k in range(1, n)]
        mine = plus(piece(0), *got)
        got = [links.swap(mine, "rows", 2 * k) for k in range(1, n)]
        a = jnp.concatenate([mine[0]] + [g[0] for g in got], axis=0)
        b = jnp.concatenate([mine[1]] + [g[1] for g in got], axis=0)
    else:
        groups = [[r for r in range(2 * n) if r % 2 == y] for y in range(2)]
        a, b = lax.psum((a, b), "rows", axis_index_groups=groups)
    ra, rb = links.side(a), links.near(b)
    a, b = jnp.concatenate([a, ra], axis=0), jnp.concatenate([b, rb], axis=0)
    ra, rb = links.near(a), links.side(b)
    a, b = jnp.concatenate([a, ra], axis=0), jnp.concatenate([b, rb], axis=0)
    ga, gb = links.core(a), links.core(b)
    return finish(me, a, b, ga, gb, by_rows=by_rows, n=n if fine else 1, tile=tile)

def total_small(links, x):
    for axis in ("bank", "rows"):
        bit = 1
        while bit < links.sizes[axis]:
            x = x + links.swap(x, axis, bit)
            bit *= 2
    return x

def body(mesh, hidden_in, lengths, ln1_gain, ln1_bias, w_qkv, w_out, b_out, ln2_gain, ln2_bias, w_up, b_up, w_down, b_down,
         bank, bank_labels, target_slots, gold_ids):
    links = Links(mesh)
    row = lambda v: v.reshape(1, -1)
    width = hidden_in.shape[1]
    ib, ir = lax.axis_index("bank"), lax.axis_index("rows")
    core, x, y = ib % 2, ib // 2, ir % 2
    me = jnp.stack([core, x * 2 + y, y * 2 + x, ir // 2 if (links.n & (links.n - 1)) == 0 else 0]).astype(jnp.int32)
    bank_all = lax.all_gather(bank, "bank", axis=0, tiled=True)
    labels_all = lax.all_gather(bank_labels, "bank", axis=0, tiled=True)
    stream, normed_a, projected = front(lengths, hidden_in, row(ln1_gain), row(ln1_bias), w_qkv)
    mixed, lse = attn_fwd(lengths, projected, block=512)
    after, normed_c, act, slope, block_out = ffn(stream, mixed, w_out, row(b_out), row(ln2_gain), row(ln2_bias), w_up, row(b_up),
                                                 w_down, row(b_down), chunk=256)
    g, loss, bdown = bank_call(lengths, block_out, gold_ids, target_slots, labels_all, bank_all, edt=f32)
    down_send, down_keep = down_grad(me, act, g)
    w_down_grad = total(links, me, down_send, down_keep, by_rows=True, tile=256)
    up_send, up_keep, gafter, gmix, out_send, out_keep, small = ffn_back(
        me, g, slope, w_down, w_up, normed_c, after, row(ln2_gain), mixed, w_out, bdown, tile=512)
    w_up_grad = total(links, me, up_send, up_keep, by_rows=False, tile=512)
    w_out_grad = total(links, me, out_send, out_keep, by_rows=False, tile=256)
    small = total_small(links, small)
    gq, gk, gv = attn_bwd(lengths, projected, mixed, gmix, lse, block=512)
    qkv_send, qkv_keep = qkv_grad(me, gq, gk, gv, normed_a)
    w_qkv_grad = total(links, me, qkv_send, qkv_keep, by_rows=False, tile=384)
    input_grad, small1 = front_back(gq, gk, gv, w_qkv, stream, gafter, row(ln1_gain))
    small1 = total_small(links, small1)
    return (block_out, loss.reshape(-1), input_grad, small1[0], small1[1], w_qkv_grad, w_out_grad, small[3], small[1], small[2],
            w_up_grad, small[4:].reshape(-1), w_down_grad, small[0])

def solution(mesh):
    in_specs = (
        P(("rows", "bank"), None),
        P(("rows", "bank"), None),
        P(),
        P(),
        P(),
        P(),
        P(),
        P(),
        P(),
        P(),
        P(),
        P(),
        P(),
        P("bank", None),
        P("bank"),
        P(("rows", "bank")),
        P(("rows", "bank")),
    )
    out_specs = (
        P(("rows", "bank"), None),
        P(("rows", "bank")),
        P(("rows", "bank"), None),
        P(),
        P(),
        P(),
        P(),
        P(),
        P(),
        P(),
        P(),
        P(),
        P(),
        P(),
    )
    return jax.shard_map(functools.partial(body, mesh), mesh=mesh, in_specs=in_specs, out_specs=out_specs, check_vma=False)
```

```python
import functools
import math

import jax
import jax.numpy as jnp
import numpy as np
from jax import lax
from jax.experimental import pallas as pl
from jax.experimental.pallas import tpu as pltpu
from jax.sharding import PartitionSpec as P

LOG2E = 1.4426950408889634
LN2 = 0.6931471805599453
NT = (((1,), (1,)), ((), ()))
NN = (((1,), (0,)), ((), ()))
f32, bf16 = jnp.float32, jnp.bfloat16

LIMIT = 60 * 2 ** 20

def spend(us):
    return pl.CostEstimate(flops=int(us * 1.0e9), bytes_accessed=0, transcendentals=0)

def column(row, rows):
    return jnp.transpose(jnp.broadcast_to(row.astype(f32), (128, rows)))[:, :1]

def bank_kernel(lengths_ref, q_ref, gold_ref, target_ref, labels_ref, bank_hbm,
                grad_ref, loss_ref, bsum_ref,
                bank_ref, s0_ref, s1_ref, e_ref, max_ref, sems, *, rows, tile, docs):
    step = pl.program_id(0)
    slots, width = bank_ref.shape
    tiles = slots // tile
    c = LOG2E / math.sqrt(width)
    copies = [pltpu.make_async_copy(bank_hbm.at[pl.ds(j * tile, tile)], bank_ref.at[pl.ds(j * tile, tile)], sems.at[j]) for j in range(tiles)]

    @pl.when(step == 0)
    def _():
        for j in range(tiles):
            copies[j].start()

    total = lengths_ref[0, 0]
    for j in range(1, docs):
        total = total + lengths_ref[0, j]
    gold = column(gold_ref[...], rows)
    target = column(target_ref[...], rows)
    gold_b = jnp.broadcast_to(gold, (rows, 128)).astype(jnp.int32)
    target_b = jnp.broadcast_to(target, (rows, 128)).astype(jnp.int32)
    place = step * rows + lax.broadcasted_iota(jnp.int32, (rows, 1), 0)
    live = place < total
    q = q_ref[...]
    lane = lax.broadcasted_iota(jnp.int32, (1, tile), 1)

    def wide(col):
        return jnp.concatenate([col] * (tile // 128), axis=1)

    def positive_of(j):
        labels = labels_ref[j]
        return (labels == wide(gold_b)) | ((lane + j * tile) == wide(target_b))

    def scores(j):
        return lax.dot_general(q, bank_ref[pl.ds(j * tile, tile), :], NT, preferred_element_type=f32)

    def fold(x):
        out = x[:, :128]
        for i in range(1, tile // 128):
            out = out + x[:, i * 128:(i + 1) * 128]
        return out

    def fold_max(x):
        out = x[:, :128]
        for i in range(1, tile // 128):
            out = jnp.maximum(out, x[:, i * 128:(i + 1) * 128])
        return out

    def eat(j, s_ref, top, sum_all, sum_pos):
        s = s_ref[...]
        here = jnp.max(fold_max(s), axis=1, keepdims=True) * c
        new_top = jnp.maximum(top, here)
        shrink = jnp.exp2(top - new_top)
        e = jnp.exp2(s * c - new_top)
        pos = positive_of(j)
        sum_all = sum_all * shrink + fold(e)
        sum_pos = sum_pos * shrink + fold(jnp.where(pos, e, 0.0))
        e_ref[j] = e.astype(e_ref.dtype)
        max_ref[j] = new_top
        return new_top, sum_all, sum_pos

    @pl.when(step == 0)
    def _():
        copies[0].wait()
    s0_ref[...] = scores(0)
    state = (jnp.full((rows, 1), -1e30, f32), jnp.zeros((rows, 128), f32), jnp.zeros((rows, 128), f32))

    bufs = (s0_ref, s1_ref)
    for j in range(tiles):
        if j + 1 < tiles:
            @pl.when(step == 0)
            def _():
                copies[j + 1].wait()
            bufs[(j + 1) % 2][...] = scores(j + 1)
        state = eat(j, bufs[j % 2], *state)
    top, sum_all, sum_pos = state
    sum_all = jnp.sum(sum_all, axis=1, keepdims=True)
    sum_pos = jnp.sum(sum_pos, axis=1, keepdims=True)
    safe = jnp.min(sum_pos) >= 2.0 ** -60
    lse_all = top + jnp.log2(sum_all)

    def finish(loss, acc):
        loss_ref[...] = jnp.transpose(jnp.broadcast_to(jnp.where(live, loss, 0.0), (rows, 128)))[:1, :]
        acc = acc * (1.0 / math.sqrt(width))
        grad_ref[...] = acc
        part = jnp.sum(acc, axis=0, keepdims=True)
        bsum_ref[...] = jnp.where(step == 0, part, bsum_ref[...] + part)

    @pl.when(safe)
    def _():
        lse_pos = top + jnp.log2(sum_pos)
        inv_all = jnp.where(live, 1.0 / sum_all, 0.0)
        inv_diff = inv_all - jnp.where(live, 1.0 / sum_pos, 0.0)
        acc = jnp.zeros((rows, width), f32)
        for j in range(tiles):
            factor = jnp.exp2(max_ref[j] - top)
            on = jnp.broadcast_to(factor * inv_diff, (rows, 128))
            off = jnp.broadcast_to(factor * inv_all, (rows, 128))
            g = e_ref[j].astype(f32) * jnp.where(positive_of(j), wide(on), wide(off))
            acc = acc + lax.dot_general(g.astype(bf16), bank_ref[pl.ds(j * tile, tile), :], NN, preferred_element_type=f32)
        finish((lse_all - lse_pos) * LN2, acc)

    @pl.when(jnp.logical_not(safe))
    def _():
        def pos_top(j, best):
            masked = jnp.where(positive_of(j), scores(j) * c, -1e30)
            return jnp.maximum(best, jnp.max(masked, axis=1, keepdims=True))
        top_pos = lax.fori_loop(0, tiles, pos_top, jnp.full((rows, 1), -1e30, f32))

        def pos_sum(j, total_pos):
            x = jnp.where(positive_of(j), scores(j) * c, -1e30)
            return total_pos + jnp.sum(jnp.exp2(x - top_pos), axis=1, keepdims=True)
        lse_pos = top_pos + jnp.log2(lax.fori_loop(0, tiles, pos_sum, jnp.zeros((rows, 1), f32)))
        cut_all = jnp.where(live, lse_all, 1e30)
        cut_pos = jnp.where(live, lse_pos, 1e30)

        def pull(j, acc):
            s = scores(j) * c
            g = jnp.exp2(s - cut_all) - jnp.exp2(jnp.where(positive_of(j), s, -1e30) - cut_pos)
            return acc + lax.dot_general(g.astype(bf16), bank_ref[pl.ds(j * tile, tile), :], NN, preferred_element_type=f32)
        finish((lse_all - lse_pos) * LN2, lax.fori_loop(0, tiles, pull, jnp.zeros((rows, width), f32)))

def bank_call(lengths, q, gold, target, labels, bank, *, rows=512, tile=1024, edt=bf16):
    length, width = q.shape
    slots = bank.shape[0]
    tiles = slots // tile
    docs = lengths.shape[1]
    return pl.pallas_call(
        functools.partial(bank_kernel, rows=rows, tile=tile, docs=docs),
        grid=(length // rows,),
        in_specs=[
            pl.BlockSpec(memory_space=pltpu.SMEM),
            pl.BlockSpec((rows, width), lambda i: (i, 0)),
            pl.BlockSpec((1, rows), lambda i: (0, i)),
            pl.BlockSpec((1, rows), lambda i: (0, i)),
            pl.BlockSpec((tiles, 1, tile), lambda i: (0, 0, 0)),
            pl.BlockSpec(memory_space=pl.ANY),
        ],
        out_specs=[
            pl.BlockSpec((rows, width), lambda i: (i, 0)),
            pl.BlockSpec((1, rows), lambda i: (0, i)),
            pl.BlockSpec((1, width), lambda i: (0, 0)),
        ],
        out_shape=[
            jax.ShapeDtypeStruct((length, width), f32),
            jax.ShapeDtypeStruct((1, length), f32),
            jax.ShapeDtypeStruct((1, width), f32),
        ],
        scratch_shapes=[
            pltpu.VMEM((slots, width), bf16),
            pltpu.VMEM((rows, tile), f32),
            pltpu.VMEM((rows, tile), f32),
            pltpu.VMEM((tiles, rows, tile), edt),
            pltpu.VMEM((tiles, rows, 1), f32),
            pltpu.SemaphoreType.DMA((tiles,)),
        ],
        compiler_params=pltpu.CompilerParams(vmem_limit_bytes=LIMIT),
        cost_estimate=spend(35),
        name="bank",
    )(lengths, q, gold.reshape(1, length), target.reshape(1, length), labels.reshape(tiles, 1, tile), bank)

TN = (((0,), (0,)), ((), ()))
BIG = 1e30
STAT = 120
NEG = -1e30

def doc_bounds(lengths_ref, docs):
    lane = lax.broadcasted_iota(jnp.int32, (1, 128), 1)
    begin = jnp.zeros((1, 128), jnp.int32)
    end = jnp.zeros((1, 128), jnp.int32)
    at = jnp.int32(0)
    for j in range(docs):
        begin = jnp.where(lane == j, at, begin)
        at = at + lengths_ref[0, j]
        end = jnp.where(lane == j, at, end)
    begin = jnp.where(lane == docs, at, begin)
    end = jnp.where(lane == docs, 2 ** 30, end)
    return begin, end, at

def one_hot_docs(lengths_ref, docs, length):
    begin, end, _ = doc_bounds(lengths_ref, docs)
    place = lax.broadcasted_iota(jnp.int32, (length, 128), 0)
    return (place >= begin) & (place < end)

def split3(col):
    hi = col.astype(bf16).astype(f32)
    mid = (col - hi).astype(bf16).astype(f32)
    lo = col - hi - mid
    return hi, mid, lo

def with_stat(base, col, lane):
    hi, mid, lo = split3(col)
    return jnp.where(lane == STAT, hi, jnp.where(lane == STAT + 1, mid, jnp.where(lane == STAT + 2, lo, base))).astype(bf16)

def key_marks(hot, lane):
    ones = (lane >= STAT) & (lane < STAT + 3)
    return jnp.where(ones, 1.0, jnp.where(hot, 0.0, -BIG)).astype(bf16)

def attn_fwd_kernel(lengths_ref, q_ref, k_ref, v_ref, mixed_ref, lse_ref, aug_q, aug_k, kk, *, docs, dim, block):
    pair = pl.program_id(0)
    length = q_ref.shape[0]
    lane = lax.broadcasted_iota(jnp.int32, (1, 128), 1)

    @pl.when(pair == 0)
    def _():
        hot = one_hot_docs(lengths_ref, docs, length)
        marks = lane < docs + 1
        aug_q[...] = jnp.where(hot & marks, 1.0, 0.0).astype(bf16)
        aug_k[...] = key_marks(hot, lane)
        lse_ref[...] = jnp.zeros_like(lse_ref)

    kk[:, :128] = k_ref[...]
    kk[:, 128:] = aug_k[...]
    scale = 1.0 / math.sqrt(dim)
    first = lane < dim
    row = lax.broadcasted_iota(jnp.int32, (block, block), 0)
    col = lax.broadcasted_iota(jnp.int32, (block, block), 1)
    causal = row >= col
    for b in range(length // block):
        rows = pl.ds(b * block, block)
        q2 = q_ref[rows, :].astype(f32) * scale
        outs, lses = [], []
        for h in range(2):
            mine = first if h == 0 else jnp.logical_not(first)
            qq = jnp.concatenate([jnp.where(mine, q2, 0.0).astype(bf16), aug_q[rows, :]], axis=1)
            s_diag = lax.dot_general(qq, kk[rows, :], NT, preferred_element_type=f32)
            s_diag = jnp.where(causal, s_diag, NEG)
            top = jnp.max(s_diag, axis=1, keepdims=True)
            if b > 0:
                s_old = lax.dot_general(qq, kk[:b * block, :], NT, preferred_element_type=f32)
                top = jnp.maximum(top, jnp.max(s_old, axis=1, keepdims=True))
            e = jnp.exp(s_diag - top)
            total = jnp.sum(e, axis=1, keepdims=True)
            o = lax.dot_general(e.astype(bf16), v_ref[rows, :], NN, preferred_element_type=f32)
            if b > 0:
                e = jnp.exp(s_old - top)
                total = total + jnp.sum(e, axis=1, keepdims=True)
                o = o + lax.dot_general(e.astype(bf16), v_ref[:b * block, :], NN, preferred_element_type=f32)
            outs.append(o * (1.0 / total))
            lses.append(top + jnp.log(total))
        mixed_ref[rows, :] = jnp.where(first, outs[0], outs[1]).astype(bf16)
        lse_ref[rows, :] = jnp.where(lane == 2 * pair, lses[0], jnp.where(lane == 2 * pair + 1, lses[1], lse_ref[rows, :]))

def attn_fwd(lengths, projected, *, dim=64, block=256):
    length, width3 = projected.shape
    width = width3 // 3
    docs = lengths.shape[1]
    pairs = width // 128
    col = lambda off: pl.BlockSpec((length, 128), lambda p: (0, p + off))
    return pl.pallas_call(
        functools.partial(attn_fwd_kernel, docs=docs, dim=dim, block=block),
        grid=(pairs,),
        in_specs=[pl.BlockSpec(memory_space=pltpu.SMEM), col(0), col(pairs), col(2 * pairs)],
        out_specs=[col(0), pl.BlockSpec((length, 128), lambda p: (0, 0))],
        out_shape=[jax.ShapeDtypeStruct((length, width), bf16), jax.ShapeDtypeStruct((length, 128), f32)],
        scratch_shapes=[pltpu.VMEM((length, 128), bf16), pltpu.VMEM((length, 128), bf16), pltpu.VMEM((length, 256), bf16)],
        compiler_params=pltpu.CompilerParams(vmem_limit_bytes=LIMIT),
        cost_estimate=spend(12),
        name="attend",
    )(lengths, projected, projected, projected)

def attn_bwd_kernel(lengths_ref, q_ref, k_ref, v_ref, mixed_ref, gmix_ref, lse_ref, dq_ref, dk_ref, dv_ref,
                    aug_q, aug_k, kk, vv, qq, gg, kt, dqt, *, docs, dim, block, first):
    step = pl.program_id(0)
    pair = step + first
    length = q_ref.shape[0]
    blocks = length // block
    lane = lax.broadcasted_iota(jnp.int32, (1, 128), 1)

    @pl.when(step == 0)
    def _():
        hot = one_hot_docs(lengths_ref, docs, length)
        marks = lane < docs + 1
        aug_q[...] = jnp.where(hot & marks, 1.0, 0.0).astype(bf16)
        aug_k[...] = key_marks(hot, lane)

    kk[:, :128] = k_ref[...]
    kk[:, 128:] = aug_k[...]
    vv[:, :128] = v_ref[...]
    vv[:, 128:] = aug_k[...]
    kt[...] = jnp.transpose(k_ref[...])
    scale = 1.0 / math.sqrt(dim)
    low = lane < dim
    q2 = q_ref[...].astype(f32) * scale
    g2 = gmix_ref[...].astype(f32)
    dots = g2 * mixed_ref[...].astype(f32)
    lse_all = lse_ref[...]
    marks_q = aug_q[...].astype(f32)
    for h in range(2):
        mine = low if h == 0 else jnp.logical_not(low)
        lse = jnp.sum(jnp.where(lane == 2 * pair + h, lse_all, 0.0), axis=1, keepdims=True)
        qq[h, :, :128] = jnp.where(mine, q2, 0.0).astype(bf16)
        qq[h, :, 128:] = with_stat(marks_q, -lse, lane)
        delta = jnp.sum(jnp.where(mine, dots, 0.0), axis=1, keepdims=True)
        gg[h, :, :128] = jnp.where(mine, g2, 0.0).astype(bf16)
        gg[h, :, 128:] = with_stat(jnp.zeros_like(marks_q), -delta, lane)
    krow = lax.broadcasted_iota(jnp.int32, (block, block), 0)
    qcol = lax.broadcasted_iota(jnp.int32, (block, block), 1)
    causal = qcol >= krow
    for kb in range(blocks):
        keys = pl.ds(kb * block, block)
        dk = jnp.zeros((block, 128), f32)
        dv = jnp.zeros((block, 128), f32)
        for h in range(2):
            for qb in range(kb, blocks):
                queries = pl.ds(qb * block, block)
                s = lax.dot_general(kk[keys, :], qq[h, queries, :], NT, preferred_element_type=f32)
                if qb == kb:
                    s = jnp.where(causal, s, NEG)
                p = jnp.exp(s)
                dp = lax.dot_general(vv[keys, :], gg[h, queries, :], NT, preferred_element_type=f32)
                ds = (p * dp).astype(bf16)
                dv = dv + lax.dot_general(p.astype(bf16), gg[h, queries, :128], NN, preferred_element_type=f32)
                dk = dk + lax.dot_general(ds, qq[h, queries, :128], NN, preferred_element_type=f32)
                part = lax.dot_general(kt[h * dim:(h + 1) * dim, keys], ds, NN, preferred_element_type=f32)
                if kb == 0:
                    dqt[h * dim:(h + 1) * dim, queries] = part
                else:
                    dqt[h * dim:(h + 1) * dim, queries] += part
        dk_ref[keys, :] = dk.astype(bf16)
        dv_ref[keys, :] = dv.astype(bf16)
    dq_ref[...] = (jnp.transpose(dqt[...]) * scale).astype(bf16)

def attn_bwd(lengths, projected, mixed, gmix, lse, *, first=0, count=4, dim=64, block=512, us=25):
    length, width3 = projected.shape
    width = width3 // 3
    docs = lengths.shape[1]
    pairs = width // 128
    col = lambda off: pl.BlockSpec((length, 128), lambda p: (0, p + off))
    here = pl.BlockSpec((length, 128), lambda p: (0, p))
    one = jax.ShapeDtypeStruct((length, 128 * count), bf16)
    return pl.pallas_call(
        functools.partial(attn_bwd_kernel, docs=docs, dim=dim, block=block, first=first),
        grid=(count,),
        in_specs=[pl.BlockSpec(memory_space=pltpu.SMEM), col(first), col(first + pairs), col(first + 2 * pairs), col(first), col(first),
                  pl.BlockSpec((length, 128), lambda p: (0, 0))],
        out_specs=[here, here, here],
        out_shape=[one, one, one],
        scratch_shapes=[pltpu.VMEM((length, 128), bf16), pltpu.VMEM((length, 128), bf16),
                        pltpu.VMEM((length, 256), bf16), pltpu.VMEM((length, 256), bf16),
                        pltpu.VMEM((2, length, 256), bf16), pltpu.VMEM((2, length, 256), bf16),
                        pltpu.VMEM((128, length), bf16), pltpu.VMEM((128, length), f32)],
        compiler_params=pltpu.CompilerParams(vmem_limit_bytes=LIMIT),
        cost_estimate=spend(us),
        name="attend_back",
    )(lengths, projected, projected, projected, mixed, gmix, lse)


def place_tables(length, width):
    freq = np.exp(np.arange(width // 2, dtype=np.float64) * (-2.0 * math.log(10000.0) / width))
    angles = np.arange(length, dtype=np.float64)[:, None] * freq[None, :]
    return (np.concatenate([np.sin(angles), np.cos(angles)], axis=1).astype(np.float32),
            freq.astype(np.float32)[None, :])

def norm_stats(v):
    center = v - jnp.mean(v, axis=1, keepdims=True)
    inv = lax.rsqrt(jnp.mean(center * center, axis=1, keepdims=True) + 1e-5)
    return center * inv, inv

def front_kernel(lengths_ref, x_ref, table_ref, freq_ref, gain_ref, bias_ref, w_ref,
                 stream_ref, normed_ref, proj_ref, starts, *, docs):
    step = pl.program_id(0)
    rows, width = x_ref.shape
    half = width // 2
    begin, end, _ = doc_bounds(lengths_ref, docs)

    @pl.when(step == 0)
    def _():
        at = jnp.transpose(jnp.broadcast_to(begin.astype(f32), (128, 128)))[:, :1]
        angle = at * freq_ref[...]
        both = jnp.concatenate([jnp.sin(angle), jnp.cos(angle)], axis=1)
        hi = both.astype(bf16)
        mid = (both - hi.astype(f32)).astype(bf16)
        starts[:128, :] = hi
        starts[128:256, :] = mid
        starts[256:, :] = (both - hi.astype(f32) - mid.astype(f32)).astype(bf16)

    place = step * rows + lax.broadcasted_iota(jnp.int32, (rows, 128), 0)
    hot = jnp.where((place >= begin) & (place < end), 1.0, 0.0).astype(bf16)
    start = lax.dot_general(jnp.concatenate([hot, hot, hot], axis=1), starts[...], NN, preferred_element_type=f32)
    sin_b, cos_b = start[:, :half], start[:, half:]
    sin_t, cos_t = table_ref[:, :half], table_ref[:, half:]
    x = x_ref[...].astype(f32)
    stream = jnp.concatenate([x[:, :half] + (sin_t * cos_b - cos_t * sin_b),
                              x[:, half:] + (cos_t * cos_b + sin_t * sin_b)], axis=1)
    stream_ref[...] = stream
    unit, _ = norm_stats(stream)
    normed = (unit * gain_ref[...] + bias_ref[...]).astype(bf16)
    normed_ref[...] = normed
    proj_ref[...] = lax.dot_general(normed, w_ref[...], NN, preferred_element_type=f32).astype(bf16)

def front(lengths, x, gain, bias, w, *, rows=256):
    length, width = x.shape
    table, freq = place_tables(length, width)
    docs = lengths.shape[1]
    blk = pl.BlockSpec((rows, width), lambda i: (i, 0))
    whole = lambda a: pl.BlockSpec(a.shape, lambda i: (0,) * a.ndim)
    return pl.pallas_call(
        functools.partial(front_kernel, docs=docs),
        grid=(length // rows,),
        in_specs=[pl.BlockSpec(memory_space=pltpu.SMEM), blk, blk, whole(freq), whole(gain), whole(bias), whole(w)],
        out_specs=[blk, blk, pl.BlockSpec((rows, w.shape[1]), lambda i: (i, 0))],
        out_shape=[jax.ShapeDtypeStruct((length, width), f32), jax.ShapeDtypeStruct((length, width), bf16),
                   jax.ShapeDtypeStruct((length, w.shape[1]), bf16)],
        scratch_shapes=[pltpu.VMEM((384, width), bf16)],
        compiler_params=pltpu.CompilerParams(vmem_limit_bytes=LIMIT),
        cost_estimate=spend(6),
        name="front",
    )(lengths, x, table, freq, gain, bias, w)

ERF = (0.254829592, -0.284496736, 1.421413741, -1.453152027, 1.061405429)
ERF_P = 0.3275911

def gelu_both(h):
    bell = jnp.exp(h * h * -0.5)
    t = 1.0 / (1.0 + jnp.abs(h) * (ERF_P / math.sqrt(2.0)))
    poly = t * (ERF[0] + t * (ERF[1] + t * (ERF[2] + t * (ERF[3] + t * ERF[4]))))
    tail = 0.5 * poly * bell
    phi = jnp.where(h < 0.0, tail, 1.0 - tail)
    return h * phi, phi + h * bell * (1.0 / math.sqrt(2.0 * math.pi))

def ffn_kernel(stream_ref, mixed_ref, w_out_ref, b_out_ref, gain_ref, bias_ref, w_up_ref, b_up_ref, w_down_ref, b_down_ref,
               after_ref, normed_ref, act_ref, slope_ref, out_ref, *, chunk):
    after = stream_ref[...] + lax.dot_general(mixed_ref[...], w_out_ref[...], NN, preferred_element_type=f32) + b_out_ref[...]
    after_ref[...] = after
    unit, _ = norm_stats(after)
    normed = (unit * gain_ref[...] + bias_ref[...]).astype(bf16)
    normed_ref[...] = normed
    acc = after + b_down_ref[...]
    wide = w_up_ref.shape[1]
    for c in range(wide // chunk):
        cols = pl.ds(c * chunk, chunk)
        hidden = lax.dot_general(normed, w_up_ref[:, cols], NN, preferred_element_type=f32) + b_up_ref[:, cols]
        act, slope = gelu_both(hidden)
        act = act.astype(bf16)
        act_ref[:, cols] = act
        slope_ref[:, cols] = slope.astype(bf16)
        acc = acc + lax.dot_general(act, w_down_ref[cols, :], NN, preferred_element_type=f32)
    out_ref[...] = acc.astype(bf16)

def ffn(stream, mixed, w_out, b_out, gain, bias, w_up, b_up, w_down, b_down, *, rows=256, chunk=512):
    length, width = stream.shape
    wide = w_up.shape[1]
    blk = pl.BlockSpec((rows, width), lambda i: (i, 0))
    big = pl.BlockSpec((rows, wide), lambda i: (i, 0))
    whole = lambda a: pl.BlockSpec(a.shape, lambda i: (0,) * a.ndim)
    args = (w_out, b_out, gain, bias, w_up, b_up, w_down, b_down)
    return pl.pallas_call(
        functools.partial(ffn_kernel, chunk=chunk),
        grid=(length // rows,),
        in_specs=[blk, blk] + [whole(a) for a in args],
        out_specs=[blk, blk, big, big, blk],
        out_shape=[jax.ShapeDtypeStruct((length, width), f32), jax.ShapeDtypeStruct((length, width), bf16),
                   jax.ShapeDtypeStruct((length, wide), bf16), jax.ShapeDtypeStruct((length, wide), bf16),
                   jax.ShapeDtypeStruct((length, width), bf16)],
        compiler_params=pltpu.CompilerParams(vmem_limit_bytes=LIMIT),
        cost_estimate=spend(16),
        name="ffn",
    )(stream, mixed, *args)

def norm_back(g, gain, unit, inv):
    gu = g * gain
    return inv * (gu - jnp.mean(gu, axis=1, keepdims=True) - unit * jnp.mean(gu * unit, axis=1, keepdims=True))

def colsum(x):
    return jnp.sum(x, axis=0, keepdims=True)


def arrange(dst, t, me_ref, ab):
    row8 = t.shape[0] // 8
    for a in range(8):
        r = lax.bitwise_xor(jnp.int32(a), me_ref[0] * 4 + me_ref[1 + ab])
        dst[pl.ds(pl.multiple_of(r * row8, row8), row8), :] = t[a * row8:(a + 1) * row8, :]

def ffn_back_kernel(me_ref, g_ref, act_ref, slope_ref, w_down_ref, w_up_ref, normed_ref, after_ref, gain_ref, mixed_ref, w_out_ref,
                    bdown_ref, send_ref, keep_ref, gafter_ref, gmix_ref, g_low, g_t, norm_t, gh_ref, bup, small):
    i = pl.program_id(0)
    steps = pl.num_programs(0)
    width = g_ref.shape[1]
    tile = slope_ref.shape[1]
    wide = steps * tile
    half = width // 2

    @pl.when(i == 0)
    def _():
        low = g_ref[...].astype(bf16)
        g_low[...] = low
        arrange(g_t, jnp.transpose(low), me_ref, 0)
        arrange(norm_t, jnp.transpose(normed_ref[...]), me_ref, 1)

    def put(at, grad, size):
        cols = pl.ds(pl.multiple_of(at, 128), size)
        keep_ref[:, cols] = grad[:half, :]
        send_ref[:, cols] = grad[half:, :]

    gh = lax.dot_general(g_low[...], w_down_ref[...], NT, preferred_element_type=f32) * slope_ref[...].astype(f32)
    bup[pl.ds(i, 1), :] = colsum(gh)
    gh = gh.astype(bf16)
    gh_ref[:, pl.ds(pl.multiple_of(i * tile, tile), tile)] = gh
    put(i * tile, lax.dot_general(g_t[...], act_ref[...], NN, preferred_element_type=f32).astype(bf16), tile)
    put(i * tile + wide + width, lax.dot_general(norm_t[...], gh, NN, preferred_element_type=f32).astype(bf16), tile)

    @pl.when(i == steps - 1)
    def _():
        unit, inv = norm_stats(after_ref[...])
        gn = lax.dot_general(gh_ref[...], w_up_ref[...], NT, preferred_element_type=f32)
        ga = g_ref[...] + norm_back(gn, gain_ref[...], unit, inv)
        gafter_ref[...] = ga
        low = ga.astype(bf16)
        gmix_ref[...] = lax.dot_general(low, w_out_ref[...], NT, preferred_element_type=f32).astype(bf16)
        arrange(g_t, jnp.transpose(mixed_ref[...]), me_ref, 0)
        put(wide, lax.dot_general(g_t[...], low, NN, preferred_element_type=f32).astype(bf16), width)
        small[...] = jnp.zeros_like(small)
        small[0:1, :] = bdown_ref[...]
        small[1:2, :] = colsum(gn * unit)
        small[2:3, :] = colsum(gn)
        small[3:4, :] = colsum(ga)
        per = width // tile if tile < width else 1
        for k in range(wide // width):
            if tile >= width:
                many = tile // width
                small[4 + k:5 + k, :] = bup[k // many:k // many + 1, (k % many) * width:(k % many + 1) * width]
            else:
                for m in range(per):
                    small[4 + k:5 + k, m * tile:(m + 1) * tile] = bup[k * per + m:k * per + m + 1, :]
        arrange(norm_t.at[:, :128], jnp.transpose(small[...]).astype(bf16), me_ref, 1)
        put(2 * wide + width, norm_t[:, :128], 128)

def ffn_back(me, g, act, slope, w_down, w_up, normed, after, gain, mixed, w_out, bdown, *, tile=512):
    length, width = g.shape
    wide = slope.shape[1]
    steps = wide // tile
    whole = lambda a: pl.BlockSpec(a.shape, lambda i, m: (0,) * a.ndim)
    full = lambda s: pl.BlockSpec(s, lambda i, m: (0,) * len(s))
    sums = (width // 2, 2 * wide + width + 128)
    return pl.pallas_call(
        ffn_back_kernel,
        grid_spec=pltpu.PrefetchScalarGridSpec(
            num_scalar_prefetch=1, grid=(steps,),
            in_specs=[whole(g), pl.BlockSpec((length, tile), lambda i, m: (0, i)), pl.BlockSpec((length, tile), lambda i, m: (0, i)),
                      pl.BlockSpec((tile, width), lambda i, m: (i, 0)),
                      whole(w_up), whole(normed), whole(after), whole(gain), whole(mixed), whole(w_out), whole(bdown)],
            out_specs=[full(sums), full(sums), full((length, width)), full((length, width))],
            scratch_shapes=[pltpu.VMEM((length, width), bf16), pltpu.VMEM((width, length), bf16), pltpu.VMEM((width, length), bf16),
                            pltpu.VMEM((length, wide), bf16), pltpu.VMEM((steps, tile), f32), pltpu.VMEM((128, width), f32)]),
        out_shape=[jax.ShapeDtypeStruct(sums, bf16)] * 2
        + [jax.ShapeDtypeStruct((length, width), f32), jax.ShapeDtypeStruct((length, width), bf16)],
        compiler_params=pltpu.CompilerParams(vmem_limit_bytes=LIMIT),
        cost_estimate=spend(20),
        name="ffn_back",
    )(me, g, act, slope, w_down, w_up, normed, after, gain, mixed, w_out, bdown)

def window(refs, start, size):
    found, at = [], 0
    for ref in refs:
        low, high = max(start, at), min(start + size, at + ref.shape[1])
        if low < high:
            found.append(ref[:, low - at:high - at])
        at += ref.shape[1]
    return found[0] if len(found) == 1 else jnp.concatenate(found, axis=1)

def qkv_grad_kernel(me_ref, *refs, parts):
    gps, (stream_ref, gain_ref, bias_ref, w_ref, send_ref, keep_ref, unit_t, rows_t) = refs[:parts], refs[parts:]
    length, width = stream_ref.shape
    half = width // 2
    unit, _ = norm_stats(stream_ref[...])
    t = jnp.transpose(unit.astype(bf16))
    column_of = lambda row: jnp.transpose(jnp.broadcast_to(row, (128, width)))
    gain, bias = column_of(gain_ref[...]), column_of(bias_ref[...])
    for ab in range(2):
        arrange(unit_t.at[ab], t, me_ref, ab)
    gains, biases, ws = [], [], []
    for ab in range(2):
        arrange(rows_t, gain, me_ref, ab)
        gains.append(rows_t[:, :1])
        arrange(rows_t, bias, me_ref, ab)
        biases.append(rows_t[:, :1])
    total = 3 * width
    cut = total // 2
    gain_grad = [jnp.zeros((width, 1), f32), jnp.zeros((width, 1), f32)]
    bias_grad = [jnp.zeros((width, 1), f32), jnp.zeros((width, 1), f32)]
    for at in range(0, total, 256):
        ab = 0 if at < cut else 1
        gp = window(gps, at, 256)
        m = lax.dot_general(unit_t[ab], gp, NN, preferred_element_type=f32)
        s = colsum(gp.astype(f32))
        grad = (m * gains[ab] + biases[ab] * s).astype(bf16)
        keep_ref[:, at:at + 256] = grad[:half, :]
        send_ref[:, at:at + 256] = grad[half:, :]
        arrange_w = []
        row8 = width // 8
        for r in range(8):
            a = lax.bitwise_xor(jnp.int32(r), me_ref[0] * 4 + me_ref[1 + ab])
            arrange_w.append(w_ref[pl.ds(pl.multiple_of(a * row8, row8), row8), at:at + 256])
        w = jnp.concatenate(arrange_w, axis=0).astype(f32)
        gain_grad[ab] = gain_grad[ab] + jnp.sum(m * w, axis=1, keepdims=True)
        bias_grad[ab] = bias_grad[ab] + jnp.sum(w * s, axis=1, keepdims=True)
    row8 = width // 8
    lane = lax.broadcasted_iota(jnp.int32, (1, 128), 1)
    both = [jnp.where(lane == 0, gain_grad[ab], jnp.where(lane == 1, bias_grad[ab], 0.0)) for ab in range(2)]
    for r in range(8):
        to = lax.bitwise_xor(jnp.int32(r), lax.bitwise_xor(me_ref[1], me_ref[2]))
        rows_t[pl.ds(pl.multiple_of(to * row8, row8), row8), :] = both[0][r * row8:(r + 1) * row8, :]
    small = (rows_t[...] + both[1]).astype(bf16)
    keep_ref[:, total:] = small[:half, :]
    send_ref[:, total:] = small[half:, :]

def qkv_grad(me, gps, stream, gain, bias, w):
    length, width = stream.shape
    vm = pl.BlockSpec(memory_space=pltpu.VMEM)
    parts = len(gps)
    return pl.pallas_call(
        functools.partial(qkv_grad_kernel, parts=parts),
        in_specs=[pl.BlockSpec(memory_space=pltpu.SMEM)] + [vm] * (parts + 4),
        out_specs=[vm, vm],
        out_shape=[jax.ShapeDtypeStruct((width // 2, 3 * width + 128), bf16)] * 2,
        scratch_shapes=[pltpu.VMEM((2, width, length), bf16), pltpu.VMEM((width, 128), f32)],
        compiler_params=pltpu.CompilerParams(vmem_limit_bytes=LIMIT),
        cost_estimate=spend(5),
        name="qkv_grad",
    )(me, *gps, stream, gain, bias, w)

def front_back_kernel(*refs, parts):
    gps, (w_ref, stream_ref, gafter_ref, gain_ref, out_ref) = refs[:parts], refs[parts:]
    gp = window(gps, 0, w_ref.shape[1])
    gn = lax.dot_general(gp, w_ref[...], NT, preferred_element_type=f32)
    unit, inv = norm_stats(stream_ref[...])
    out_ref[...] = (gafter_ref[...] + norm_back(gn, gain_ref[...], unit, inv)).astype(bf16)

def front_back(gps, w, stream, gafter, gain, *, rows=256):
    length, width = stream.shape
    blk = pl.BlockSpec((rows, width), lambda i: (i, 0))
    whole = lambda a: pl.BlockSpec(a.shape, lambda i: (0,) * a.ndim)
    return pl.pallas_call(
        functools.partial(front_back_kernel, parts=len(gps)),
        grid=(length // rows,),
        in_specs=[pl.BlockSpec((rows, gp.shape[1]), lambda i: (i, 0)) for gp in gps] + [whole(w), blk, blk, whole(gain)],
        out_specs=blk,
        out_shape=jax.ShapeDtypeStruct((length, width), bf16),
        compiler_params=pltpu.CompilerParams(vmem_limit_bytes=LIMIT),
        cost_estimate=spend(5),
        name="front_back",
    )(*gps, w, stream, gafter, gain)


def finish_kernel(me_ref, own_a, own_b, got_a, got_b, *refs, plan, n):
    outs, whole = refs[:-1], refs[-1]
    rows, cut = own_a.shape
    chunk = rows // (4 * n)

    def lay(dst, at, size):
        ab = 0 if at < cut else 1
        at -= ab * cut
        for near, ref in ((0, (own_a, own_b)[ab]), (1, (got_a, got_b)[ab])):
            core = lax.bitwise_xor(jnp.int32(near), me_ref[0])
            for pq in range(4):
                for z in range(n):
                    to = core * 4 + lax.bitwise_xor(jnp.int32(pq), me_ref[1 + ab])
                    to = to * n + lax.bitwise_xor(jnp.int32(z), me_ref[3])
                    r = (pq * n + z) * chunk
                    dst[pl.ds(pl.multiple_of(to * chunk, chunk), chunk), :] = ref[r:r + chunk, at:at + size].astype(f32)

    for at, size, out, col, turned in plan:
        if out < 0:
            lay(whole.at[:, :size], at, size)
            flat = jnp.transpose(whole[:, :size])
            done = 0
            for v in outs[out:]:
                width = flat.shape[1]
                for k in range(v.shape[1] // width):
                    v[:, k * width:(k + 1) * width] = flat[done:done + 1, :]
                    done += 1
        elif not turned:
            lay(outs[out].at[:, col:col + size], at, size)
        else:
            lay(whole.at[:, :size], at, size)
            flat = jnp.transpose(whole[:, :size])
            outs[out][col:col + size, :] = flat[:outs[out].shape[0] - col, :]

def finish(me, pieces, shapes, plan, *, n, us):
    rows = pieces[0].shape[0]
    vm = pl.BlockSpec(memory_space=pltpu.VMEM)
    return pl.pallas_call(
        functools.partial(finish_kernel, plan=plan, n=n),
        in_specs=[pl.BlockSpec(memory_space=pltpu.SMEM)] + [vm] * 4,
        out_specs=[vm] * len(shapes),
        out_shape=[jax.ShapeDtypeStruct(s, f32) for s in shapes],
        scratch_shapes=[pltpu.VMEM((2 * rows, 256), f32)],
        compiler_params=pltpu.CompilerParams(vmem_limit_bytes=LIMIT),
        cost_estimate=spend(us),
        name="finish",
    )(me, *pieces)

class Links:
    def __init__(self, mesh):
        self.sizes = dict(mesh.shape)
        self.n = self.sizes["rows"] // 2
        self.fine = self.n == 4
        self.zi = lax.axis_index("rows") // 2

    def swap(self, x, axis, bit):
        return lax.ppermute(x, axis, [(a, a ^ bit) for a in range(self.sizes[axis])])

    def core(self, x):
        return self.swap(x, "bank", 1)

    def near(self, x):
        return self.swap(x, "bank", 2)

    def side(self, x):
        return self.swap(x, "rows", 1)

def plus(*terms):
    out = terms[0].astype(f32)
    for t in terms[1:]:
        out = out + t.astype(f32)
    return out.astype(bf16)

def chain(links, send, keep, cut):
    n = links.n
    got, = yield [(links.core, send)]
    half = keep.shape[0] // 2
    sa, sb = plus(keep[half:, :cut], got[half:, :cut]), plus(keep[half:, cut:], got[half:, cut:])
    a, b = plus(keep[:half, :cut], got[:half, :cut]), plus(keep[:half, cut:], got[:half, cut:])
    ra, rb = yield [(links.near, sa), (links.side, sb)]
    half //= 2
    sa, sb = plus(a[half:], ra[half:]), plus(b[half:], rb[half:])
    a, b = plus(a[:half], ra[:half]), plus(b[:half], rb[:half])
    ra, rb = yield [(links.side, sa), (links.near, sb)]
    z = jnp.concatenate([plus(a, ra), plus(b, rb)], axis=1)
    chunk = half // n
    if links.fine:
        piece = lambda k: lax.dynamic_slice(z, ((links.zi ^ k) * chunk, 0), (chunk, z.shape[1]))
        hops = [functools.partial(links.swap, axis="rows", bit=2 * k) for k in range(1, n)]
        got = yield [(hop, piece(k + 1)) for k, hop in enumerate(hops)]
        mine = plus(piece(0), *got)
        got = yield [(hop, mine) for hop in hops]
        a = jnp.concatenate([v[:, :cut] for v in (mine, *got)], axis=0)
        b = jnp.concatenate([v[:, cut:] for v in (mine, *got)], axis=0)
    else:
        groups = [[r for r in range(2 * n) if r % 2 == y] for y in range(2)]
        z, = yield [(lambda v: lax.psum(v, "rows", axis_index_groups=groups), z)]
        yield []
        a, b = z[:, :cut], z[:, cut:]
    ra, rb = yield [(links.side, a), (links.near, b)]
    a, b = jnp.concatenate([a, ra], axis=0), jnp.concatenate([b, rb], axis=0)
    ra, rb = yield [(links.near, a), (links.side, b)]
    a, b = jnp.concatenate([a, ra], axis=0), jnp.concatenate([b, rb], axis=0)
    ga, gb = yield [(links.core, a), (links.core, b)]
    yield (a, b, ga, gb)

class Step:
    def __init__(self, *args):
        self.run = chain(*args)
        self.sends = next(self.run)

    def go(self):
        self.got = [how(what) for how, what in self.sends]

    def take(self):
        self.sends = self.run.send(self.got)

def tie(steps, *extra):
    flat = [what for s in steps for _, what in s.sends] + list(extra)
    flat = list(lax.optimization_barrier(tuple(flat)))
    for s in steps:
        s.sends = [(how, flat.pop(0)) for how, _ in s.sends]
    return flat

def tiles_of(start, width, out, turned):
    plan, at = [], 0
    while at < width:
        size = min(256, width - at)
        plan.append((start + at, size, out, at, turned))
        at += size
    return plan

def body(mesh, hidden_in, lengths, ln1_gain, ln1_bias, w_qkv, w_out, b_out, ln2_gain, ln2_bias, w_up, b_up, w_down, b_down,
         bank, bank_labels, target_slots, gold_ids):
    links = Links(mesh)
    row = lambda v: v.reshape(1, -1)
    width = hidden_in.shape[1]
    wide = w_up.shape[1]
    ib, ir = lax.axis_index("bank"), lax.axis_index("rows")
    core, x, y = ib % 2, ib // 2, ir % 2
    me = jnp.stack([core, x * 2 + y, y * 2 + x, links.zi if links.fine else 0]).astype(jnp.int32)
    bank_all = lax.all_gather(bank, "bank", axis=0, tiled=True)
    labels_all = lax.all_gather(bank_labels, "bank", axis=0, tiled=True)
    stream, normed_a, projected = front(lengths, hidden_in, row(ln1_gain), row(ln1_bias), w_qkv)
    mixed, lse = attn_fwd(lengths, projected, block=512)
    after, normed_c, act, slope, block_out = ffn(stream, mixed, w_out, row(b_out), row(ln2_gain), row(ln2_bias), w_up, row(b_up),
                                                 w_down, row(b_down), chunk=256)
    g, loss, bdown = bank_call(lengths, block_out, gold_ids, target_slots, labels_all, bank_all, edt=f32)
    send, keep, gafter, gmix = ffn_back(me, g, act, slope, w_down, w_up, normed_c, after, row(ln2_gain), mixed, w_out, bdown)
    cut = wide + width
    n = links.n if links.fine else 1
    one = Step(links, send, keep, cut)
    one.go()
    parts = []
    back = lambda first, count: parts.append(attn_bwd(lengths, projected, mixed, gmix, lse, first=first, count=count, us=6.5 * count))
    back(0, 1)
    one.take()
    gmix, = tie([one], gmix)
    one.go()
    back(1, 2)
    one.take()
    gmix, = tie([one], gmix, )
    one.go()
    back(3, 1)
    one.take()
    gps = [p[k] for k in range(3) for p in parts]
    gps[0], = tie([one], gps[0])
    one.go()
    send, keep = qkv_grad(me, gps, stream, row(ln1_gain), row(ln1_bias), w_qkv)
    cut2 = 3 * width // 2
    two = Step(links, send, keep, cut2)
    two.go()
    for slot in range(4):
        one.take()
        two.take()
        if slot == 0:
            gafter, = tie([one, two], gafter)
        elif slot == 1:
            input_grad, = tie([one, two], input_grad)
        else:
            tie([one, two])
        one.go()
        two.go()
        if slot == 0:
            input_grad = front_back(gps, w_qkv, stream, gafter, row(ln1_gain))
    one.take()
    two.take()
    two.go()
    vector = (1, width)
    two.take()
    pieces = tie([two], *one.sends)
    two.go()
    w_down_grad, w_out_grad, w_up_grad, *small = finish(
        me, pieces, [(wide, width), (width, width), (width, wide)] + [vector] * 4 + [(1, wide)],
        tiles_of(0, wide, 0, True) + tiles_of(wide, width, 1, False) + tiles_of(cut, wide, 2, False) + tiles_of(cut + wide, 128, -5, True),
        n=n, us=8)
    two.take()
    w_down_grad, = tie([two], w_down_grad)
    two.go()
    two.take()
    w_qkv_grad, *small1 = finish(me, two.sends, [(width, 3 * width), vector, vector],
                                 tiles_of(0, 3 * width, 0, False) + tiles_of(3 * width, 128, -2, True), n=n, us=4)
    flat = lambda v: v.reshape(-1)
    return (block_out, flat(loss), input_grad, flat(small1[0]), flat(small1[1]), w_qkv_grad, w_out_grad, flat(small[3]),
            flat(small[1]), flat(small[2]), w_up_grad, flat(small[4]), w_down_grad, flat(small[0]))

def solution(mesh):
    in_specs = (
        P(("rows", "bank"), None),
        P(("rows", "bank"), None),
        P(),
        P(),
        P(),
        P(),
        P(),
        P(),
        P(),
        P(),
        P(),
        P(),
        P(),
        P("bank", None),
        P("bank"),
        P(("rows", "bank")),
        P(("rows", "bank")),
    )
    out_specs = (
        P(("rows", "bank"), None),
        P(("rows", "bank")),
        P(("rows", "bank"), None),
        P(),
        P(),
        P(),
        P(),
        P(),
        P(),
        P(),
        P(),
        P(),
        P(),
        P(),
    )
    return jax.shard_map(functools.partial(body, mesh), mesh=mesh, in_specs=in_specs, out_specs=out_specs, check_vma=False)
```

```python
import functools
import math

import jax
import jax.numpy as jnp
import numpy as np
from jax import lax
from jax.experimental import pallas as pl
from jax.experimental.pallas import tpu as pltpu
from jax.sharding import PartitionSpec as P

LOG2E = 1.4426950408889634
LN2 = 0.6931471805599453
NT = (((1,), (1,)), ((), ()))
NN = (((1,), (0,)), ((), ()))
f32, bf16 = jnp.float32, jnp.bfloat16

LIMIT = 60 * 2 ** 20

def spend(us):
    return pl.CostEstimate(flops=int(us * 1.0e9), bytes_accessed=0, transcendentals=0)

def column(row, rows):
    return jnp.transpose(jnp.broadcast_to(row.astype(f32), (128, rows)))[:, :1]

class Slots:
    def __init__(self, bank_ref, marks_ref, gold_ref, target_ref, rows, tile, strip):
        self.bank_ref, self.marks_ref, self.gold_ref, self.target_ref = bank_ref, marks_ref, gold_ref, target_ref
        self.rows, self.tile, self.strip = rows, tile, strip
        self.width = bank_ref.shape[1]
        self.c = LOG2E / math.sqrt(self.width)

    def wide(self, col):
        return jnp.concatenate([col] * (self.tile // 128), axis=1)

    def keys(self, j):
        return self.bank_ref[pl.ds(pl.multiple_of(j * self.tile, self.tile), self.tile), :]

    def positive(self, j, at):
        tall = lambda v: jnp.concatenate([v] * (self.strip // 8), axis=0)
        mine = pl.ds(at, self.strip)
        return (tall(self.marks_ref[0, j]) == self.wide(self.gold_ref[mine, :])) | (
            tall(self.marks_ref[1, j]) == self.wide(self.target_ref[mine, :]))

    def fold(self, x, op):
        out = x[:, :128]
        for i in range(1, self.tile // 128):
            out = op(out, x[:, i * 128:(i + 1) * 128])
        return out

    def scores(self, q, j):
        return lax.dot_general(q, self.keys(j), NT, preferred_element_type=f32)

    def eat(self, j, s_ref, e_ref, at, top_ref, all_ref, pos_ref, hist_ref):
        for r in range(0, self.rows, self.strip):
            mine = pl.ds(r, self.strip)
            s = s_ref[mine, :]
            top = top_ref[mine, :]
            new_top = jnp.maximum(top, jnp.max(self.fold(s, jnp.maximum), axis=1, keepdims=True) * self.c)
            shrink = jnp.exp2(top - new_top)
            e = jnp.exp2(s * self.c - self.wide(new_top))
            e_ref[at, mine, :] = e
            all_ref[mine, :] = all_ref[mine, :] * shrink + self.fold(e, jnp.add)
            pos_ref[mine, :] = pos_ref[mine, :] * shrink + self.fold(jnp.where(self.positive(j, r), e, 0.0), jnp.add)
            top_ref[mine, :] = new_top
            hist_ref[at, mine, :] = new_top

    def eat_all(self, q, first, count, s0_ref, s1_ref, e_ref, top_ref, all_ref, pos_ref, hist_ref):
        bufs = (s0_ref, s1_ref)
        bufs[0][...] = self.scores(q, first)
        for k in range(count):
            if k + 1 < count:
                bufs[(k + 1) % 2][...] = self.scores(q, first + k + 1)
            self.eat(first + k, bufs[k % 2], e_ref, k, top_ref, all_ref, pos_ref, hist_ref)

def fetch(shards, bank_ref, label_ref, sems):
    size = bank_ref.shape[0] // len(shards)
    copies = []
    for k, ref in enumerate(shards):
        copies.append((pltpu.make_async_copy(ref.at[pl.ds(0, size)], bank_ref.at[pl.ds(k * size, size)], sems.at[2 * k]),
                       pltpu.make_async_copy(ref.at[pl.ds(size, 16)], label_ref.at[k], sems.at[2 * k + 1])))
    return copies

def write_marks(label_ref, marks_ref, shard):
    tiles, _, tile = marks_ref.shape[1:]
    width = label_ref.shape[2]
    for j in range(tiles):
        owner, at = j * tile // shard, j * tile % shard // width
        for k in range(tile // width):
            marks_ref[0, j, :, k * width:(k + 1) * width] = jnp.broadcast_to(label_ref[owner, at + k:at + k + 1, :].astype(f32), (8, width))
        marks_ref[1, j] = (lax.broadcasted_iota(jnp.int32, (8, tile), 1) + j * tile).astype(f32)

def write_wanted(me_ref, gold_ref, target_ref, gold_b, target_b, shard, rows):
    turn = lambda row: jnp.transpose(jnp.broadcast_to(row.astype(f32), (128, rows)))
    gold_b[...] = turn(gold_ref[...])
    target_b[...] = turn(lax.bitwise_xor(target_ref[...], me_ref[4] * shard))

def bank_first_kernel(me_ref, q_ref, gold_ref, target_ref, own_hbm, core_hbm, e_ref, hist_ref, sums_ref,
                      bank_ref, label_ref, marks_ref, gold_b, target_b, top_ref, all_ref, pos_ref, s0_ref, s1_ref, sems,
                      *, rows, tile, strip):
    step = pl.program_id(0)
    tiles = bank_ref.shape[0] // tile
    shard = bank_ref.shape[0] // 2
    copies = fetch((own_hbm, core_hbm), bank_ref, label_ref, sems)

    @pl.when(step == 0)
    def _():
        for pair in copies:
            for copy in pair:
                copy.start()
        for pair in copies:
            for copy in pair:
                copy.wait()
        write_marks(label_ref, marks_ref, shard)
    write_wanted(me_ref, gold_ref, target_ref, gold_b, target_b, shard, rows)
    know = Slots(bank_ref, marks_ref, gold_b, target_b, rows, tile, strip)
    top_ref[...] = jnp.full((rows, 128), -3e38, f32)
    all_ref[...] = jnp.zeros((rows, 128), f32)
    pos_ref[...] = jnp.zeros((rows, 128), f32)
    know.eat_all(q_ref[...], 0, tiles, s0_ref, s1_ref, e_ref, top_ref, all_ref, pos_ref, hist_ref)
    sums_ref[0] = all_ref[...]
    sums_ref[1] = pos_ref[...]

def bank_last_kernel(me_ref, lengths_ref, q_ref, gold_ref, target_ref, e_ref, hist_ref, sums_ref, own_hbm, core_hbm, near_hbm, far_hbm,
                     grad_ref, loss_ref, bsum_ref,
                     bank_ref, label_ref, marks_ref, gold_b, target_b, top_ref, all_ref, pos_ref, on_ref, off_ref, g_ref, g2_ref,
                     s0_ref, s1_ref, e2_ref, hist2_ref, sems, *, rows, tile, docs, strip):
    step = pl.program_id(0)
    width = q_ref.shape[1]
    tiles = bank_ref.shape[0] // tile
    half = tiles // 2
    shard = bank_ref.shape[0] // 4
    copies = fetch((own_hbm, core_hbm, near_hbm, far_hbm), bank_ref, label_ref, sems)

    @pl.when(step == 0)
    def _():
        for pair in copies[2:] + copies[:2]:
            for copy in pair:
                copy.start()
        for pair in copies:
            pair[1].wait()
        for pair in copies[2:]:
            pair[0].wait()
        write_marks(label_ref, marks_ref, shard)
    write_wanted(me_ref, gold_ref, target_ref, gold_b, target_b, shard, rows)
    know = Slots(bank_ref, marks_ref, gold_b, target_b, rows, tile, strip)
    q = q_ref[...]
    total = lengths_ref[0, 0]
    for j in range(1, docs):
        total = total + lengths_ref[0, j]
    live = step * rows + lax.broadcasted_iota(jnp.int32, (rows, 128), 0) < total
    top_ref[...] = hist_ref[half - 1]
    all_ref[...] = sums_ref[0]
    pos_ref[...] = sums_ref[1]
    know.eat_all(q, half, half, s0_ref, s1_ref, e2_ref, top_ref, all_ref, pos_ref, hist2_ref)
    broad = lambda col: jnp.broadcast_to(col, (rows, 128))
    top = top_ref[...]
    sum_all = broad(jnp.sum(all_ref[...], axis=1, keepdims=True))
    sum_pos = broad(jnp.sum(pos_ref[...], axis=1, keepdims=True))
    inv_all = jnp.where(live, 1.0 / sum_all, 0.0)
    off_ref[...] = inv_all
    on_ref[...] = inv_all - jnp.where(live, 1.0 / sum_pos, 0.0)

    def show(loss):
        loss_ref[...] = jnp.transpose(jnp.where(live, loss, 0.0))[:1, :]
    show((jnp.log2(sum_all) - jnp.log2(sum_pos)) * LN2)

    safe = jnp.min(sum_pos) >= 2.0 ** -60

    def pull(source, hists, j, at, g_ref):
        for r in range(0, rows, strip):
            mine = pl.ds(r, strip)
            factor = jnp.exp2(hists[at, mine, :] - top_ref[mine, :])
            weight = jnp.where(know.positive(j, r), know.wide(factor * on_ref[mine, :]), know.wide(factor * off_ref[mine, :]))
            g_ref[mine, :] = (source[at, mine, :] * weight).astype(bf16)
        return lax.dot_general(g_ref[...], know.keys(j), NN, preferred_element_type=f32)

    @pl.when(step == 0)
    def _():
        for pair in copies[:2]:
            pair[0].wait()

    @pl.when(safe)
    def _():
        acc = None
        for j in range(tiles):
            near = j >= half
            term = pull(e2_ref if near else e_ref, hist2_ref if near else hist_ref, j, j - half if near else j, (g_ref, g2_ref)[j % 2])
            acc = term if acc is None else acc + term
        grad_ref[...] = acc

    @pl.when(jnp.logical_not(safe))
    def _():
        grad_ref[...] = jnp.zeros_like(grad_ref)
        all_ref[...] = jnp.where(live, top + jnp.log2(sum_all), 1e30)
        top_ref[...] = jnp.full((rows, 128), -1e30, f32)
        pos_ref[...] = jnp.zeros((rows, 128), f32)

        def own_top(j, _):
            s0_ref[...] = know.scores(q, j)
            for r in range(0, rows, strip):
                mine = pl.ds(r, strip)
                x = jnp.where(know.positive(j, r), s0_ref[mine, :] * know.c, -1e30)
                top_ref[mine, :] = jnp.maximum(top_ref[mine, :], know.fold(x, jnp.maximum))
            return 0
        lax.fori_loop(0, tiles, own_top, 0)
        top_ref[...] = broad(jnp.max(top_ref[...], axis=1, keepdims=True))

        def own_sum(j, _):
            s0_ref[...] = know.scores(q, j)
            for r in range(0, rows, strip):
                mine = pl.ds(r, strip)
                x = jnp.where(know.positive(j, r), s0_ref[mine, :] * know.c, -1e30)
                pos_ref[mine, :] += know.fold(jnp.exp2(x - know.wide(top_ref[mine, :])), jnp.add)
            return 0
        lax.fori_loop(0, tiles, own_sum, 0)
        lse_pos = top_ref[...] + jnp.log2(broad(jnp.sum(pos_ref[...], axis=1, keepdims=True)))
        show((top + jnp.log2(sum_all) - lse_pos) * LN2)
        pos_ref[...] = jnp.where(live, lse_pos, 1e30)

        def draw(j, _):
            s0_ref[...] = know.scores(q, j)
            for r in range(0, rows, strip):
                mine = pl.ds(r, strip)
                s = s0_ref[mine, :] * know.c
                x = jnp.where(know.positive(j, r), s, -1e30)
                g = jnp.exp2(s - know.wide(all_ref[mine, :])) - jnp.exp2(x - know.wide(pos_ref[mine, :]))
                g_ref[mine, :] = g.astype(bf16)
            grad_ref[...] += lax.dot_general(g_ref[...], know.keys(j), NN, preferred_element_type=f32)
            return 0
        lax.fori_loop(0, tiles, draw, 0)
    grad_ref[...] = grad_ref[...] * (1.0 / math.sqrt(width))
    part = jnp.sum(grad_ref[...], axis=0, keepdims=True)
    bsum_ref[...] = jnp.where(step == 0, part, bsum_ref[...] + part)

def with_labels(bank, labels):
    width = bank.shape[1]
    rows = labels.astype(bf16).reshape(-1, width)
    return jnp.concatenate([bank, jnp.pad(rows, ((0, 16 - rows.shape[0]), (0, 0)))], axis=0)

def bank_specs(rows, width):
    smem, hbm = pl.BlockSpec(memory_space=pltpu.SMEM), pl.BlockSpec(memory_space=pl.ANY)
    blk = pl.BlockSpec((rows, width), lambda i: (i, 0))
    line = pl.BlockSpec((1, rows), lambda i: (0, i))
    return smem, hbm, blk, line

def bank_first(me, q, gold, target, own, core, *, rows=256, tile=1024, strip=32):
    length, width = q.shape
    tiles = 2 * (own.shape[0] - 16) // tile
    smem, hbm, blk, line = bank_specs(rows, width)
    part = pltpu.VMEM((rows, 128), f32)
    return pl.pallas_call(
        functools.partial(bank_first_kernel, rows=rows, tile=tile, strip=strip),
        grid=(length // rows,),
        in_specs=[smem, blk, line, line, hbm, hbm],
        out_specs=[pl.BlockSpec((tiles, rows, tile), lambda i: (0, i, 0)), pl.BlockSpec((tiles, rows, 128), lambda i: (0, i, 0)),
                   pl.BlockSpec((2, rows, 128), lambda i: (0, i, 0))],
        out_shape=[jax.ShapeDtypeStruct((tiles, length, tile), f32), jax.ShapeDtypeStruct((tiles, length, 128), f32),
                   jax.ShapeDtypeStruct((2, length, 128), f32)],
        scratch_shapes=[pltpu.VMEM((tiles * tile, width), bf16), pltpu.VMEM((2, 16, width), bf16), pltpu.VMEM((2, tiles, 8, tile), f32),
                        part, part, part, part, part,
                        pltpu.VMEM((rows, tile), f32), pltpu.VMEM((rows, tile), f32), pltpu.SemaphoreType.DMA((4,))],
        compiler_params=pltpu.CompilerParams(vmem_limit_bytes=LIMIT),
        cost_estimate=spend(13),
        name="bank_first",
    )(me, q, gold.reshape(1, length), target.reshape(1, length), own, core)

def bank_last(me, lengths, q, gold, target, e, hist, sums, own, core, near, far, *, rows=256, tile=1024, strip=32):
    length, width = q.shape
    half = e.shape[0]
    docs = lengths.shape[1]
    smem, hbm, blk, line = bank_specs(rows, width)
    part = pltpu.VMEM((rows, 128), f32)
    return pl.pallas_call(
        functools.partial(bank_last_kernel, rows=rows, tile=tile, docs=docs, strip=strip),
        grid=(length // rows,),
        in_specs=[smem, smem, blk, line, line, pl.BlockSpec((half, rows, tile), lambda i: (0, i, 0)),
                  pl.BlockSpec((half, rows, 128), lambda i: (0, i, 0)), pl.BlockSpec((2, rows, 128), lambda i: (0, i, 0)),
                  hbm, hbm, hbm, hbm],
        out_specs=[blk, line, pl.BlockSpec((1, width), lambda i: (0, 0))],
        out_shape=[jax.ShapeDtypeStruct((length, width), f32), jax.ShapeDtypeStruct((1, length), f32),
                   jax.ShapeDtypeStruct((1, width), f32)],
        scratch_shapes=[pltpu.VMEM((2 * half * tile, width), bf16), pltpu.VMEM((4, 16, width), bf16),
                        pltpu.VMEM((2, 2 * half, 8, tile), f32),
                        part, part, part, part, part, part, part, pltpu.VMEM((rows, tile), bf16), pltpu.VMEM((rows, tile), bf16),
                        pltpu.VMEM((rows, tile), f32), pltpu.VMEM((rows, tile), f32), pltpu.VMEM((half, rows, tile), f32),
                        pltpu.VMEM((half, rows, 128), f32), pltpu.SemaphoreType.DMA((8,))],
        compiler_params=pltpu.CompilerParams(vmem_limit_bytes=LIMIT),
        cost_estimate=spend(25),
        name="bank_last",
    )(me, lengths, q, gold.reshape(1, length), target.reshape(1, length), e, hist, sums, own, core, near, far)

TN = (((0,), (0,)), ((), ()))
BIG = 1e30
STAT = 120
NEG = -1e30

def doc_bounds(lengths_ref, docs):
    lane = lax.broadcasted_iota(jnp.int32, (1, 128), 1)
    begin = jnp.zeros((1, 128), jnp.int32)
    end = jnp.zeros((1, 128), jnp.int32)
    at = jnp.int32(0)
    for j in range(docs):
        begin = jnp.where(lane == j, at, begin)
        at = at + lengths_ref[0, j]
        end = jnp.where(lane == j, at, end)
    begin = jnp.where(lane == docs, at, begin)
    end = jnp.where(lane == docs, 2 ** 30, end)
    return begin, end, at

def one_hot_docs(lengths_ref, docs, length):
    begin, end, _ = doc_bounds(lengths_ref, docs)
    place = lax.broadcasted_iota(jnp.int32, (length, 128), 0)
    return (place >= begin) & (place < end)

def split3(col):
    hi = col.astype(bf16).astype(f32)
    mid = (col - hi).astype(bf16).astype(f32)
    lo = col - hi - mid
    return hi, mid, lo

def with_stat(base, col, lane):
    hi, mid, lo = split3(col)
    return jnp.where(lane == STAT, hi, jnp.where(lane == STAT + 1, mid, jnp.where(lane == STAT + 2, lo, base))).astype(bf16)

def key_marks(hot, lane):
    ones = (lane >= STAT) & (lane < STAT + 3)
    return jnp.where(ones, 1.0, jnp.where(hot, 0.0, -BIG)).astype(bf16)

def attn_fwd_kernel(lengths_ref, q_ref, k_ref, v_ref, mixed_ref, lse_ref, aug_q, aug_k, kk, s_0, s_1, e_0, e_1, scales, held,
                    *, docs, dim, block, strip):
    s_refs, e_refs = (s_0, s_1), (e_0, e_1)
    pair = pl.program_id(0)
    length = q_ref.shape[0]
    lane = lax.broadcasted_iota(jnp.int32, (1, 128), 1)

    @pl.when(pair == 0)
    def _():
        hot = one_hot_docs(lengths_ref, docs, length)
        marks = lane < docs + 1
        aug_q[...] = jnp.where(hot & marks, 1.0, 0.0).astype(bf16)
        aug_k[...] = key_marks(hot, lane)
        lse_ref[...] = jnp.zeros_like(lse_ref)

    kk[:, :128] = k_ref[...]
    kk[:, 128:] = aug_k[...]
    scale = 1.0 / math.sqrt(dim)
    first = lane < dim
    jobs = [(b, h) for b in range(length // block) for h in range(2)]

    def score(k):
        b, h = jobs[k]
        rows = pl.ds(b * block, block)
        mine = first if h == 0 else jnp.logical_not(first)
        qq = jnp.concatenate([jnp.where(mine, q_ref[rows, :].astype(f32) * scale, 0.0).astype(bf16), aug_q[rows, :]], axis=1)
        s_refs[k % 2][:, :(b + 1) * block] = lax.dot_general(qq, kk[:(b + 1) * block, :], NT, preferred_element_type=f32)

    def soften(k):
        b, h = jobs[k]
        s_ref, e_ref, many = s_refs[k % 2], e_refs[k % 2], (b + 1) * block
        for r in range(0, block, strip):
            mine = pl.ds(r, strip)
            row = lax.broadcasted_iota(jnp.int32, (strip, block), 0) + r
            col = lax.broadcasted_iota(jnp.int32, (strip, block), 1)
            s = jnp.where(row >= col, s_ref[mine, b * block:many], NEG)
            if b > 0:
                s = jnp.concatenate([s_ref[mine, :b * block], s], axis=1)
            top = jnp.max(s, axis=1, keepdims=True)
            e = jnp.exp(s - top)
            total = jnp.sum(e, axis=1, keepdims=True)
            e_ref[mine, :many] = e.astype(bf16)
            scales[k % 2, mine, :] = jnp.broadcast_to(1.0 / total, (strip, 128))
            at = pl.ds(b * block + r, strip)
            lse_ref[at, :] = jnp.where(lane == 2 * pair + h, top + jnp.log(total), lse_ref[at, :])

    def mix(k):
        b, h = jobs[k]
        many = (b + 1) * block
        o = lax.dot_general(e_refs[k % 2][:, :many], v_ref[:many, :], NN, preferred_element_type=f32) * scales[k % 2]
        rows = pl.ds(b * block, block)
        if h == 0:
            held[...] = o
        else:
            mixed_ref[rows, :] = jnp.where(first, held[...], o).astype(bf16)

    score(0)
    for k in range(len(jobs)):
        if k + 1 < len(jobs):
            score(k + 1)
        soften(k)
        mix(k)

def attn_fwd(lengths, projected, *, dim=64, block=256, strip=32):
    length, width3 = projected.shape
    width = width3 // 3
    docs = lengths.shape[1]
    pairs = width // 128
    col = lambda off: pl.BlockSpec((length, 128), lambda p: (0, p + off))
    return pl.pallas_call(
        functools.partial(attn_fwd_kernel, docs=docs, dim=dim, block=block, strip=strip),
        grid=(pairs,),
        in_specs=[pl.BlockSpec(memory_space=pltpu.SMEM), col(0), col(pairs), col(2 * pairs)],
        out_specs=[col(0), pl.BlockSpec((length, 128), lambda p: (0, 0))],
        out_shape=[jax.ShapeDtypeStruct((length, width), bf16), jax.ShapeDtypeStruct((length, 128), f32)],
        scratch_shapes=[pltpu.VMEM((length, 128), bf16), pltpu.VMEM((length, 128), bf16), pltpu.VMEM((length, 256), bf16),
                        pltpu.VMEM((block, length), f32), pltpu.VMEM((block, length), f32),
                        pltpu.VMEM((block, length), bf16), pltpu.VMEM((block, length), bf16),
                        pltpu.VMEM((2, block, 128), f32), pltpu.VMEM((block, 128), f32)],
        compiler_params=pltpu.CompilerParams(vmem_limit_bytes=LIMIT),
        cost_estimate=spend(12),
        name="attend",
    )(lengths, projected, projected, projected)

def attn_bwd_kernel(lengths_ref, q_ref, k_ref, v_ref, mixed_ref, gmix_ref, lse_ref, dq_ref, dk_ref, dv_ref,
                    aug_q, aug_k, kk, vv, qq, gg, kt, dqt, dk_acc, dv_acc, s_0, s_1, d_0, d_1, p_0, p_1, c_0, c_1,
                    *, docs, dim, block, first, strip):
    s_refs, d_refs, p_refs, c_refs = (s_0, s_1), (d_0, d_1), (p_0, p_1), (c_0, c_1)
    step = pl.program_id(0)
    pair = step + first
    length = q_ref.shape[0]
    blocks = length // block
    lane = lax.broadcasted_iota(jnp.int32, (1, 128), 1)

    @pl.when(step == 0)
    def _():
        hot = one_hot_docs(lengths_ref, docs, length)
        marks = lane < docs + 1
        aug_q[...] = jnp.where(hot & marks, 1.0, 0.0).astype(bf16)
        aug_k[...] = key_marks(hot, lane)

    kk[:, :128] = k_ref[...]
    kk[:, 128:] = aug_k[...]
    vv[:, :128] = v_ref[...]
    vv[:, 128:] = aug_k[...]
    kt[...] = jnp.transpose(k_ref[...])
    scale = 1.0 / math.sqrt(dim)
    low = lane < dim
    q2 = q_ref[...].astype(f32) * scale
    g2 = gmix_ref[...].astype(f32)
    dots = g2 * mixed_ref[...].astype(f32)
    lse_all = lse_ref[...]
    marks_q = aug_q[...].astype(f32)
    for h in range(2):
        mine = low if h == 0 else jnp.logical_not(low)
        lse = jnp.sum(jnp.where(lane == 2 * pair + h, lse_all, 0.0), axis=1, keepdims=True)
        qq[h, :, :128] = jnp.where(mine, q2, 0.0).astype(bf16)
        qq[h, :, 128:] = with_stat(marks_q, -lse, lane)
        delta = jnp.sum(jnp.where(mine, dots, 0.0), axis=1, keepdims=True)
        gg[h, :, :128] = jnp.where(mine, g2, 0.0).astype(bf16)
        gg[h, :, 128:] = with_stat(jnp.zeros_like(marks_q), -delta, lane)
    jobs = [(h, kb, qb) for kb in range(blocks) for h in range(2) for qb in range(kb, blocks)]

    def score(k):
        h, kb, qb = jobs[k]
        keys, queries = pl.ds(kb * block, block), pl.ds(qb * block, block)
        s_refs[k % 2][...] = lax.dot_general(kk[keys, :], qq[h, queries, :], NT, preferred_element_type=f32)
        d_refs[k % 2][...] = lax.dot_general(vv[keys, :], gg[h, queries, :], NT, preferred_element_type=f32)

    def bend(k):
        h, kb, qb = jobs[k]
        for r in range(0, block, strip):
            mine = pl.ds(r, strip)
            s = s_refs[k % 2][mine, :]
            if qb == kb:
                krow = lax.broadcasted_iota(jnp.int32, (strip, block), 0) + r
                qcol = lax.broadcasted_iota(jnp.int32, (strip, block), 1)
                s = jnp.where(qcol >= krow, s, NEG)
            p = jnp.exp(s)
            p_refs[k % 2][mine, :] = p.astype(bf16)
            c_refs[k % 2][mine, :] = (p * d_refs[k % 2][mine, :]).astype(bf16)

    def pull(k):
        h, kb, qb = jobs[k]
        keys, queries = pl.ds(kb * block, block), pl.ds(qb * block, block)
        p, ds = p_refs[k % 2][...], c_refs[k % 2][...]
        dv = lax.dot_general(p, gg[h, queries, :128], NN, preferred_element_type=f32)
        dk = lax.dot_general(ds, qq[h, queries, :128], NN, preferred_element_type=f32)
        dq = lax.dot_general(kt[h * dim:(h + 1) * dim, keys], ds, NN, preferred_element_type=f32)
        if h == 0 and qb == kb:
            dk_acc[keys, :] = dk
            dv_acc[keys, :] = dv
        else:
            dk_acc[keys, :] += dk
            dv_acc[keys, :] += dv
        if kb == 0:
            dqt[h * dim:(h + 1) * dim, queries] = dq
        else:
            dqt[h * dim:(h + 1) * dim, queries] += dq

    score(0)
    for k in range(len(jobs)):
        if k + 1 < len(jobs):
            score(k + 1)
        bend(k)
        pull(k)
    dk_ref[...] = dk_acc[...].astype(bf16)
    dv_ref[...] = dv_acc[...].astype(bf16)
    dq_ref[...] = (jnp.transpose(dqt[...]) * scale).astype(bf16)

def attn_bwd(lengths, projected, mixed, gmix, lse, *, first=0, count=4, dim=64, block=256, strip=32, us=25):
    length, width3 = projected.shape
    width = width3 // 3
    docs = lengths.shape[1]
    pairs = width // 128
    col = lambda off: pl.BlockSpec((length, 128), lambda p: (0, p + off))
    here = pl.BlockSpec((length, 128), lambda p: (0, p))
    one = jax.ShapeDtypeStruct((length, 128 * count), bf16)
    return pl.pallas_call(
        functools.partial(attn_bwd_kernel, docs=docs, dim=dim, block=block, first=first, strip=strip),
        grid=(count,),
        in_specs=[pl.BlockSpec(memory_space=pltpu.SMEM), col(first), col(first + pairs), col(first + 2 * pairs), col(first), col(first),
                  pl.BlockSpec((length, 128), lambda p: (0, 0))],
        out_specs=[here, here, here],
        out_shape=[one, one, one],
        scratch_shapes=[pltpu.VMEM((length, 128), bf16), pltpu.VMEM((length, 128), bf16),
                        pltpu.VMEM((length, 256), bf16), pltpu.VMEM((length, 256), bf16),
                        pltpu.VMEM((2, length, 256), bf16), pltpu.VMEM((2, length, 256), bf16),
                        pltpu.VMEM((128, length), bf16), pltpu.VMEM((128, length), f32),
                        pltpu.VMEM((length, 128), f32), pltpu.VMEM((length, 128), f32)]
        + [pltpu.VMEM((block, block), f32)] * 4 + [pltpu.VMEM((block, block), bf16)] * 4,
        compiler_params=pltpu.CompilerParams(vmem_limit_bytes=LIMIT),
        cost_estimate=spend(us),
        name="attend_back",
    )(lengths, projected, projected, projected, mixed, gmix, lse)


def place_tables(length, width):
    freq = np.exp(np.arange(width // 2, dtype=np.float64) * (-2.0 * math.log(10000.0) / width))
    angles = np.arange(length, dtype=np.float64)[:, None] * freq[None, :]
    return (np.concatenate([np.sin(angles), np.cos(angles)], axis=1).astype(np.float32),
            freq.astype(np.float32)[None, :])

def norm_stats(v):
    center = v - jnp.mean(v, axis=1, keepdims=True)
    inv = lax.rsqrt(jnp.mean(center * center, axis=1, keepdims=True) + 1e-5)
    return center * inv, inv

def front_kernel(lengths_ref, x_ref, table_ref, freq_ref, gain_ref, bias_ref, w_ref,
                 stream_ref, proj_ref, starts, turned, normed, *, docs):
    step = pl.program_id(0)
    rows, width = x_ref.shape
    half = width // 2
    begin, end, _ = doc_bounds(lengths_ref, docs)

    @pl.when(step == 0)
    def _():
        some = -(-(docs + 1) // 16) * 16
        at = jnp.transpose(jnp.broadcast_to(begin.astype(f32), (128, 128)))[:some, :1]
        angle = at * freq_ref[...]
        both = jnp.concatenate([jnp.sin(angle), jnp.cos(angle)], axis=1)
        hi = both.astype(bf16)
        mid = (both - hi.astype(f32)).astype(bf16)
        low = (both - hi.astype(f32) - mid.astype(f32)).astype(bf16)
        starts[...] = jnp.zeros_like(starts)
        for k, part in enumerate((hi, mid, low)):
            starts[k * 128:k * 128 + some, :] = part

    place = step * rows + lax.broadcasted_iota(jnp.int32, (rows, 128), 0)
    hot = jnp.where((place >= begin) & (place < end), 1.0, 0.0).astype(bf16)
    start = lax.dot_general(jnp.concatenate([hot, hot, hot], axis=1), starts[...], NN, preferred_element_type=f32)
    turned[...] = start
    for r in range(0, rows, 32):
        mine = pl.ds(r, 32)
        sin_b, cos_b = turned[mine, :half], turned[mine, half:]
        sin_t, cos_t = table_ref[mine, :half], table_ref[mine, half:]
        x = x_ref[mine, :].astype(f32)
        stream = jnp.concatenate([x[:, :half] + (sin_t * cos_b - cos_t * sin_b),
                                  x[:, half:] + (cos_t * cos_b + sin_t * sin_b)], axis=1)
        stream_ref[mine, :] = stream
        unit, _ = norm_stats(stream)
        normed[mine, :] = (unit * gain_ref[...] + bias_ref[...]).astype(bf16)
    proj_ref[...] = lax.dot_general(normed[...], w_ref[...], NN, preferred_element_type=f32).astype(bf16)

def front(lengths, x, gain, bias, w, *, rows=256):
    length, width = x.shape
    table, freq = place_tables(length, width)
    docs = lengths.shape[1]
    blk = pl.BlockSpec((rows, width), lambda i: (i, 0))
    whole = lambda a: pl.BlockSpec(a.shape, lambda i: (0,) * a.ndim)
    return pl.pallas_call(
        functools.partial(front_kernel, docs=docs),
        grid=(length // rows,),
        in_specs=[pl.BlockSpec(memory_space=pltpu.SMEM), blk, blk, whole(freq), whole(gain), whole(bias), whole(w)],
        out_specs=[blk, pl.BlockSpec((rows, w.shape[1]), lambda i: (i, 0))],
        out_shape=[jax.ShapeDtypeStruct((length, width), f32),
                   jax.ShapeDtypeStruct((length, w.shape[1]), bf16)],
        scratch_shapes=[pltpu.VMEM((384, width), bf16), pltpu.VMEM((rows, width), f32), pltpu.VMEM((rows, width), bf16)],
        compiler_params=pltpu.CompilerParams(vmem_limit_bytes=LIMIT),
        cost_estimate=spend(6),
        name="front",
    )(lengths, x, table, freq, gain, bias, w)

ERF = (0.254829592, -0.284496736, 1.421413741, -1.453152027, 1.061405429)
ERF_P = 0.3275911

def gelu_both(h):
    bell = jnp.exp(h * h * -0.5)
    t = 1.0 / (1.0 + jnp.abs(h) * (ERF_P / math.sqrt(2.0)))
    poly = t * (ERF[0] + t * (ERF[1] + t * (ERF[2] + t * (ERF[3] + t * ERF[4]))))
    tail = 0.5 * poly * bell
    phi = jnp.where(h < 0.0, tail, 1.0 - tail)
    return h * phi, phi + h * bell * (1.0 / math.sqrt(2.0 * math.pi))

def ffn_kernel(stream_ref, mixed_ref, w_out_ref, b_out_ref, gain_ref, bias_ref, w_up_ref, b_up_ref, w_down_ref, b_down_ref,
               after_ref, normed_ref, act_ref, slope_ref, out_ref, h_0, h_1, *, chunk):
    rows = stream_ref.shape[0]
    wide = w_up_ref.shape[1]
    after_ref[...] = lax.dot_general(mixed_ref[...], w_out_ref[...], NN, preferred_element_type=f32)
    for r in range(0, rows, 32):
        mine = pl.ds(r, 32)
        after = stream_ref[mine, :] + after_ref[mine, :] + b_out_ref[...]
        after_ref[mine, :] = after
        unit, _ = norm_stats(after)
        normed_ref[mine, :] = (unit * gain_ref[...] + bias_ref[...]).astype(bf16)
    hs = (h_0, h_1)

    def up(c):
        hs[c % 2][...] = lax.dot_general(normed_ref[...], w_up_ref[:, c * chunk:(c + 1) * chunk], NN, preferred_element_type=f32)

    def bend(c):
        for r in range(0, rows, 32):
            for k in range(0, chunk, 256):
                mine, cols = pl.ds(r, 32), pl.ds(c * chunk + k, 256)
                act, slope = gelu_both(hs[c % 2][mine, k:k + 256] + b_up_ref[:, cols])
                act_ref[mine, cols] = act.astype(bf16)
                slope_ref[mine, cols] = slope.astype(bf16)

    up(0)
    for c in range(wide // chunk):
        if c + 1 < wide // chunk:
            up(c + 1)
        bend(c)
    out = lax.dot_general(act_ref[...], w_down_ref[...], NN, preferred_element_type=f32)
    out_ref[...] = (out + after_ref[...] + b_down_ref[...]).astype(bf16)

def ffn(stream, mixed, w_out, b_out, gain, bias, w_up, b_up, w_down, b_down, *, rows=256, chunk=512):
    length, width = stream.shape
    wide = w_up.shape[1]
    blk = pl.BlockSpec((rows, width), lambda i: (i, 0))
    big = pl.BlockSpec((rows, wide), lambda i: (i, 0))
    whole = lambda a: pl.BlockSpec(a.shape, lambda i: (0,) * a.ndim)
    args = (w_out, b_out, gain, bias, w_up, b_up, w_down, b_down)
    return pl.pallas_call(
        functools.partial(ffn_kernel, chunk=chunk),
        grid=(length // rows,),
        in_specs=[blk, blk] + [whole(a) for a in args],
        out_specs=[blk, blk, big, big, blk],
        out_shape=[jax.ShapeDtypeStruct((length, width), f32), jax.ShapeDtypeStruct((length, width), bf16),
                   jax.ShapeDtypeStruct((length, wide), bf16), jax.ShapeDtypeStruct((length, wide), bf16),
                   jax.ShapeDtypeStruct((length, width), bf16)],
        scratch_shapes=[pltpu.VMEM((rows, chunk), f32), pltpu.VMEM((rows, chunk), f32)],
        compiler_params=pltpu.CompilerParams(vmem_limit_bytes=LIMIT),
        cost_estimate=spend(16),
        name="ffn",
    )(stream, mixed, *args)

def norm_back(g, gain, unit, inv):
    gu = g * gain
    return inv * (gu - jnp.mean(gu, axis=1, keepdims=True) - unit * jnp.mean(gu * unit, axis=1, keepdims=True))

def colsum(x):
    return jnp.sum(x, axis=0, keepdims=True)


def arrange(dst, t, me_ref, ab):
    row8 = t.shape[0] // 8
    for a in range(8):
        r = lax.bitwise_xor(jnp.int32(a), me_ref[0] * 4 + me_ref[1 + ab])
        dst[pl.ds(pl.multiple_of(r * row8, row8), row8), :] = t[a * row8:(a + 1) * row8, :]

def ffn_back_kernel(me_ref, g_ref, act_ref, slope_ref, w_down_ref, w_up_ref, normed_ref, after_ref, gain_ref, mixed_ref, w_out_ref,
                    bdown_ref, send_ref, keep_ref, gafter_ref, gmix_ref, g_low, g_t, norm_t, gh_ref, bup, small):
    i = pl.program_id(0)
    steps = pl.num_programs(0)
    width = g_ref.shape[1]
    tile = slope_ref.shape[1]
    wide = steps * tile
    half = width // 2

    @pl.when(i == 0)
    def _():
        low = g_ref[...].astype(bf16)
        g_low[...] = low
        arrange(g_t, jnp.transpose(low), me_ref, 0)
        arrange(norm_t, jnp.transpose(normed_ref[...]), me_ref, 1)

    def put(at, grad, size):
        cols = pl.ds(pl.multiple_of(at, 128), size)
        keep_ref[:, cols] = grad[:half, :]
        send_ref[:, cols] = grad[half:, :]

    gh = lax.dot_general(g_low[...], w_down_ref[...], NT, preferred_element_type=f32) * slope_ref[...].astype(f32)
    bup[pl.ds(i, 1), :] = colsum(gh)
    gh = gh.astype(bf16)
    gh_ref[:, pl.ds(pl.multiple_of(i * tile, tile), tile)] = gh
    put(i * tile, lax.dot_general(g_t[...], act_ref[...], NN, preferred_element_type=f32).astype(bf16), tile)
    put(i * tile + wide + width, lax.dot_general(norm_t[...], gh, NN, preferred_element_type=f32).astype(bf16), tile)

    @pl.when(i == steps - 1)
    def _():
        gafter_ref[...] = lax.dot_general(gh_ref[...], w_up_ref[...], NT, preferred_element_type=f32)
        fold = lambda x: x[0:8] + x[8:16] + x[16:24] + x[24:32]
        sums = [jnp.zeros((8, width), f32)] * 3
        for r in range(0, g_ref.shape[0], 32):
            mine = pl.ds(r, 32)
            unit, inv = norm_stats(after_ref[mine, :])
            gn = gafter_ref[mine, :]
            ga = g_ref[mine, :] + norm_back(gn, gain_ref[...], unit, inv)
            gafter_ref[mine, :] = ga
            g_low[mine, :] = ga.astype(bf16)
            sums = [s + fold(x) for s, x in zip(sums, (gn * unit, gn, ga))]
        gmix_ref[...] = lax.dot_general(g_low[...], w_out_ref[...], NT, preferred_element_type=f32).astype(bf16)
        arrange(g_t, jnp.transpose(mixed_ref[...]), me_ref, 0)
        put(wide, lax.dot_general(g_t[...], g_low[...], NN, preferred_element_type=f32).astype(bf16), width)
        small[...] = jnp.zeros_like(small)
        small[0:1, :] = bdown_ref[...]
        for k in range(3):
            small[1 + k:2 + k, :] = colsum(sums[k])
        per = width // tile if tile < width else 1
        for k in range(wide // width):
            if tile >= width:
                many = tile // width
                small[4 + k:5 + k, :] = bup[k // many:k // many + 1, (k % many) * width:(k % many + 1) * width]
            else:
                for m in range(per):
                    small[4 + k:5 + k, m * tile:(m + 1) * tile] = bup[k * per + m:k * per + m + 1, :]
        arrange(norm_t.at[:, :128], jnp.transpose(small[...]).astype(bf16), me_ref, 1)
        put(2 * wide + width, norm_t[:, :128], 128)

def ffn_back(me, g, act, slope, w_down, w_up, normed, after, gain, mixed, w_out, bdown, *, tile=512):
    length, width = g.shape
    wide = slope.shape[1]
    steps = wide // tile
    whole = lambda a: pl.BlockSpec(a.shape, lambda i, m: (0,) * a.ndim)
    full = lambda s: pl.BlockSpec(s, lambda i, m: (0,) * len(s))
    sums = (width // 2, 2 * wide + width + 128)
    return pl.pallas_call(
        ffn_back_kernel,
        grid_spec=pltpu.PrefetchScalarGridSpec(
            num_scalar_prefetch=1, grid=(steps,),
            in_specs=[whole(g), pl.BlockSpec((length, tile), lambda i, m: (0, i)), pl.BlockSpec((length, tile), lambda i, m: (0, i)),
                      pl.BlockSpec((tile, width), lambda i, m: (i, 0)),
                      whole(w_up), whole(normed), whole(after), whole(gain), whole(mixed), whole(w_out), whole(bdown)],
            out_specs=[full(sums), full(sums), full((length, width)), full((length, width))],
            scratch_shapes=[pltpu.VMEM((length, width), bf16), pltpu.VMEM((width, length), bf16), pltpu.VMEM((width, length), bf16),
                            pltpu.VMEM((length, wide), bf16), pltpu.VMEM((steps, tile), f32), pltpu.VMEM((128, width), f32)]),
        out_shape=[jax.ShapeDtypeStruct(sums, bf16)] * 2
        + [jax.ShapeDtypeStruct((length, width), f32), jax.ShapeDtypeStruct((length, width), bf16)],
        compiler_params=pltpu.CompilerParams(vmem_limit_bytes=LIMIT),
        cost_estimate=spend(20),
        name="ffn_back",
    )(me, g, act, slope, w_down, w_up, normed, after, gain, mixed, w_out, bdown)

def window(refs, start, size):
    found, at = [], 0
    for ref in refs:
        low, high = max(start, at), min(start + size, at + ref.shape[1])
        if low < high:
            found.append(ref[:, low - at:high - at])
        at += ref.shape[1]
    return found[0] if len(found) == 1 else jnp.concatenate(found, axis=1)

def qkv_grad_kernel(me_ref, *refs, parts):
    gps, (stream_ref, gain_ref, bias_ref, w_ref, send_ref, keep_ref, unit_t, rows_t, unit_ref) = refs[:parts], refs[parts:]
    length, width = stream_ref.shape
    half = width // 2
    for r in range(0, length, 32):
        unit, _ = norm_stats(stream_ref[pl.ds(r, 32), :])
        unit_ref[pl.ds(r, 32), :] = unit.astype(bf16)
    t = jnp.transpose(unit_ref[...])
    column_of = lambda row: jnp.transpose(jnp.broadcast_to(row, (128, width)))
    gain, bias = column_of(gain_ref[...]), column_of(bias_ref[...])
    for ab in range(2):
        arrange(unit_t.at[ab], t, me_ref, ab)
    gains, biases, ws = [], [], []
    for ab in range(2):
        arrange(rows_t, gain, me_ref, ab)
        gains.append(rows_t[:, :1])
        arrange(rows_t, bias, me_ref, ab)
        biases.append(rows_t[:, :1])
    total = 3 * width
    cut = total // 2
    gain_grad = [jnp.zeros((width, 1), f32), jnp.zeros((width, 1), f32)]
    bias_grad = [jnp.zeros((width, 1), f32), jnp.zeros((width, 1), f32)]
    for at in range(0, total, 256):
        ab = 0 if at < cut else 1
        gp = window(gps, at, 256)
        m = lax.dot_general(unit_t[ab], gp, NN, preferred_element_type=f32)
        s = colsum(gp.astype(f32))
        grad = (m * gains[ab] + biases[ab] * s).astype(bf16)
        keep_ref[:, at:at + 256] = grad[:half, :]
        send_ref[:, at:at + 256] = grad[half:, :]
        arrange_w = []
        row8 = width // 8
        for r in range(8):
            a = lax.bitwise_xor(jnp.int32(r), me_ref[0] * 4 + me_ref[1 + ab])
            arrange_w.append(w_ref[pl.ds(pl.multiple_of(a * row8, row8), row8), at:at + 256])
        w = jnp.concatenate(arrange_w, axis=0).astype(f32)
        gain_grad[ab] = gain_grad[ab] + jnp.sum(m * w, axis=1, keepdims=True)
        bias_grad[ab] = bias_grad[ab] + jnp.sum(w * s, axis=1, keepdims=True)
    row8 = width // 8
    lane = lax.broadcasted_iota(jnp.int32, (1, 128), 1)
    both = [jnp.where(lane == 0, gain_grad[ab], jnp.where(lane == 1, bias_grad[ab], 0.0)) for ab in range(2)]
    for r in range(8):
        to = lax.bitwise_xor(jnp.int32(r), lax.bitwise_xor(me_ref[1], me_ref[2]))
        rows_t[pl.ds(pl.multiple_of(to * row8, row8), row8), :] = both[0][r * row8:(r + 1) * row8, :]
    small = (rows_t[...] + both[1]).astype(bf16)
    keep_ref[:, total:] = small[:half, :]
    send_ref[:, total:] = small[half:, :]

def qkv_grad(me, gps, stream, gain, bias, w):
    length, width = stream.shape
    vm = pl.BlockSpec(memory_space=pltpu.VMEM)
    parts = len(gps)
    return pl.pallas_call(
        functools.partial(qkv_grad_kernel, parts=parts),
        in_specs=[pl.BlockSpec(memory_space=pltpu.SMEM)] + [vm] * (parts + 4),
        out_specs=[vm, vm],
        out_shape=[jax.ShapeDtypeStruct((width // 2, 3 * width + 128), bf16)] * 2,
        scratch_shapes=[pltpu.VMEM((2, width, length), bf16), pltpu.VMEM((width, 128), f32),
                        pltpu.VMEM((length, width), bf16)],
        compiler_params=pltpu.CompilerParams(vmem_limit_bytes=LIMIT),
        cost_estimate=spend(5),
        name="qkv_grad",
    )(me, *gps, stream, gain, bias, w)

def front_back_kernel(*refs, parts):
    gps, (w_ref, stream_ref, gafter_ref, gain_ref, out_ref, gn_ref) = refs[:parts], refs[parts:]
    gp = window(gps, 0, w_ref.shape[1])
    gn_ref[...] = lax.dot_general(gp, w_ref[...], NT, preferred_element_type=f32)
    for r in range(0, gn_ref.shape[0], 32):
        mine = pl.ds(r, 32)
        unit, inv = norm_stats(stream_ref[mine, :])
        out_ref[mine, :] = (gafter_ref[mine, :] + norm_back(gn_ref[mine, :], gain_ref[...], unit, inv)).astype(bf16)

def front_back(gps, w, stream, gafter, gain, *, rows=256):
    length, width = stream.shape
    blk = pl.BlockSpec((rows, width), lambda i: (i, 0))
    whole = lambda a: pl.BlockSpec(a.shape, lambda i: (0,) * a.ndim)
    return pl.pallas_call(
        functools.partial(front_back_kernel, parts=len(gps)),
        grid=(length // rows,),
        in_specs=[pl.BlockSpec((rows, gp.shape[1]), lambda i: (i, 0)) for gp in gps] + [whole(w), blk, blk, whole(gain)],
        out_specs=blk,
        out_shape=jax.ShapeDtypeStruct((length, width), bf16),
        scratch_shapes=[pltpu.VMEM((rows, width), f32)],
        compiler_params=pltpu.CompilerParams(vmem_limit_bytes=LIMIT),
        cost_estimate=spend(5),
        name="front_back",
    )(*gps, w, stream, gafter, gain)


def finish_kernel(me_ref, own_a, own_b, got_a, got_b, *refs, plan, n):
    outs, whole = refs[:-1], refs[-1]
    rows, cut = own_a.shape
    chunk = rows // (4 * n)

    def lay(dst, at, size):
        ab = 0 if at < cut else 1
        at -= ab * cut
        for near, ref in ((0, (own_a, own_b)[ab]), (1, (got_a, got_b)[ab])):
            core = lax.bitwise_xor(jnp.int32(near), me_ref[0])
            for pq in range(4):
                for z in range(n):
                    to = core * 4 + lax.bitwise_xor(jnp.int32(pq), me_ref[1 + ab])
                    to = to * n + lax.bitwise_xor(jnp.int32(z), me_ref[3])
                    r = (pq * n + z) * chunk
                    dst[pl.ds(pl.multiple_of(to * chunk, chunk), chunk), :] = ref[r:r + chunk, at:at + size].astype(f32)

    for at, size, out, col, turned in plan:
        if out < 0:
            lay(whole.at[:, :size], at, size)
            flat = jnp.transpose(whole[:, :size])
            done = 0
            for v in outs[out:]:
                width = flat.shape[1]
                for k in range(v.shape[1] // width):
                    v[:, k * width:(k + 1) * width] = flat[done:done + 1, :]
                    done += 1
        elif not turned:
            lay(outs[out].at[:, col:col + size], at, size)
        else:
            lay(whole.at[:, :size], at, size)
            flat = jnp.transpose(whole[:, :size])
            outs[out][col:col + size, :] = flat[:outs[out].shape[0] - col, :]

def finish(me, pieces, shapes, plan, *, n, us):
    rows = pieces[0].shape[0]
    vm = pl.BlockSpec(memory_space=pltpu.VMEM)
    return pl.pallas_call(
        functools.partial(finish_kernel, plan=plan, n=n),
        in_specs=[pl.BlockSpec(memory_space=pltpu.SMEM)] + [vm] * 4,
        out_specs=[vm] * len(shapes),
        out_shape=[jax.ShapeDtypeStruct(s, f32) for s in shapes],
        scratch_shapes=[pltpu.VMEM((2 * rows, 256), f32)],
        compiler_params=pltpu.CompilerParams(vmem_limit_bytes=LIMIT),
        cost_estimate=spend(us),
        name="finish",
    )(me, *pieces)

class Links:
    def __init__(self, mesh):
        self.sizes = dict(mesh.shape)
        self.n = self.sizes["rows"] // 2
        self.fine = self.n == 4
        self.zi = lax.axis_index("rows") // 2

    def swap(self, x, axis, bit):
        return lax.ppermute(x, axis, [(a, a ^ bit) for a in range(self.sizes[axis])])

    def core(self, x):
        return self.swap(x, "bank", 1)

    def near(self, x):
        return self.swap(x, "bank", 2)

    def side(self, x):
        return self.swap(x, "rows", 1)

def plus(*terms):
    out = terms[0].astype(f32)
    for t in terms[1:]:
        out = out + t.astype(f32)
    return out.astype(bf16)

def chain(links, send, keep, cut):
    n = links.n
    got, = yield [(links.core, send)]
    half = keep.shape[0] // 2
    sa, sb = plus(keep[half:, :cut], got[half:, :cut]), plus(keep[half:, cut:], got[half:, cut:])
    a, b = plus(keep[:half, :cut], got[:half, :cut]), plus(keep[:half, cut:], got[:half, cut:])
    ra, rb = yield [(links.near, sa), (links.side, sb)]
    half //= 2
    sa, sb = plus(a[half:], ra[half:]), plus(b[half:], rb[half:])
    a, b = plus(a[:half], ra[:half]), plus(b[:half], rb[:half])
    ra, rb = yield [(links.side, sa), (links.near, sb)]
    z = jnp.concatenate([plus(a, ra), plus(b, rb)], axis=1)
    chunk = half // n
    if links.fine:
        piece = lambda k: lax.dynamic_slice(z, ((links.zi ^ k) * chunk, 0), (chunk, z.shape[1]))
        hops = [functools.partial(links.swap, axis="rows", bit=2 * k) for k in range(1, n)]
        got = yield [(hop, piece(k + 1)) for k, hop in enumerate(hops)]
        mine = plus(piece(0), *got)
        got = yield [(hop, mine) for hop in hops]
        a = jnp.concatenate([v[:, :cut] for v in (mine, *got)], axis=0)
        b = jnp.concatenate([v[:, cut:] for v in (mine, *got)], axis=0)
    else:
        groups = [[r for r in range(2 * n) if r % 2 == y] for y in range(2)]
        z, = yield [(lambda v: lax.psum(v, "rows", axis_index_groups=groups), z)]
        yield []
        a, b = z[:, :cut], z[:, cut:]
    ra, rb = yield [(links.side, a), (links.near, b)]
    a, b = jnp.concatenate([a, ra], axis=0), jnp.concatenate([b, rb], axis=0)
    ra, rb = yield [(links.near, a), (links.side, b)]
    a, b = jnp.concatenate([a, ra], axis=0), jnp.concatenate([b, rb], axis=0)
    ga, gb = yield [(links.core, a), (links.core, b)]
    yield (a, b, ga, gb)

class Step:
    def __init__(self, *args):
        self.run = chain(*args)
        self.sends = next(self.run)

    def go(self):
        self.got = [how(what) for how, what in self.sends]

    def take(self):
        self.sends = self.run.send(self.got)

def tie(steps, *extra):
    flat = [what for s in steps for _, what in s.sends] + list(extra)
    flat = list(lax.optimization_barrier(tuple(flat)))
    for s in steps:
        s.sends = [(how, flat.pop(0)) for how, _ in s.sends]
    return flat

def tiles_of(start, width, out, turned):
    plan, at = [], 0
    while at < width:
        size = min(256, width - at)
        plan.append((start + at, size, out, at, turned))
        at += size
    return plan

def body(mesh, hidden_in, lengths, ln1_gain, ln1_bias, w_qkv, w_out, b_out, ln2_gain, ln2_bias, w_up, b_up, w_down, b_down,
         bank, bank_labels, target_slots, gold_ids):
    links = Links(mesh)
    row = lambda v: v.reshape(1, -1)
    width = hidden_in.shape[1]
    wide = w_up.shape[1]
    ib, ir = lax.axis_index("bank"), lax.axis_index("rows")
    core, x, y = ib % 2, ib // 2, ir % 2
    me = jnp.stack([core, x * 2 + y, y * 2 + x, links.zi if links.fine else 0, ib]).astype(jnp.int32)
    own = with_labels(bank, bank_labels)
    other = links.core(own)
    near = links.near(own)
    stream, projected = front(lengths, hidden_in, row(ln1_gain), row(ln1_bias), w_qkv)
    mixed, lse = attn_fwd(lengths, projected)
    after, normed_c, act, slope, block_out = ffn(stream, mixed, w_out, row(b_out), row(ln2_gain), row(ln2_bias), w_up, row(b_up),
                                                 w_down, row(b_down), chunk=256)
    e, hist, sums = bank_first(me, block_out, gold_ids, target_slots, own, other)
    near, e = lax.optimization_barrier((near, e))
    far = links.core(near)
    g, loss, bdown = bank_last(me, lengths, block_out, gold_ids, target_slots, e, hist, sums, own, other, near, far)
    send, keep, gafter, gmix = ffn_back(me, g, act, slope, w_down, w_up, normed_c, after, row(ln2_gain), mixed, w_out, bdown)
    cut = wide + width
    n = links.n if links.fine else 1
    one = Step(links, send, keep, cut)
    one.go()
    parts = []
    back = lambda first, count: parts.append(attn_bwd(lengths, projected, mixed, gmix, lse, first=first, count=count, us=6.5 * count))
    back(0, 1)
    one.take()
    gmix, = tie([one], gmix)
    one.go()
    back(1, 2)
    one.take()
    gmix, = tie([one], gmix, )
    one.go()
    back(3, 1)
    one.take()
    gps = [p[k] for k in range(3) for p in parts]
    gps[0], = tie([one], gps[0])
    one.go()
    send, keep = qkv_grad(me, gps, stream, row(ln1_gain), row(ln1_bias), w_qkv)
    cut2 = 3 * width // 2
    two = Step(links, send, keep, cut2)
    two.go()
    for slot in range(4):
        one.take()
        two.take()
        if slot == 0:
            gafter, = tie([one, two], gafter)
        elif slot == 1:
            input_grad, = tie([one, two], input_grad)
        else:
            tie([one, two])
        one.go()
        two.go()
        if slot == 0:
            input_grad = front_back(gps, w_qkv, stream, gafter, row(ln1_gain))
    one.take()
    two.take()
    two.go()
    vector = (1, width)
    two.take()
    pieces = tie([two], *one.sends)
    two.go()
    w_down_grad, w_out_grad, w_up_grad, *small = finish(
        me, pieces, [(wide, width), (width, width), (width, wide)] + [vector] * 4 + [(1, wide)],
        tiles_of(0, wide, 0, True) + tiles_of(wide, width, 1, False) + tiles_of(cut, wide, 2, False) + tiles_of(cut + wide, 128, -5, True),
        n=n, us=8)
    two.take()
    w_down_grad, = tie([two], w_down_grad)
    two.go()
    two.take()
    w_qkv_grad, *small1 = finish(me, two.sends, [(width, 3 * width), vector, vector],
                                 tiles_of(0, 3 * width, 0, False) + tiles_of(3 * width, 128, -2, True), n=n, us=4)
    flat = lambda v: v.reshape(-1)
    return (block_out, flat(loss), input_grad, flat(small1[0]), flat(small1[1]), w_qkv_grad, w_out_grad, flat(small[3]),
            flat(small[1]), flat(small[2]), w_up_grad, flat(small[4]), w_down_grad, flat(small[0]))

def solution(mesh):
    in_specs = (
        P(("rows", "bank"), None),
        P(("rows", "bank"), None),
        P(),
        P(),
        P(),
        P(),
        P(),
        P(),
        P(),
        P(),
        P(),
        P(),
        P(),
        P("bank", None),
        P("bank"),
        P(("rows", "bank")),
        P(("rows", "bank")),
    )
    out_specs = (
        P(("rows", "bank"), None),
        P(("rows", "bank")),
        P(("rows", "bank"), None),
        P(),
        P(),
        P(),
        P(),
        P(),
        P(),
        P(),
        P(),
        P(),
        P(),
        P(),
    )
    return jax.shard_map(functools.partial(body, mesh), mesh=mesh, in_specs=in_specs, out_specs=out_specs, check_vma=False)
```

```python
import functools
import math

import jax
import jax.numpy as jnp
import numpy as np
from jax import lax
from jax.experimental import pallas as pl
from jax.experimental.pallas import tpu as pltpu
from jax.sharding import PartitionSpec as P

LOG2E = 1.4426950408889634
LN2 = 0.6931471805599453
NT = (((1,), (1,)), ((), ()))
NN = (((1,), (0,)), ((), ()))
f32, bf16 = jnp.float32, jnp.bfloat16

LIMIT = 60 * 2 ** 20

def spend(us):
    return pl.CostEstimate(flops=int(us * 1.0e9), bytes_accessed=0, transcendentals=0)

def column(row, rows):
    return jnp.transpose(jnp.broadcast_to(row.astype(f32), (128, rows)))[:, :1]

class Slots:
    def __init__(self, bank_ref, marks_ref, gold_ref, target_ref, rows, tile, strip):
        self.bank_ref, self.marks_ref, self.gold_ref, self.target_ref = bank_ref, marks_ref, gold_ref, target_ref
        self.rows, self.tile, self.strip = rows, tile, strip
        self.width = bank_ref.shape[1]
        self.c = LOG2E / math.sqrt(self.width)

    def wide(self, col):
        return jnp.concatenate([col] * (self.tile // 128), axis=1)

    def keys(self, j):
        return self.bank_ref[pl.ds(pl.multiple_of(j * self.tile, self.tile), self.tile), :]

    def positive(self, j, at):
        tall = lambda v: jnp.concatenate([v] * (self.strip // 8), axis=0)
        mine = pl.ds(at, self.strip)
        return (tall(self.marks_ref[0, j]) == self.wide(self.gold_ref[mine, :])) | (
            tall(self.marks_ref[1, j]) == self.wide(self.target_ref[mine, :]))

    def fold(self, x, op):
        out = x[:, :128]
        for i in range(1, self.tile // 128):
            out = op(out, x[:, i * 128:(i + 1) * 128])
        return out

    def scores(self, q, j):
        return lax.dot_general(q, self.keys(j), NT, preferred_element_type=f32)

    def eat(self, j, s_ref, e_ref, at, top_ref, all_ref, pos_ref, hist_ref):
        for r in range(0, self.rows, self.strip):
            mine = pl.ds(r, self.strip)
            s = s_ref[mine, :]
            top = top_ref[mine, :]
            new_top = jnp.maximum(top, jnp.max(self.fold(s, jnp.maximum), axis=1, keepdims=True) * self.c)
            shrink = jnp.exp2(top - new_top)
            e = jnp.exp2(s * self.c - self.wide(new_top))
            e_ref[at, mine, :] = e
            all_ref[mine, :] = all_ref[mine, :] * shrink + self.fold(e, jnp.add)
            pos_ref[mine, :] = pos_ref[mine, :] * shrink + self.fold(jnp.where(self.positive(j, r), e, 0.0), jnp.add)
            top_ref[mine, :] = new_top
            hist_ref[at, mine, :] = new_top

    def eat_all(self, q, first, count, s0_ref, s1_ref, e_ref, top_ref, all_ref, pos_ref, hist_ref):
        bufs = (s0_ref, s1_ref)
        bufs[0][...] = self.scores(q, first)
        for k in range(count):
            if k + 1 < count:
                bufs[(k + 1) % 2][...] = self.scores(q, first + k + 1)
            self.eat(first + k, bufs[k % 2], e_ref, k, top_ref, all_ref, pos_ref, hist_ref)

def fetch(shards, bank_ref, label_ref, sems):
    size = bank_ref.shape[0] // len(shards)
    copies = []
    for k, ref in enumerate(shards):
        copies.append((pltpu.make_async_copy(ref.at[pl.ds(0, size)], bank_ref.at[pl.ds(k * size, size)], sems.at[2 * k]),
                       pltpu.make_async_copy(ref.at[pl.ds(size, 16)], label_ref.at[k], sems.at[2 * k + 1])))
    return copies

def write_marks(label_ref, marks_ref, shard):
    tiles, _, tile = marks_ref.shape[1:]
    width = label_ref.shape[2]
    for j in range(tiles):
        owner, at = j * tile // shard, j * tile % shard // width
        for k in range(tile // width):
            marks_ref[0, j, :, k * width:(k + 1) * width] = jnp.broadcast_to(label_ref[owner, at + k:at + k + 1, :].astype(f32), (8, width))
        marks_ref[1, j] = (lax.broadcasted_iota(jnp.int32, (8, tile), 1) + j * tile).astype(f32)

def write_wanted(me_ref, gold_ref, target_ref, gold_b, target_b, shard, rows):
    turn = lambda row: jnp.transpose(jnp.broadcast_to(row.astype(f32), (128, rows)))
    gold_b[...] = turn(gold_ref[...])
    target_b[...] = turn(lax.bitwise_xor(target_ref[...], me_ref[4] * shard))

def bank_first_kernel(me_ref, q_ref, gold_ref, target_ref, own_hbm, core_hbm, e_ref, hist_ref, sums_ref,
                      bank_ref, label_ref, marks_ref, gold_b, target_b, top_ref, all_ref, pos_ref, s0_ref, s1_ref, sems,
                      *, rows, tile, strip):
    step = pl.program_id(0)
    tiles = bank_ref.shape[0] // tile
    shard = bank_ref.shape[0] // 2
    copies = fetch((own_hbm, core_hbm), bank_ref, label_ref, sems)

    @pl.when(step == 0)
    def _():
        for pair in copies:
            for copy in pair:
                copy.start()
        for pair in copies:
            for copy in pair:
                copy.wait()
        write_marks(label_ref, marks_ref, shard)
    write_wanted(me_ref, gold_ref, target_ref, gold_b, target_b, shard, rows)
    know = Slots(bank_ref, marks_ref, gold_b, target_b, rows, tile, strip)
    top_ref[...] = jnp.full((rows, 128), -3e38, f32)
    all_ref[...] = jnp.zeros((rows, 128), f32)
    pos_ref[...] = jnp.zeros((rows, 128), f32)
    know.eat_all(q_ref[...], 0, tiles, s0_ref, s1_ref, e_ref, top_ref, all_ref, pos_ref, hist_ref)
    sums_ref[0] = all_ref[...]
    sums_ref[1] = pos_ref[...]

def bank_last_kernel(me_ref, lengths_ref, q_ref, gold_ref, target_ref, e_ref, hist_ref, sums_ref, own_hbm, core_hbm, near_hbm, far_hbm,
                     grad_ref, loss_ref, bsum_ref,
                     bank_ref, label_ref, marks_ref, gold_b, target_b, top_ref, all_ref, pos_ref, on_ref, off_ref, g_ref, g2_ref,
                     s0_ref, s1_ref, e2_ref, hist2_ref, sems, *, rows, tile, docs, strip):
    step = pl.program_id(0)
    width = q_ref.shape[1]
    tiles = bank_ref.shape[0] // tile
    half = tiles // 2
    shard = bank_ref.shape[0] // 4
    copies = fetch((own_hbm, core_hbm, near_hbm, far_hbm), bank_ref, label_ref, sems)

    @pl.when(step == 0)
    def _():
        for pair in copies[2:] + copies[:2]:
            for copy in pair:
                copy.start()
        for pair in copies:
            pair[1].wait()
        for pair in copies[2:]:
            pair[0].wait()
        write_marks(label_ref, marks_ref, shard)
    write_wanted(me_ref, gold_ref, target_ref, gold_b, target_b, shard, rows)
    know = Slots(bank_ref, marks_ref, gold_b, target_b, rows, tile, strip)
    q = q_ref[...]
    total = lengths_ref[0, 0]
    for j in range(1, docs):
        total = total + lengths_ref[0, j]
    live = step * rows + lax.broadcasted_iota(jnp.int32, (rows, 128), 0) < total
    top_ref[...] = hist_ref[half - 1]
    all_ref[...] = sums_ref[0]
    pos_ref[...] = sums_ref[1]
    know.eat_all(q, half, half, s0_ref, s1_ref, e2_ref, top_ref, all_ref, pos_ref, hist2_ref)
    broad = lambda col: jnp.broadcast_to(col, (rows, 128))
    top = top_ref[...]
    sum_all = broad(jnp.sum(all_ref[...], axis=1, keepdims=True))
    sum_pos = broad(jnp.sum(pos_ref[...], axis=1, keepdims=True))
    inv_all = jnp.where(live, 1.0 / sum_all, 0.0)
    off_ref[...] = inv_all
    on_ref[...] = inv_all - jnp.where(live, 1.0 / sum_pos, 0.0)

    def show(loss):
        loss_ref[...] = jnp.transpose(jnp.where(live, loss, 0.0))[:1, :]
    show((jnp.log2(sum_all) - jnp.log2(sum_pos)) * LN2)

    safe = jnp.min(sum_pos) >= 2.0 ** -60

    def pull(source, hists, j, at, g_ref):
        for r in range(0, rows, strip):
            mine = pl.ds(r, strip)
            factor = jnp.exp2(hists[at, mine, :] - top_ref[mine, :])
            weight = jnp.where(know.positive(j, r), know.wide(factor * on_ref[mine, :]), know.wide(factor * off_ref[mine, :]))
            g_ref[mine, :] = (source[at, mine, :] * weight).astype(bf16)
        return lax.dot_general(g_ref[...], know.keys(j), NN, preferred_element_type=f32)

    @pl.when(step == 0)
    def _():
        for pair in copies[:2]:
            pair[0].wait()

    @pl.when(safe)
    def _():
        acc = None
        for j in range(tiles):
            near = j >= half
            term = pull(e2_ref if near else e_ref, hist2_ref if near else hist_ref, j, j - half if near else j, (g_ref, g2_ref)[j % 2])
            acc = term if acc is None else acc + term
        grad_ref[...] = acc

    @pl.when(jnp.logical_not(safe))
    def _():
        grad_ref[...] = jnp.zeros_like(grad_ref)
        all_ref[...] = jnp.where(live, top + jnp.log2(sum_all), 1e30)
        top_ref[...] = jnp.full((rows, 128), -1e30, f32)
        pos_ref[...] = jnp.zeros((rows, 128), f32)

        def own_top(j, _):
            s0_ref[...] = know.scores(q, j)
            for r in range(0, rows, strip):
                mine = pl.ds(r, strip)
                x = jnp.where(know.positive(j, r), s0_ref[mine, :] * know.c, -1e30)
                top_ref[mine, :] = jnp.maximum(top_ref[mine, :], know.fold(x, jnp.maximum))
            return 0
        lax.fori_loop(0, tiles, own_top, 0)
        top_ref[...] = broad(jnp.max(top_ref[...], axis=1, keepdims=True))

        def own_sum(j, _):
            s0_ref[...] = know.scores(q, j)
            for r in range(0, rows, strip):
                mine = pl.ds(r, strip)
                x = jnp.where(know.positive(j, r), s0_ref[mine, :] * know.c, -1e30)
                pos_ref[mine, :] += know.fold(jnp.exp2(x - know.wide(top_ref[mine, :])), jnp.add)
            return 0
        lax.fori_loop(0, tiles, own_sum, 0)
        lse_pos = top_ref[...] + jnp.log2(broad(jnp.sum(pos_ref[...], axis=1, keepdims=True)))
        show((top + jnp.log2(sum_all) - lse_pos) * LN2)
        pos_ref[...] = jnp.where(live, lse_pos, 1e30)

        def draw(j, _):
            s0_ref[...] = know.scores(q, j)
            for r in range(0, rows, strip):
                mine = pl.ds(r, strip)
                s = s0_ref[mine, :] * know.c
                x = jnp.where(know.positive(j, r), s, -1e30)
                g = jnp.exp2(s - know.wide(all_ref[mine, :])) - jnp.exp2(x - know.wide(pos_ref[mine, :]))
                g_ref[mine, :] = g.astype(bf16)
            grad_ref[...] += lax.dot_general(g_ref[...], know.keys(j), NN, preferred_element_type=f32)
            return 0
        lax.fori_loop(0, tiles, draw, 0)
    grad_ref[...] = grad_ref[...] * (1.0 / math.sqrt(width))
    part = jnp.sum(grad_ref[...], axis=0, keepdims=True)
    bsum_ref[...] = jnp.where(step == 0, part, bsum_ref[...] + part)

def with_labels(bank, labels):
    width = bank.shape[1]
    rows = labels.astype(bf16).reshape(-1, width)
    return jnp.concatenate([bank, jnp.pad(rows, ((0, 16 - rows.shape[0]), (0, 0)))], axis=0)

def bank_specs(rows, width):
    smem, hbm = pl.BlockSpec(memory_space=pltpu.SMEM), pl.BlockSpec(memory_space=pl.ANY)
    blk = pl.BlockSpec((rows, width), lambda i: (i, 0))
    line = pl.BlockSpec((1, rows), lambda i: (0, i))
    return smem, hbm, blk, line

def bank_first(me, q, gold, target, own, core, *, rows=256, tile=1024, strip=32):
    length, width = q.shape
    tiles = 2 * (own.shape[0] - 16) // tile
    smem, hbm, blk, line = bank_specs(rows, width)
    part = pltpu.VMEM((rows, 128), f32)
    return pl.pallas_call(
        functools.partial(bank_first_kernel, rows=rows, tile=tile, strip=strip),
        grid=(length // rows,),
        in_specs=[smem, blk, line, line, hbm, hbm],
        out_specs=[pl.BlockSpec((tiles, rows, tile), lambda i: (0, i, 0)), pl.BlockSpec((tiles, rows, 128), lambda i: (0, i, 0)),
                   pl.BlockSpec((2, rows, 128), lambda i: (0, i, 0))],
        out_shape=[jax.ShapeDtypeStruct((tiles, length, tile), f32), jax.ShapeDtypeStruct((tiles, length, 128), f32),
                   jax.ShapeDtypeStruct((2, length, 128), f32)],
        scratch_shapes=[pltpu.VMEM((tiles * tile, width), bf16), pltpu.VMEM((2, 16, width), bf16), pltpu.VMEM((2, tiles, 8, tile), f32),
                        part, part, part, part, part,
                        pltpu.VMEM((rows, tile), f32), pltpu.VMEM((rows, tile), f32), pltpu.SemaphoreType.DMA((4,))],
        compiler_params=pltpu.CompilerParams(vmem_limit_bytes=LIMIT),
        cost_estimate=spend(13),
        name="bank_first",
    )(me, q, gold.reshape(1, length), target.reshape(1, length), own, core)

def bank_last(me, lengths, q, gold, target, e, hist, sums, own, core, near, far, *, rows=256, tile=1024, strip=32):
    length, width = q.shape
    half = e.shape[0]
    docs = lengths.shape[1]
    smem, hbm, blk, line = bank_specs(rows, width)
    part = pltpu.VMEM((rows, 128), f32)
    return pl.pallas_call(
        functools.partial(bank_last_kernel, rows=rows, tile=tile, docs=docs, strip=strip),
        grid=(length // rows,),
        in_specs=[smem, smem, blk, line, line, pl.BlockSpec((half, rows, tile), lambda i: (0, i, 0)),
                  pl.BlockSpec((half, rows, 128), lambda i: (0, i, 0)), pl.BlockSpec((2, rows, 128), lambda i: (0, i, 0)),
                  hbm, hbm, hbm, hbm],
        out_specs=[blk, line, pl.BlockSpec((1, width), lambda i: (0, 0))],
        out_shape=[jax.ShapeDtypeStruct((length, width), f32), jax.ShapeDtypeStruct((1, length), f32),
                   jax.ShapeDtypeStruct((1, width), f32)],
        scratch_shapes=[pltpu.VMEM((2 * half * tile, width), bf16), pltpu.VMEM((4, 16, width), bf16),
                        pltpu.VMEM((2, 2 * half, 8, tile), f32),
                        part, part, part, part, part, part, part, pltpu.VMEM((rows, tile), bf16), pltpu.VMEM((rows, tile), bf16),
                        pltpu.VMEM((rows, tile), f32), pltpu.VMEM((rows, tile), f32), pltpu.VMEM((half, rows, tile), f32),
                        pltpu.VMEM((half, rows, 128), f32), pltpu.SemaphoreType.DMA((8,))],
        compiler_params=pltpu.CompilerParams(vmem_limit_bytes=LIMIT),
        cost_estimate=spend(25),
        name="bank_last",
    )(me, lengths, q, gold.reshape(1, length), target.reshape(1, length), e, hist, sums, own, core, near, far)

TN = (((0,), (0,)), ((), ()))
BIG = 1e30
STAT = 120
NEG = -1e30

def doc_bounds(lengths_ref, docs):
    lane = lax.broadcasted_iota(jnp.int32, (1, 128), 1)
    begin = jnp.zeros((1, 128), jnp.int32)
    end = jnp.zeros((1, 128), jnp.int32)
    at = jnp.int32(0)
    for j in range(docs):
        begin = jnp.where(lane == j, at, begin)
        at = at + lengths_ref[0, j]
        end = jnp.where(lane == j, at, end)
    begin = jnp.where(lane == docs, at, begin)
    end = jnp.where(lane == docs, 2 ** 30, end)
    return begin, end, at

def one_hot_docs(lengths_ref, docs, length):
    begin, end, _ = doc_bounds(lengths_ref, docs)
    place = lax.broadcasted_iota(jnp.int32, (length, 128), 0)
    return (place >= begin) & (place < end)

def split3(col):
    hi = col.astype(bf16).astype(f32)
    mid = (col - hi).astype(bf16).astype(f32)
    lo = col - hi - mid
    return hi, mid, lo

def with_stat(base, col, lane):
    hi, mid, lo = split3(col)
    return jnp.where(lane == STAT, hi, jnp.where(lane == STAT + 1, mid, jnp.where(lane == STAT + 2, lo, base))).astype(bf16)

def key_marks(hot, lane):
    ones = (lane >= STAT) & (lane < STAT + 3)
    return jnp.where(ones, 1.0, jnp.where(hot, 0.0, -BIG)).astype(bf16)

def attn_fwd_kernel(lengths_ref, q_ref, k_ref, v_ref, mixed_ref, lse_ref, aug_q, aug_k, kk, s_0, s_1, e_0, e_1, scales, held,
                    *, docs, dim, block, strip):
    s_refs, e_refs = (s_0, s_1), (e_0, e_1)
    pair = pl.program_id(0)
    length = q_ref.shape[0]
    lane = lax.broadcasted_iota(jnp.int32, (1, 128), 1)

    @pl.when(pair == 0)
    def _():
        hot = one_hot_docs(lengths_ref, docs, length)
        marks = lane < docs + 1
        aug_q[...] = jnp.where(hot & marks, 1.0, 0.0).astype(bf16)
        aug_k[...] = key_marks(hot, lane)
        lse_ref[...] = jnp.zeros_like(lse_ref)

    kk[:, :128] = k_ref[...]
    kk[:, 128:] = aug_k[...]
    scale = 1.0 / math.sqrt(dim)
    first = lane < dim
    jobs = [(b, h) for b in range(length // block) for h in range(2)]

    def score(k):
        b, h = jobs[k]
        rows = pl.ds(b * block, block)
        mine = first if h == 0 else jnp.logical_not(first)
        qq = jnp.concatenate([jnp.where(mine, q_ref[rows, :].astype(f32) * scale, 0.0).astype(bf16), aug_q[rows, :]], axis=1)
        s_refs[k % 2][:, :(b + 1) * block] = lax.dot_general(qq, kk[:(b + 1) * block, :], NT, preferred_element_type=f32)

    def soften(k):
        b, h = jobs[k]
        s_ref, e_ref, many = s_refs[k % 2], e_refs[k % 2], (b + 1) * block
        for r in range(0, block, strip):
            mine = pl.ds(r, strip)
            row = lax.broadcasted_iota(jnp.int32, (strip, block), 0) + r
            col = lax.broadcasted_iota(jnp.int32, (strip, block), 1)
            s = jnp.where(row >= col, s_ref[mine, b * block:many], NEG)
            if b > 0:
                s = jnp.concatenate([s_ref[mine, :b * block], s], axis=1)
            top = jnp.max(s, axis=1, keepdims=True)
            e = jnp.exp(s - top)
            total = jnp.sum(e, axis=1, keepdims=True)
            e_ref[mine, :many] = e.astype(bf16)
            scales[k % 2, mine, :] = jnp.broadcast_to(1.0 / total, (strip, 128))
            at = pl.ds(b * block + r, strip)
            lse_ref[at, :] = jnp.where(lane == 2 * pair + h, top + jnp.log(total), lse_ref[at, :])

    def mix(k):
        b, h = jobs[k]
        many = (b + 1) * block
        o = lax.dot_general(e_refs[k % 2][:, :many], v_ref[:many, :], NN, preferred_element_type=f32) * scales[k % 2]
        rows = pl.ds(b * block, block)
        if h == 0:
            held[...] = o
        else:
            mixed_ref[rows, :] = jnp.where(first, held[...], o).astype(bf16)

    score(0)
    for k in range(len(jobs)):
        if k + 1 < len(jobs):
            score(k + 1)
        soften(k)
        mix(k)

def attn_fwd(lengths, projected, *, dim=64, block=256, strip=32):
    length, width3 = projected.shape
    width = width3 // 3
    docs = lengths.shape[1]
    pairs = width // 128
    col = lambda off: pl.BlockSpec((length, 128), lambda p: (0, p + off))
    return pl.pallas_call(
        functools.partial(attn_fwd_kernel, docs=docs, dim=dim, block=block, strip=strip),
        grid=(pairs,),
        in_specs=[pl.BlockSpec(memory_space=pltpu.SMEM), col(0), col(pairs), col(2 * pairs)],
        out_specs=[col(0), pl.BlockSpec((length, 128), lambda p: (0, 0))],
        out_shape=[jax.ShapeDtypeStruct((length, width), bf16), jax.ShapeDtypeStruct((length, 128), f32)],
        scratch_shapes=[pltpu.VMEM((length, 128), bf16), pltpu.VMEM((length, 128), bf16), pltpu.VMEM((length, 256), bf16),
                        pltpu.VMEM((block, length), f32), pltpu.VMEM((block, length), f32),
                        pltpu.VMEM((block, length), bf16), pltpu.VMEM((block, length), bf16),
                        pltpu.VMEM((2, block, 128), f32), pltpu.VMEM((block, 128), f32)],
        compiler_params=pltpu.CompilerParams(vmem_limit_bytes=LIMIT),
        cost_estimate=spend(12),
        name="attend",
    )(lengths, projected, projected, projected)

def attn_bwd_kernel(lengths_ref, q_ref, k_ref, v_ref, mixed_ref, gmix_ref, lse_ref, dq_ref, dk_ref, dv_ref,
                    aug_q, aug_k, kk, vv, qq, gg, kt, dqt, dk_acc, dv_acc, s_0, s_1, d_0, d_1, p_0, p_1, c_0, c_1,
                    *, docs, dim, block, first, strip):
    s_refs, d_refs, p_refs, c_refs = (s_0, s_1), (d_0, d_1), (p_0, p_1), (c_0, c_1)
    step = pl.program_id(0)
    pair = step + first
    length = q_ref.shape[0]
    blocks = length // block
    lane = lax.broadcasted_iota(jnp.int32, (1, 128), 1)

    @pl.when(step == 0)
    def _():
        hot = one_hot_docs(lengths_ref, docs, length)
        marks = lane < docs + 1
        aug_q[...] = jnp.where(hot & marks, 1.0, 0.0).astype(bf16)
        aug_k[...] = key_marks(hot, lane)

    kk[:, :128] = k_ref[...]
    kk[:, 128:] = aug_k[...]
    vv[:, :128] = v_ref[...]
    vv[:, 128:] = aug_k[...]
    kt[...] = jnp.transpose(k_ref[...])
    scale = 1.0 / math.sqrt(dim)
    low = lane < dim
    q2 = q_ref[...].astype(f32) * scale
    g2 = gmix_ref[...].astype(f32)
    dots = g2 * mixed_ref[...].astype(f32)
    lse_all = lse_ref[...]
    marks_q = aug_q[...].astype(f32)
    for h in range(2):
        mine = low if h == 0 else jnp.logical_not(low)
        lse = jnp.sum(jnp.where(lane == 2 * pair + h, lse_all, 0.0), axis=1, keepdims=True)
        qq[h, :, :128] = jnp.where(mine, q2, 0.0).astype(bf16)
        qq[h, :, 128:] = with_stat(marks_q, -lse, lane)
        delta = jnp.sum(jnp.where(mine, dots, 0.0), axis=1, keepdims=True)
        gg[h, :, :128] = jnp.where(mine, g2, 0.0).astype(bf16)
        gg[h, :, 128:] = with_stat(jnp.zeros_like(marks_q), -delta, lane)
    jobs = [(h, kb, qb) for kb in range(blocks) for h in range(2) for qb in range(kb, blocks)]

    def score(k):
        h, kb, qb = jobs[k]
        keys, queries = pl.ds(kb * block, block), pl.ds(qb * block, block)
        s_refs[k % 2][...] = lax.dot_general(kk[keys, :], qq[h, queries, :], NT, preferred_element_type=f32)
        d_refs[k % 2][...] = lax.dot_general(vv[keys, :], gg[h, queries, :], NT, preferred_element_type=f32)

    def bend(k):
        h, kb, qb = jobs[k]
        for r in range(0, block, strip):
            mine = pl.ds(r, strip)
            s = s_refs[k % 2][mine, :]
            if qb == kb:
                krow = lax.broadcasted_iota(jnp.int32, (strip, block), 0) + r
                qcol = lax.broadcasted_iota(jnp.int32, (strip, block), 1)
                s = jnp.where(qcol >= krow, s, NEG)
            p = jnp.exp(s)
            p_refs[k % 2][mine, :] = p.astype(bf16)
            c_refs[k % 2][mine, :] = (p * d_refs[k % 2][mine, :]).astype(bf16)

    def pull(k):
        h, kb, qb = jobs[k]
        keys, queries = pl.ds(kb * block, block), pl.ds(qb * block, block)
        p, ds = p_refs[k % 2][...], c_refs[k % 2][...]
        dv = lax.dot_general(p, gg[h, queries, :128], NN, preferred_element_type=f32)
        dk = lax.dot_general(ds, qq[h, queries, :128], NN, preferred_element_type=f32)
        dq = lax.dot_general(kt[h * dim:(h + 1) * dim, keys], ds, NN, preferred_element_type=f32)
        if h == 0 and qb == kb:
            dk_acc[keys, :] = dk
            dv_acc[keys, :] = dv
        else:
            dk_acc[keys, :] += dk
            dv_acc[keys, :] += dv
        if kb == 0:
            dqt[h * dim:(h + 1) * dim, queries] = dq
        else:
            dqt[h * dim:(h + 1) * dim, queries] += dq

    score(0)
    for k in range(len(jobs)):
        if k + 1 < len(jobs):
            score(k + 1)
        bend(k)
        pull(k)
    dk_ref[...] = dk_acc[...].astype(bf16)
    dv_ref[...] = dv_acc[...].astype(bf16)
    dq_ref[...] = (jnp.transpose(dqt[...]) * scale).astype(bf16)

def attn_bwd(lengths, projected, mixed, gmix, lse, *, first=0, count=4, dim=64, block=256, strip=32, us=25):
    length, width3 = projected.shape
    width = width3 // 3
    docs = lengths.shape[1]
    pairs = width // 128
    col = lambda off: pl.BlockSpec((length, 128), lambda p: (0, p + off))
    here = pl.BlockSpec((length, 128), lambda p: (0, p))
    one = jax.ShapeDtypeStruct((length, 128 * count), bf16)
    return pl.pallas_call(
        functools.partial(attn_bwd_kernel, docs=docs, dim=dim, block=block, first=first, strip=strip),
        grid=(count,),
        in_specs=[pl.BlockSpec(memory_space=pltpu.SMEM), col(first), col(first + pairs), col(first + 2 * pairs), col(first), col(first),
                  pl.BlockSpec((length, 128), lambda p: (0, 0))],
        out_specs=[here, here, here],
        out_shape=[one, one, one],
        scratch_shapes=[pltpu.VMEM((length, 128), bf16), pltpu.VMEM((length, 128), bf16),
                        pltpu.VMEM((length, 256), bf16), pltpu.VMEM((length, 256), bf16),
                        pltpu.VMEM((2, length, 256), bf16), pltpu.VMEM((2, length, 256), bf16),
                        pltpu.VMEM((128, length), bf16), pltpu.VMEM((128, length), f32),
                        pltpu.VMEM((length, 128), f32), pltpu.VMEM((length, 128), f32)]
        + [pltpu.VMEM((block, block), f32)] * 4 + [pltpu.VMEM((block, block), bf16)] * 4,
        compiler_params=pltpu.CompilerParams(vmem_limit_bytes=LIMIT),
        cost_estimate=spend(us),
        name="attend_back",
    )(lengths, projected, projected, projected, mixed, gmix, lse)


def place_tables(length, width):
    freq = np.exp(np.arange(width // 2, dtype=np.float64) * (-2.0 * math.log(10000.0) / width))
    angles = np.arange(length, dtype=np.float64)[:, None] * freq[None, :]
    return (np.concatenate([np.sin(angles), np.cos(angles)], axis=1).astype(np.float32),
            freq.astype(np.float32)[None, :])

def norm_stats(v):
    center = v - jnp.mean(v, axis=1, keepdims=True)
    inv = lax.rsqrt(jnp.mean(center * center, axis=1, keepdims=True) + 1e-5)
    return center * inv, inv

def front_kernel(lengths_ref, x_ref, table_ref, freq_ref, gain_ref, bias_ref, w_ref,
                 stream_ref, proj_ref, starts, turned, normed, *, docs):
    step = pl.program_id(0)
    rows, width = x_ref.shape
    half = width // 2
    begin, end, _ = doc_bounds(lengths_ref, docs)

    @pl.when(step == 0)
    def _():
        some = -(-(docs + 1) // 16) * 16
        at = jnp.transpose(jnp.broadcast_to(begin.astype(f32), (128, 128)))[:some, :1]
        angle = at * freq_ref[...]
        both = jnp.concatenate([jnp.sin(angle), jnp.cos(angle)], axis=1)
        hi = both.astype(bf16)
        mid = (both - hi.astype(f32)).astype(bf16)
        low = (both - hi.astype(f32) - mid.astype(f32)).astype(bf16)
        starts[...] = jnp.zeros_like(starts)
        for k, part in enumerate((hi, mid, low)):
            starts[k * 128:k * 128 + some, :] = part

    place = step * rows + lax.broadcasted_iota(jnp.int32, (rows, 128), 0)
    hot = jnp.where((place >= begin) & (place < end), 1.0, 0.0).astype(bf16)
    start = lax.dot_general(jnp.concatenate([hot, hot, hot], axis=1), starts[...], NN, preferred_element_type=f32)
    turned[...] = start
    for r in range(0, rows, 32):
        mine = pl.ds(r, 32)
        sin_b, cos_b = turned[mine, :half], turned[mine, half:]
        sin_t, cos_t = table_ref[mine, :half], table_ref[mine, half:]
        x = x_ref[mine, :].astype(f32)
        stream = jnp.concatenate([x[:, :half] + (sin_t * cos_b - cos_t * sin_b),
                                  x[:, half:] + (cos_t * cos_b + sin_t * sin_b)], axis=1)
        stream_ref[mine, :] = stream
        unit, _ = norm_stats(stream)
        normed[mine, :] = (unit * gain_ref[...] + bias_ref[...]).astype(bf16)
    proj_ref[...] = lax.dot_general(normed[...], w_ref[...], NN, preferred_element_type=f32).astype(bf16)

def front(lengths, x, gain, bias, w, *, rows=256):
    length, width = x.shape
    table, freq = place_tables(length, width)
    docs = lengths.shape[1]
    blk = pl.BlockSpec((rows, width), lambda i: (i, 0))
    whole = lambda a: pl.BlockSpec(a.shape, lambda i: (0,) * a.ndim)
    return pl.pallas_call(
        functools.partial(front_kernel, docs=docs),
        grid=(length // rows,),
        in_specs=[pl.BlockSpec(memory_space=pltpu.SMEM), blk, blk, whole(freq), whole(gain), whole(bias), whole(w)],
        out_specs=[blk, pl.BlockSpec((rows, w.shape[1]), lambda i: (i, 0))],
        out_shape=[jax.ShapeDtypeStruct((length, width), f32),
                   jax.ShapeDtypeStruct((length, w.shape[1]), bf16)],
        scratch_shapes=[pltpu.VMEM((384, width), bf16), pltpu.VMEM((rows, width), f32), pltpu.VMEM((rows, width), bf16)],
        compiler_params=pltpu.CompilerParams(vmem_limit_bytes=LIMIT),
        cost_estimate=spend(6),
        name="front",
    )(lengths, x, table, freq, gain, bias, w)

ERF = tuple(0.5 * v for v in (0.254829592, -0.284496736, 1.421413741, -1.453152027, 1.061405429))
ERF_P = 0.3275911

def gelu_both(h):
    bell = jnp.exp2(h * h * (-0.5 * LOG2E))
    d = 1.0 + jnp.abs(h) * (ERF_P / math.sqrt(2.0))
    t = pl.reciprocal(d, approx=True)
    t = t * (2.0 - d * t)
    poly = t * (ERF[0] + t * (ERF[1] + t * (ERF[2] + t * (ERF[3] + t * ERF[4]))))
    tail = poly * bell
    phi = jnp.where(h < 0.0, tail, 1.0 - tail)
    return h * phi, phi + h * bell * (1.0 / math.sqrt(2.0 * math.pi))

def ffn_kernel(stream_ref, mixed_ref, w_out_ref, b_out_ref, gain_ref, bias_ref, w_up_ref, b_up_ref, w_down_ref, b_down_ref,
               after_ref, normed_ref, act_ref, slope_ref, out_ref, h_0, h_1, *, chunk):
    rows = stream_ref.shape[0]
    wide = w_up_ref.shape[1]
    after_ref[...] = lax.dot_general(mixed_ref[...], w_out_ref[...], NN, preferred_element_type=f32)
    for r in range(0, rows, 32):
        mine = pl.ds(r, 32)
        after = stream_ref[mine, :] + after_ref[mine, :] + b_out_ref[...]
        after_ref[mine, :] = after
        unit, _ = norm_stats(after)
        normed_ref[mine, :] = (unit * gain_ref[...] + bias_ref[...]).astype(bf16)
    hs = (h_0, h_1)

    def up(c):
        hs[c % 2][...] = lax.dot_general(normed_ref[...], w_up_ref[:, c * chunk:(c + 1) * chunk], NN, preferred_element_type=f32)

    def bend(c):
        for r in range(0, rows, 32):
            for k in range(0, chunk, 256):
                mine, cols = pl.ds(r, 32), pl.ds(c * chunk + k, 256)
                act, slope = gelu_both(hs[c % 2][mine, k:k + 256] + b_up_ref[:, cols])
                act_ref[mine, cols] = act.astype(bf16)
                slope_ref[mine, cols] = slope.astype(bf16)

    up(0)
    for c in range(wide // chunk):
        if c + 1 < wide // chunk:
            up(c + 1)
        bend(c)
    out = lax.dot_general(act_ref[...], w_down_ref[...], NN, preferred_element_type=f32)
    out_ref[...] = (out + after_ref[...] + b_down_ref[...]).astype(bf16)

def ffn(stream, mixed, w_out, b_out, gain, bias, w_up, b_up, w_down, b_down, *, rows=256, chunk=512):
    length, width = stream.shape
    wide = w_up.shape[1]
    blk = pl.BlockSpec((rows, width), lambda i: (i, 0))
    big = pl.BlockSpec((rows, wide), lambda i: (i, 0))
    whole = lambda a: pl.BlockSpec(a.shape, lambda i: (0,) * a.ndim)
    args = (w_out, b_out, gain, bias, w_up, b_up, w_down, b_down)
    return pl.pallas_call(
        functools.partial(ffn_kernel, chunk=chunk),
        grid=(length // rows,),
        in_specs=[blk, blk] + [whole(a) for a in args],
        out_specs=[blk, blk, big, big, blk],
        out_shape=[jax.ShapeDtypeStruct((length, width), f32), jax.ShapeDtypeStruct((length, width), bf16),
                   jax.ShapeDtypeStruct((length, wide), bf16), jax.ShapeDtypeStruct((length, wide), bf16),
                   jax.ShapeDtypeStruct((length, width), bf16)],
        scratch_shapes=[pltpu.VMEM((rows, chunk), f32), pltpu.VMEM((rows, chunk), f32)],
        compiler_params=pltpu.CompilerParams(vmem_limit_bytes=LIMIT),
        cost_estimate=spend(16),
        name="ffn",
    )(stream, mixed, *args)

def norm_back(g, gain, unit, inv):
    gu = g * gain
    return inv * (gu - jnp.mean(gu, axis=1, keepdims=True) - unit * jnp.mean(gu * unit, axis=1, keepdims=True))

def colsum(x):
    return jnp.sum(x, axis=0, keepdims=True)


def arrange(dst, t, me_ref, ab):
    row8 = t.shape[0] // 8
    for a in range(8):
        r = lax.bitwise_xor(jnp.int32(a), me_ref[0] * 4 + me_ref[1 + ab])
        dst[pl.ds(pl.multiple_of(r * row8, row8), row8), :] = t[a * row8:(a + 1) * row8, :]

def ffn_back_kernel(me_ref, g_ref, act_ref, slope_ref, w_down_ref, w_up_ref, normed_ref, after_ref, gain_ref, mixed_ref, w_out_ref,
                    bdown_ref, send_ref, keep_ref, gafter_ref, gmix_ref, g_low, g_t, norm_t, gh_ref, bup, small):
    i = pl.program_id(0)
    steps = pl.num_programs(0)
    width = g_ref.shape[1]
    tile = slope_ref.shape[1]
    wide = steps * tile
    half = width // 2

    @pl.when(i == 0)
    def _():
        low = g_ref[...].astype(bf16)
        g_low[...] = low
        arrange(g_t, jnp.transpose(low), me_ref, 0)
        arrange(norm_t, jnp.transpose(normed_ref[...]), me_ref, 1)

    def put(at, grad, size):
        cols = pl.ds(pl.multiple_of(at, 128), size)
        keep_ref[:, cols] = grad[:half, :]
        send_ref[:, cols] = grad[half:, :]

    gh = lax.dot_general(g_low[...], w_down_ref[...], NT, preferred_element_type=f32) * slope_ref[...].astype(f32)
    bup[pl.ds(i, 1), :] = colsum(gh)
    gh = gh.astype(bf16)
    gh_ref[:, pl.ds(pl.multiple_of(i * tile, tile), tile)] = gh
    put(i * tile, lax.dot_general(g_t[...], act_ref[...], NN, preferred_element_type=f32).astype(bf16), tile)
    put(i * tile + wide + width, lax.dot_general(norm_t[...], gh, NN, preferred_element_type=f32).astype(bf16), tile)

    @pl.when(i == steps - 1)
    def _():
        gafter_ref[...] = lax.dot_general(gh_ref[...], w_up_ref[...], NT, preferred_element_type=f32)
        fold = lambda x: x[0:8] + x[8:16] + x[16:24] + x[24:32]
        sums = [jnp.zeros((8, width), f32)] * 3
        for r in range(0, g_ref.shape[0], 32):
            mine = pl.ds(r, 32)
            unit, inv = norm_stats(after_ref[mine, :])
            gn = gafter_ref[mine, :]
            ga = g_ref[mine, :] + norm_back(gn, gain_ref[...], unit, inv)
            gafter_ref[mine, :] = ga
            g_low[mine, :] = ga.astype(bf16)
            sums = [s + fold(x) for s, x in zip(sums, (gn * unit, gn, ga))]
        gmix_ref[...] = lax.dot_general(g_low[...], w_out_ref[...], NT, preferred_element_type=f32).astype(bf16)
        arrange(g_t, jnp.transpose(mixed_ref[...]), me_ref, 0)
        put(wide, lax.dot_general(g_t[...], g_low[...], NN, preferred_element_type=f32).astype(bf16), width)
        small[...] = jnp.zeros_like(small)
        small[0:1, :] = bdown_ref[...]
        for k in range(3):
            small[1 + k:2 + k, :] = colsum(sums[k])
        per = width // tile if tile < width else 1
        for k in range(wide // width):
            if tile >= width:
                many = tile // width
                small[4 + k:5 + k, :] = bup[k // many:k // many + 1, (k % many) * width:(k % many + 1) * width]
            else:
                for m in range(per):
                    small[4 + k:5 + k, m * tile:(m + 1) * tile] = bup[k * per + m:k * per + m + 1, :]
        arrange(norm_t.at[:, :128], jnp.transpose(small[...]).astype(bf16), me_ref, 1)
        put(2 * wide + width, norm_t[:, :128], 128)

def ffn_back(me, g, act, slope, w_down, w_up, normed, after, gain, mixed, w_out, bdown, *, tile=512):
    length, width = g.shape
    wide = slope.shape[1]
    steps = wide // tile
    whole = lambda a: pl.BlockSpec(a.shape, lambda i, m: (0,) * a.ndim)
    full = lambda s: pl.BlockSpec(s, lambda i, m: (0,) * len(s))
    sums = (width // 2, 2 * wide + width + 128)
    return pl.pallas_call(
        ffn_back_kernel,
        grid_spec=pltpu.PrefetchScalarGridSpec(
            num_scalar_prefetch=1, grid=(steps,),
            in_specs=[whole(g), pl.BlockSpec((length, tile), lambda i, m: (0, i)), pl.BlockSpec((length, tile), lambda i, m: (0, i)),
                      pl.BlockSpec((tile, width), lambda i, m: (i, 0)),
                      whole(w_up), whole(normed), whole(after), whole(gain), whole(mixed), whole(w_out), whole(bdown)],
            out_specs=[full(sums), full(sums), full((length, width)), full((length, width))],
            scratch_shapes=[pltpu.VMEM((length, width), bf16), pltpu.VMEM((width, length), bf16), pltpu.VMEM((width, length), bf16),
                            pltpu.VMEM((length, wide), bf16), pltpu.VMEM((steps, tile), f32), pltpu.VMEM((128, width), f32)]),
        out_shape=[jax.ShapeDtypeStruct(sums, bf16)] * 2
        + [jax.ShapeDtypeStruct((length, width), f32), jax.ShapeDtypeStruct((length, width), bf16)],
        compiler_params=pltpu.CompilerParams(vmem_limit_bytes=LIMIT),
        cost_estimate=spend(20),
        name="ffn_back",
    )(me, g, act, slope, w_down, w_up, normed, after, gain, mixed, w_out, bdown)

def window(refs, start, size):
    found, at = [], 0
    for ref in refs:
        low, high = max(start, at), min(start + size, at + ref.shape[1])
        if low < high:
            found.append(ref[:, low - at:high - at])
        at += ref.shape[1]
    return found[0] if len(found) == 1 else jnp.concatenate(found, axis=1)

def qkv_grad_kernel(me_ref, *refs, parts):
    gps, (stream_ref, gain_ref, bias_ref, w_ref, send_ref, keep_ref, unit_t, rows_t, unit_ref) = refs[:parts], refs[parts:]
    length, width = stream_ref.shape
    half = width // 2
    for r in range(0, length, 32):
        unit, _ = norm_stats(stream_ref[pl.ds(r, 32), :])
        unit_ref[pl.ds(r, 32), :] = unit.astype(bf16)
    t = jnp.transpose(unit_ref[...])
    column_of = lambda row: jnp.transpose(jnp.broadcast_to(row, (128, width)))
    gain, bias = column_of(gain_ref[...]), column_of(bias_ref[...])
    for ab in range(2):
        arrange(unit_t.at[ab], t, me_ref, ab)
    gains, biases, ws = [], [], []
    for ab in range(2):
        arrange(rows_t, gain, me_ref, ab)
        gains.append(rows_t[:, :1])
        arrange(rows_t, bias, me_ref, ab)
        biases.append(rows_t[:, :1])
    total = 3 * width
    cut = total // 2
    gain_grad = [jnp.zeros((width, 1), f32), jnp.zeros((width, 1), f32)]
    bias_grad = [jnp.zeros((width, 1), f32), jnp.zeros((width, 1), f32)]
    for at in range(0, total, 256):
        ab = 0 if at < cut else 1
        gp = window(gps, at, 256)
        m = lax.dot_general(unit_t[ab], gp, NN, preferred_element_type=f32)
        s = colsum(gp.astype(f32))
        grad = (m * gains[ab] + biases[ab] * s).astype(bf16)
        keep_ref[:, at:at + 256] = grad[:half, :]
        send_ref[:, at:at + 256] = grad[half:, :]
        arrange_w = []
        row8 = width // 8
        for r in range(8):
            a = lax.bitwise_xor(jnp.int32(r), me_ref[0] * 4 + me_ref[1 + ab])
            arrange_w.append(w_ref[pl.ds(pl.multiple_of(a * row8, row8), row8), at:at + 256])
        w = jnp.concatenate(arrange_w, axis=0).astype(f32)
        gain_grad[ab] = gain_grad[ab] + jnp.sum(m * w, axis=1, keepdims=True)
        bias_grad[ab] = bias_grad[ab] + jnp.sum(w * s, axis=1, keepdims=True)
    row8 = width // 8
    lane = lax.broadcasted_iota(jnp.int32, (1, 128), 1)
    both = [jnp.where(lane == 0, gain_grad[ab], jnp.where(lane == 1, bias_grad[ab], 0.0)) for ab in range(2)]
    for r in range(8):
        to = lax.bitwise_xor(jnp.int32(r), lax.bitwise_xor(me_ref[1], me_ref[2]))
        rows_t[pl.ds(pl.multiple_of(to * row8, row8), row8), :] = both[0][r * row8:(r + 1) * row8, :]
    small = (rows_t[...] + both[1]).astype(bf16)
    keep_ref[:, total:] = small[:half, :]
    send_ref[:, total:] = small[half:, :]

def qkv_grad(me, gps, stream, gain, bias, w):
    length, width = stream.shape
    vm = pl.BlockSpec(memory_space=pltpu.VMEM)
    parts = len(gps)
    return pl.pallas_call(
        functools.partial(qkv_grad_kernel, parts=parts),
        in_specs=[pl.BlockSpec(memory_space=pltpu.SMEM)] + [vm] * (parts + 4),
        out_specs=[vm, vm],
        out_shape=[jax.ShapeDtypeStruct((width // 2, 3 * width + 128), bf16)] * 2,
        scratch_shapes=[pltpu.VMEM((2, width, length), bf16), pltpu.VMEM((width, 128), f32),
                        pltpu.VMEM((length, width), bf16)],
        compiler_params=pltpu.CompilerParams(vmem_limit_bytes=LIMIT),
        cost_estimate=spend(0.2),
        name="qkv_grad",
    )(me, *gps, stream, gain, bias, w)

def front_back_kernel(*refs, parts):
    gps, (w_ref, stream_ref, gafter_ref, gain_ref, out_ref, gn_ref) = refs[:parts], refs[parts:]
    gp = window(gps, 0, w_ref.shape[1])
    gn_ref[...] = lax.dot_general(gp, w_ref[...], NT, preferred_element_type=f32)
    for r in range(0, gn_ref.shape[0], 32):
        mine = pl.ds(r, 32)
        unit, inv = norm_stats(stream_ref[mine, :])
        out_ref[mine, :] = (gafter_ref[mine, :] + norm_back(gn_ref[mine, :], gain_ref[...], unit, inv)).astype(bf16)

def front_back(gps, w, stream, gafter, gain, *, rows=256):
    length, width = stream.shape
    blk = pl.BlockSpec((rows, width), lambda i: (i, 0))
    whole = lambda a: pl.BlockSpec(a.shape, lambda i: (0,) * a.ndim)
    return pl.pallas_call(
        functools.partial(front_back_kernel, parts=len(gps)),
        grid=(length // rows,),
        in_specs=[pl.BlockSpec((rows, gp.shape[1]), lambda i: (i, 0)) for gp in gps] + [whole(w), blk, blk, whole(gain)],
        out_specs=blk,
        out_shape=jax.ShapeDtypeStruct((length, width), bf16),
        scratch_shapes=[pltpu.VMEM((rows, width), f32)],
        compiler_params=pltpu.CompilerParams(vmem_limit_bytes=LIMIT),
        cost_estimate=spend(0.2),
        name="front_back",
    )(*gps, w, stream, gafter, gain)


def finish_kernel(me_ref, own_a, own_b, got_a, got_b, *refs, plan, n):
    outs, whole = refs[:-1], refs[-1]
    rows, cut = own_a.shape
    chunk = rows // (4 * n)

    def lay(dst, at, size):
        ab = 0 if at < cut else 1
        at -= ab * cut
        for near, ref in ((0, (own_a, own_b)[ab]), (1, (got_a, got_b)[ab])):
            core = lax.bitwise_xor(jnp.int32(near), me_ref[0])
            for pq in range(4):
                for z in range(n):
                    to = core * 4 + lax.bitwise_xor(jnp.int32(pq), me_ref[1 + ab])
                    to = to * n + lax.bitwise_xor(jnp.int32(z), me_ref[3])
                    r = (pq * n + z) * chunk
                    dst[pl.ds(pl.multiple_of(to * chunk, chunk), chunk), :] = ref[r:r + chunk, at:at + size].astype(f32)

    for at, size, out, col, turned in plan:
        if out < 0:
            lay(whole.at[:, :size], at, size)
            flat = jnp.transpose(whole[:, :size])
            done = 0
            for v in outs[out:]:
                width = flat.shape[1]
                for k in range(v.shape[1] // width):
                    v[:, k * width:(k + 1) * width] = flat[done:done + 1, :]
                    done += 1
        elif not turned:
            lay(outs[out].at[:, col:col + size], at, size)
        else:
            lay(whole.at[:, :size], at, size)
            flat = jnp.transpose(whole[:, :size])
            outs[out][col:col + size, :] = flat[:outs[out].shape[0] - col, :]

def finish(me, pieces, shapes, plan, *, n, us):
    rows = pieces[0].shape[0]
    vm = pl.BlockSpec(memory_space=pltpu.VMEM)
    return pl.pallas_call(
        functools.partial(finish_kernel, plan=plan, n=n),
        in_specs=[pl.BlockSpec(memory_space=pltpu.SMEM)] + [vm] * 4,
        out_specs=[vm] * len(shapes),
        out_shape=[jax.ShapeDtypeStruct(s, f32) for s in shapes],
        scratch_shapes=[pltpu.VMEM((2 * rows, 256), f32)],
        compiler_params=pltpu.CompilerParams(vmem_limit_bytes=LIMIT),
        cost_estimate=spend(us),
        name="finish",
    )(me, *pieces)

class Links:
    def __init__(self, mesh):
        self.sizes = dict(mesh.shape)
        self.n = self.sizes["rows"] // 2
        self.fine = self.n == 4
        self.zi = lax.axis_index("rows") // 2

    def swap(self, x, axis, bit):
        return lax.ppermute(x, axis, [(a, a ^ bit) for a in range(self.sizes[axis])])

    def core(self, x):
        return self.swap(x, "bank", 1)

    def near(self, x):
        return self.swap(x, "bank", 2)

    def side(self, x):
        return self.swap(x, "rows", 1)

def plus(*terms):
    out = terms[0].astype(f32)
    for t in terms[1:]:
        out = out + t.astype(f32)
    return out.astype(bf16)

def stacked(pieces):
    rows = sum(p.shape[0] for p in pieces)
    out, at = None, 0
    for p in pieces:
        term = lax.pad(p, jnp.zeros((), p.dtype), [(at, rows - at - p.shape[0], 0), (0, 0, 0)])
        out = term if out is None else out + term
        at += p.shape[0]
    return out

def chain(links, send, keep, cut):
    n = links.n
    got, = yield [(links.core, send)]
    half = keep.shape[0] // 2
    sa, sb = plus(keep[half:, :cut], got[half:, :cut]), plus(keep[half:, cut:], got[half:, cut:])
    a, b = plus(keep[:half, :cut], got[:half, :cut]), plus(keep[:half, cut:], got[:half, cut:])
    ra, rb = yield [(links.near, sa), (links.side, sb)]
    half //= 2
    sa, sb = plus(a[half:], ra[half:]), plus(b[half:], rb[half:])
    a, b = plus(a[:half], ra[:half]), plus(b[:half], rb[:half])
    ra, rb = yield [(links.side, sa), (links.near, sb)]
    z = jnp.concatenate([plus(a, ra), plus(b, rb)], axis=1)
    chunk = half // n
    if links.fine:
        piece = lambda k: lax.dynamic_slice(z, ((links.zi ^ k) * chunk, 0), (chunk, z.shape[1]))
        hops = [functools.partial(links.swap, axis="rows", bit=2 * k) for k in range(1, n)]
        got = yield [(hop, piece(k + 1)) for k, hop in enumerate(hops)]
        mine = plus(piece(0), *got)
        got = yield [(hop, mine) for hop in hops]
        a = stacked([v[:, :cut] for v in (mine, *got)])
        b = stacked([v[:, cut:] for v in (mine, *got)])
    else:
        groups = [[r for r in range(2 * n) if r % 2 == y] for y in range(2)]
        z, = yield [(lambda v: lax.psum(v, "rows", axis_index_groups=groups), z)]
        yield []
        a, b = z[:, :cut], z[:, cut:]
    ra, rb = yield [(links.side, a), (links.near, b)]
    a, b = stacked([a, ra]), stacked([b, rb])
    ra, rb = yield [(links.near, a), (links.side, b)]
    a, b = stacked([a, ra]), stacked([b, rb])
    ga, gb = yield [(links.core, a), (links.core, b)]
    yield (a, b, ga, gb)

class Step:
    def __init__(self, *args):
        self.run = chain(*args)
        self.sends = next(self.run)

    def go(self):
        self.got = [how(what) for how, what in self.sends]

    def take(self):
        self.sends = self.run.send(self.got)

def tie(steps, *extra):
    flat = [what for s in steps for _, what in s.sends] + list(extra)
    flat = list(lax.optimization_barrier(tuple(flat)))
    for s in steps:
        s.sends = [(how, flat.pop(0)) for how, _ in s.sends]
    return flat

def tiles_of(start, width, out, turned):
    plan, at = [], 0
    while at < width:
        size = min(256, width - at)
        plan.append((start + at, size, out, at, turned))
        at += size
    return plan

def body(mesh, hidden_in, lengths, ln1_gain, ln1_bias, w_qkv, w_out, b_out, ln2_gain, ln2_bias, w_up, b_up, w_down, b_down,
         bank, bank_labels, target_slots, gold_ids):
    links = Links(mesh)
    row = lambda v: v.reshape(1, -1)
    width = hidden_in.shape[1]
    wide = w_up.shape[1]
    ib, ir = lax.axis_index("bank"), lax.axis_index("rows")
    core, x, y = ib % 2, ib // 2, ir % 2
    me = jnp.stack([core, x * 2 + y, y * 2 + x, links.zi if links.fine else 0, ib]).astype(jnp.int32)
    own = with_labels(bank, bank_labels)
    other = links.core(own)
    near = links.near(own)
    stream, projected = front(lengths, hidden_in, row(ln1_gain), row(ln1_bias), w_qkv)
    mixed, lse = attn_fwd(lengths, projected)
    after, normed_c, act, slope, block_out = ffn(stream, mixed, w_out, row(b_out), row(ln2_gain), row(ln2_bias), w_up, row(b_up),
                                                 w_down, row(b_down), chunk=256)
    e, hist, sums = bank_first(me, block_out, gold_ids, target_slots, own, other)
    near, e = lax.optimization_barrier((near, e))
    far = links.core(near)
    g, loss, bdown = bank_last(me, lengths, block_out, gold_ids, target_slots, e, hist, sums, own, other, near, far)
    send, keep, gafter, gmix = ffn_back(me, g, act, slope, w_down, w_up, normed_c, after, row(ln2_gain), mixed, w_out, bdown)
    cut = wide + width
    n = links.n if links.fine else 1
    one = Step(links, send, keep, cut)
    one.go()
    parts = []
    back = lambda first, count: parts.append(attn_bwd(lengths, projected, mixed, gmix, lse, first=first, count=count, us=0.2 * count))
    for first, count in ((0, 1), (1, 2), (3, 1)):
        back(first, count)
        one.take()
        gmix, *parts[-1] = tie([one], gmix, *parts[-1])
        one.go()
    gps = [p[k] for k in range(3) for p in parts]
    send, keep = qkv_grad(me, gps, stream, row(ln1_gain), row(ln1_bias), w_qkv)
    cut2 = 3 * width // 2
    two = Step(links, send, keep, cut2)
    two.go()
    one.take()
    two.take()
    tie([one, two])
    one.go()
    two.go()
    two.take()
    tie([two])
    two.go()
    one.take()
    two.take()
    tie([one, two])
    one.go()
    two.go()
    one.take()
    two.take()
    gafter, = tie([one, two], gafter)
    one.go()
    two.go()
    input_grad = front_back(gps, w_qkv, stream, gafter, row(ln1_gain))
    one.take()
    two.take()
    input_grad, = tie([one, two], input_grad)
    one.go()
    two.go()
    one.take()
    vector = (1, width)
    two.take()
    pieces = tie([two], *one.sends)
    two.go()
    w_down_grad, w_out_grad, w_up_grad, *small = finish(
        me, pieces, [(wide, width), (width, width), (width, wide)] + [vector] * 4 + [(1, wide)],
        tiles_of(0, wide, 0, True) + tiles_of(wide, width, 1, False) + tiles_of(cut, wide, 2, False) + tiles_of(cut + wide, 128, -5, True),
        n=n, us=0.2)
    two.take()
    w_down_grad, = tie([two], w_down_grad)
    two.go()
    two.take()
    w_qkv_grad, *small1 = finish(me, two.sends, [(width, 3 * width), vector, vector],
                                 tiles_of(0, 3 * width, 0, False) + tiles_of(3 * width, 128, -2, True), n=n, us=0.2)
    flat = lambda v: v.reshape(-1)
    return (block_out, flat(loss), input_grad, flat(small1[0]), flat(small1[1]), w_qkv_grad, w_out_grad, flat(small[3]),
            flat(small[1]), flat(small[2]), w_up_grad, flat(small[4]), w_down_grad, flat(small[0]))

def solution(mesh):
    in_specs = (
        P(("rows", "bank"), None),
        P(("rows", "bank"), None),
        P(),
        P(),
        P(),
        P(),
        P(),
        P(),
        P(),
        P(),
        P(),
        P(),
        P(),
        P("bank", None),
        P("bank"),
        P(("rows", "bank")),
        P(("rows", "bank")),
    )
    out_specs = (
        P(("rows", "bank"), None),
        P(("rows", "bank")),
        P(("rows", "bank"), None),
        P(),
        P(),
        P(),
        P(),
        P(),
        P(),
        P(),
        P(),
        P(),
        P(),
        P(),
    )
    return jax.shard_map(functools.partial(body, mesh), mesh=mesh, in_specs=in_specs, out_specs=out_specs, check_vma=False)
```

```python
import functools
import math

import jax
import jax.numpy as jnp
import numpy as np
from jax import lax
from jax.experimental import pallas as pl
from jax.experimental.pallas import tpu as pltpu
from jax.sharding import PartitionSpec as P

LOG2E = 1.4426950408889634
LN2 = 0.6931471805599453
NT = (((1,), (1,)), ((), ()))
NN = (((1,), (0,)), ((), ()))
f32, bf16 = jnp.float32, jnp.bfloat16

LIMIT = 60 * 2 ** 20

def spend(us):
    return pl.CostEstimate(flops=int(us * 1.0e9), bytes_accessed=0, transcendentals=0)

def column(row, rows):
    return jnp.transpose(jnp.broadcast_to(row.astype(f32), (128, rows)))[:, :1]

class Slots:
    def __init__(self, bank_ref, marks_ref, gold_ref, target_ref, rows, tile, strip):
        self.bank_ref, self.marks_ref, self.gold_ref, self.target_ref = bank_ref, marks_ref, gold_ref, target_ref
        self.rows, self.tile, self.strip = rows, tile, strip
        self.width = bank_ref.shape[1]
        self.c = LOG2E / math.sqrt(self.width)

    def wide(self, col):
        return jnp.concatenate([col] * (self.tile // 128), axis=1)

    def keys(self, j):
        return self.bank_ref[pl.ds(pl.multiple_of(j * self.tile, self.tile), self.tile), :]

    def positive(self, j, at):
        tall = lambda v: jnp.concatenate([v] * (self.strip // 8), axis=0)
        mine = pl.ds(at, self.strip)
        return (tall(self.marks_ref[0, j]) == self.wide(self.gold_ref[mine, :])) | (
            tall(self.marks_ref[1, j]) == self.wide(self.target_ref[mine, :]))

    def fold(self, x, op):
        out = x[:, :128]
        for i in range(1, self.tile // 128):
            out = op(out, x[:, i * 128:(i + 1) * 128])
        return out

    def scores(self, q, j):
        return lax.dot_general(q, self.keys(j), NT, preferred_element_type=f32)

    def eat(self, j, s_ref, e_ref, at, top_ref, all_ref, pos_ref, hist_ref):
        for r in range(0, self.rows, self.strip):
            mine = pl.ds(r, self.strip)
            s = s_ref[mine, :]
            top = top_ref[mine, :]
            new_top = jnp.maximum(top, jnp.max(self.fold(s, jnp.maximum), axis=1, keepdims=True) * self.c)
            shrink = jnp.exp2(top - new_top)
            e = jnp.exp2(s * self.c - self.wide(new_top))
            e_ref[at, mine, :] = e
            all_ref[mine, :] = all_ref[mine, :] * shrink + self.fold(e, jnp.add)
            pos_ref[mine, :] = pos_ref[mine, :] * shrink + self.fold(jnp.where(self.positive(j, r), e, 0.0), jnp.add)
            top_ref[mine, :] = new_top
            hist_ref[at, mine, :] = new_top

    def eat_all(self, q, first, count, s0_ref, s1_ref, e_ref, top_ref, all_ref, pos_ref, hist_ref):
        bufs = (s0_ref, s1_ref)
        bufs[0][...] = self.scores(q, first)
        for k in range(count):
            if k + 1 < count:
                bufs[(k + 1) % 2][...] = self.scores(q, first + k + 1)
            self.eat(first + k, bufs[k % 2], e_ref, k, top_ref, all_ref, pos_ref, hist_ref)

def fetch(shards, bank_ref, label_ref, sems):
    size = bank_ref.shape[0] // len(shards)
    copies = []
    for k, ref in enumerate(shards):
        copies.append((pltpu.make_async_copy(ref.at[pl.ds(0, size)], bank_ref.at[pl.ds(k * size, size)], sems.at[2 * k]),
                       pltpu.make_async_copy(ref.at[pl.ds(size, 16)], label_ref.at[k], sems.at[2 * k + 1])))
    return copies

def write_marks(label_ref, marks_ref, shard):
    tiles, _, tile = marks_ref.shape[1:]
    width = label_ref.shape[2]
    for j in range(tiles):
        owner, at = j * tile // shard, j * tile % shard // width
        for k in range(tile // width):
            marks_ref[0, j, :, k * width:(k + 1) * width] = jnp.broadcast_to(label_ref[owner, at + k:at + k + 1, :].astype(f32), (8, width))
        marks_ref[1, j] = (lax.broadcasted_iota(jnp.int32, (8, tile), 1) + j * tile).astype(f32)

def write_wanted(me_ref, gold_ref, target_ref, gold_b, target_b, shard, rows):
    turn = lambda row: jnp.transpose(jnp.broadcast_to(row.astype(f32), (128, rows)))
    gold_b[...] = turn(gold_ref[...])
    target_b[...] = turn(lax.bitwise_xor(target_ref[...], me_ref[4] * shard))

def bank_first_kernel(me_ref, q_ref, gold_ref, target_ref, own_hbm, core_hbm, e_ref, hist_ref, sums_ref,
                      bank_ref, label_ref, marks_ref, gold_b, target_b, top_ref, all_ref, pos_ref, s0_ref, s1_ref, sems,
                      *, rows, tile, strip):
    step = pl.program_id(0)
    tiles = bank_ref.shape[0] // tile
    shard = bank_ref.shape[0] // 2
    copies = fetch((own_hbm, core_hbm), bank_ref, label_ref, sems)

    @pl.when(step == 0)
    def _():
        for pair in copies:
            for copy in pair:
                copy.start()
        for pair in copies:
            for copy in pair:
                copy.wait()
        write_marks(label_ref, marks_ref, shard)
    write_wanted(me_ref, gold_ref, target_ref, gold_b, target_b, shard, rows)
    know = Slots(bank_ref, marks_ref, gold_b, target_b, rows, tile, strip)
    top_ref[...] = jnp.full((rows, 128), -3e38, f32)
    all_ref[...] = jnp.zeros((rows, 128), f32)
    pos_ref[...] = jnp.zeros((rows, 128), f32)
    know.eat_all(q_ref[...], 0, tiles, s0_ref, s1_ref, e_ref, top_ref, all_ref, pos_ref, hist_ref)
    sums_ref[0] = all_ref[...]
    sums_ref[1] = pos_ref[...]

def bank_last_kernel(me_ref, lengths_ref, q_ref, gold_ref, target_ref, e_ref, hist_ref, sums_ref, own_hbm, core_hbm, near_hbm, far_hbm,
                     grad_ref, loss_ref, bsum_ref,
                     bank_ref, label_ref, marks_ref, gold_b, target_b, top_ref, all_ref, pos_ref, on_ref, off_ref, g_ref, g2_ref,
                     s0_ref, s1_ref, e2_ref, hist2_ref, sems, *, rows, tile, docs, strip):
    step = pl.program_id(0)
    width = q_ref.shape[1]
    tiles = bank_ref.shape[0] // tile
    half = tiles // 2
    shard = bank_ref.shape[0] // 4
    copies = fetch((own_hbm, core_hbm, near_hbm, far_hbm), bank_ref, label_ref, sems)

    @pl.when(step == 0)
    def _():
        for pair in copies[2:] + copies[:2]:
            for copy in pair:
                copy.start()
        for pair in copies:
            pair[1].wait()
        for pair in copies[2:]:
            pair[0].wait()
        write_marks(label_ref, marks_ref, shard)
    write_wanted(me_ref, gold_ref, target_ref, gold_b, target_b, shard, rows)
    know = Slots(bank_ref, marks_ref, gold_b, target_b, rows, tile, strip)
    q = q_ref[...]
    total = lengths_ref[0, 0]
    for j in range(1, docs):
        total = total + lengths_ref[0, j]
    live = step * rows + lax.broadcasted_iota(jnp.int32, (rows, 128), 0) < total
    top_ref[...] = hist_ref[half - 1]
    all_ref[...] = sums_ref[0]
    pos_ref[...] = sums_ref[1]
    know.eat_all(q, half, half, s0_ref, s1_ref, e2_ref, top_ref, all_ref, pos_ref, hist2_ref)
    broad = lambda col: jnp.broadcast_to(col, (rows, 128))
    top = top_ref[...]
    sum_all = broad(jnp.sum(all_ref[...], axis=1, keepdims=True))
    sum_pos = broad(jnp.sum(pos_ref[...], axis=1, keepdims=True))
    inv_all = jnp.where(live, 1.0 / sum_all, 0.0)
    off_ref[...] = inv_all
    on_ref[...] = inv_all - jnp.where(live, 1.0 / sum_pos, 0.0)

    def show(loss):
        loss_ref[...] = jnp.transpose(jnp.where(live, loss, 0.0))[:1, :]
    show((jnp.log2(sum_all) - jnp.log2(sum_pos)) * LN2)

    safe = jnp.min(sum_pos) >= 2.0 ** -60

    def pull(source, hists, j, at, g_ref):
        for r in range(0, rows, strip):
            mine = pl.ds(r, strip)
            factor = jnp.exp2(hists[at, mine, :] - top_ref[mine, :])
            weight = jnp.where(know.positive(j, r), know.wide(factor * on_ref[mine, :]), know.wide(factor * off_ref[mine, :]))
            g_ref[mine, :] = (source[at, mine, :] * weight).astype(bf16)
        return lax.dot_general(g_ref[...], know.keys(j), NN, preferred_element_type=f32)

    @pl.when(step == 0)
    def _():
        for pair in copies[:2]:
            pair[0].wait()

    @pl.when(safe)
    def _():
        acc = None
        for j in range(tiles):
            near = j >= half
            term = pull(e2_ref if near else e_ref, hist2_ref if near else hist_ref, j, j - half if near else j, (g_ref, g2_ref)[j % 2])
            acc = term if acc is None else acc + term
        grad_ref[...] = acc

    @pl.when(jnp.logical_not(safe))
    def _():
        grad_ref[...] = jnp.zeros_like(grad_ref)
        all_ref[...] = jnp.where(live, top + jnp.log2(sum_all), 1e30)
        top_ref[...] = jnp.full((rows, 128), -1e30, f32)
        pos_ref[...] = jnp.zeros((rows, 128), f32)

        def own_top(j, _):
            s0_ref[...] = know.scores(q, j)
            for r in range(0, rows, strip):
                mine = pl.ds(r, strip)
                x = jnp.where(know.positive(j, r), s0_ref[mine, :] * know.c, -1e30)
                top_ref[mine, :] = jnp.maximum(top_ref[mine, :], know.fold(x, jnp.maximum))
            return 0
        lax.fori_loop(0, tiles, own_top, 0)
        top_ref[...] = broad(jnp.max(top_ref[...], axis=1, keepdims=True))

        def own_sum(j, _):
            s0_ref[...] = know.scores(q, j)
            for r in range(0, rows, strip):
                mine = pl.ds(r, strip)
                x = jnp.where(know.positive(j, r), s0_ref[mine, :] * know.c, -1e30)
                pos_ref[mine, :] += know.fold(jnp.exp2(x - know.wide(top_ref[mine, :])), jnp.add)
            return 0
        lax.fori_loop(0, tiles, own_sum, 0)
        lse_pos = top_ref[...] + jnp.log2(broad(jnp.sum(pos_ref[...], axis=1, keepdims=True)))
        show((top + jnp.log2(sum_all) - lse_pos) * LN2)
        pos_ref[...] = jnp.where(live, lse_pos, 1e30)

        def draw(j, _):
            s0_ref[...] = know.scores(q, j)
            for r in range(0, rows, strip):
                mine = pl.ds(r, strip)
                s = s0_ref[mine, :] * know.c
                x = jnp.where(know.positive(j, r), s, -1e30)
                g = jnp.exp2(s - know.wide(all_ref[mine, :])) - jnp.exp2(x - know.wide(pos_ref[mine, :]))
                g_ref[mine, :] = g.astype(bf16)
            grad_ref[...] += lax.dot_general(g_ref[...], know.keys(j), NN, preferred_element_type=f32)
            return 0
        lax.fori_loop(0, tiles, draw, 0)
    grad_ref[...] = grad_ref[...] * (1.0 / math.sqrt(width))
    part = jnp.sum(grad_ref[...], axis=0, keepdims=True)
    bsum_ref[...] = jnp.where(step == 0, part, bsum_ref[...] + part)

def with_labels(bank, labels):
    width = bank.shape[1]
    rows = labels.astype(bf16).reshape(-1, width)
    return jnp.concatenate([bank, jnp.pad(rows, ((0, 16 - rows.shape[0]), (0, 0)))], axis=0)

def bank_specs(rows, width):
    smem, hbm = pl.BlockSpec(memory_space=pltpu.SMEM), pl.BlockSpec(memory_space=pl.ANY)
    blk = pl.BlockSpec((rows, width), lambda i: (i, 0))
    line = pl.BlockSpec((1, rows), lambda i: (0, i))
    return smem, hbm, blk, line

def bank_first(me, q, gold, target, own, core, *, rows=256, tile=1024, strip=32):
    length, width = q.shape
    tiles = 2 * (own.shape[0] - 16) // tile
    smem, hbm, blk, line = bank_specs(rows, width)
    part = pltpu.VMEM((rows, 128), f32)
    return pl.pallas_call(
        functools.partial(bank_first_kernel, rows=rows, tile=tile, strip=strip),
        grid=(length // rows,),
        in_specs=[smem, blk, line, line, hbm, hbm],
        out_specs=[pl.BlockSpec((tiles, rows, tile), lambda i: (0, i, 0)), pl.BlockSpec((tiles, rows, 128), lambda i: (0, i, 0)),
                   pl.BlockSpec((2, rows, 128), lambda i: (0, i, 0))],
        out_shape=[jax.ShapeDtypeStruct((tiles, length, tile), f32), jax.ShapeDtypeStruct((tiles, length, 128), f32),
                   jax.ShapeDtypeStruct((2, length, 128), f32)],
        scratch_shapes=[pltpu.VMEM((tiles * tile, width), bf16), pltpu.VMEM((2, 16, width), bf16), pltpu.VMEM((2, tiles, 8, tile), f32),
                        part, part, part, part, part,
                        pltpu.VMEM((rows, tile), f32), pltpu.VMEM((rows, tile), f32), pltpu.SemaphoreType.DMA((4,))],
        compiler_params=pltpu.CompilerParams(vmem_limit_bytes=LIMIT),
        cost_estimate=spend(13),
        name="bank_first",
    )(me, q, gold.reshape(1, length), target.reshape(1, length), own, core)

def bank_last(me, lengths, q, gold, target, e, hist, sums, own, core, near, far, *, rows=256, tile=1024, strip=32):
    length, width = q.shape
    half = e.shape[0]
    docs = lengths.shape[1]
    smem, hbm, blk, line = bank_specs(rows, width)
    part = pltpu.VMEM((rows, 128), f32)
    return pl.pallas_call(
        functools.partial(bank_last_kernel, rows=rows, tile=tile, docs=docs, strip=strip),
        grid=(length // rows,),
        in_specs=[smem, smem, blk, line, line, pl.BlockSpec((half, rows, tile), lambda i: (0, i, 0)),
                  pl.BlockSpec((half, rows, 128), lambda i: (0, i, 0)), pl.BlockSpec((2, rows, 128), lambda i: (0, i, 0)),
                  hbm, hbm, hbm, hbm],
        out_specs=[blk, line, pl.BlockSpec((1, width), lambda i: (0, 0))],
        out_shape=[jax.ShapeDtypeStruct((length, width), f32), jax.ShapeDtypeStruct((1, length), f32),
                   jax.ShapeDtypeStruct((1, width), f32)],
        scratch_shapes=[pltpu.VMEM((2 * half * tile, width), bf16), pltpu.VMEM((4, 16, width), bf16),
                        pltpu.VMEM((2, 2 * half, 8, tile), f32),
                        part, part, part, part, part, part, part, pltpu.VMEM((rows, tile), bf16), pltpu.VMEM((rows, tile), bf16),
                        pltpu.VMEM((rows, tile), f32), pltpu.VMEM((rows, tile), f32), pltpu.VMEM((half, rows, tile), f32),
                        pltpu.VMEM((half, rows, 128), f32), pltpu.SemaphoreType.DMA((8,))],
        compiler_params=pltpu.CompilerParams(vmem_limit_bytes=LIMIT),
        cost_estimate=spend(25),
        name="bank_last",
    )(me, lengths, q, gold.reshape(1, length), target.reshape(1, length), e, hist, sums, own, core, near, far)

TN = (((0,), (0,)), ((), ()))
BIG = 1e30
STAT = 120
NEG = -1e30

def doc_bounds(lengths_ref, docs):
    lane = lax.broadcasted_iota(jnp.int32, (1, 128), 1)
    begin = jnp.zeros((1, 128), jnp.int32)
    end = jnp.zeros((1, 128), jnp.int32)
    at = jnp.int32(0)
    for j in range(docs):
        begin = jnp.where(lane == j, at, begin)
        at = at + lengths_ref[0, j]
        end = jnp.where(lane == j, at, end)
    begin = jnp.where(lane == docs, at, begin)
    end = jnp.where(lane == docs, 2 ** 30, end)
    return begin, end, at

def one_hot_docs(lengths_ref, docs, length):
    begin, end, _ = doc_bounds(lengths_ref, docs)
    place = lax.broadcasted_iota(jnp.int32, (length, 128), 0)
    return (place >= begin) & (place < end)

def split3(col):
    hi = col.astype(bf16).astype(f32)
    mid = (col - hi).astype(bf16).astype(f32)
    lo = col - hi - mid
    return hi, mid, lo

def with_stat(base, col, lane):
    hi, mid, lo = split3(col)
    return jnp.where(lane == STAT, hi, jnp.where(lane == STAT + 1, mid, jnp.where(lane == STAT + 2, lo, base))).astype(bf16)

def key_marks(hot, lane):
    ones = (lane >= STAT) & (lane < STAT + 3)
    return jnp.where(ones, 1.0, jnp.where(hot, 0.0, -BIG)).astype(bf16)

def attn_fwd_kernel(lengths_ref, q_ref, k_ref, v_ref, mixed_ref, lse_ref, aug_q, aug_k, kk, s_0, s_1, e_0, e_1, scales, held,
                    *, docs, dim, block, strip):
    s_refs, e_refs = (s_0, s_1), (e_0, e_1)
    pair = pl.program_id(0)
    length = q_ref.shape[0]
    lane = lax.broadcasted_iota(jnp.int32, (1, 128), 1)

    @pl.when(pair == 0)
    def _():
        hot = one_hot_docs(lengths_ref, docs, length)
        marks = lane < docs + 1
        aug_q[...] = jnp.where(hot & marks, 1.0, 0.0).astype(bf16)
        aug_k[...] = key_marks(hot, lane)
        lse_ref[...] = jnp.zeros_like(lse_ref)

    kk[:, :128] = k_ref[...]
    kk[:, 128:] = aug_k[...]
    scale = 1.0 / math.sqrt(dim)
    first = lane < dim
    jobs = [(b, h) for b in range(length // block) for h in range(2)]

    def score(k):
        b, h = jobs[k]
        rows = pl.ds(b * block, block)
        mine = first if h == 0 else jnp.logical_not(first)
        qq = jnp.concatenate([jnp.where(mine, q_ref[rows, :].astype(f32) * scale, 0.0).astype(bf16), aug_q[rows, :]], axis=1)
        s_refs[k % 2][:, :(b + 1) * block] = lax.dot_general(qq, kk[:(b + 1) * block, :], NT, preferred_element_type=f32)

    def soften(k):
        b, h = jobs[k]
        s_ref, e_ref, many = s_refs[k % 2], e_refs[k % 2], (b + 1) * block
        for r in range(0, block, strip):
            mine = pl.ds(r, strip)
            row = lax.broadcasted_iota(jnp.int32, (strip, block), 0) + r
            col = lax.broadcasted_iota(jnp.int32, (strip, block), 1)
            s = jnp.where(row >= col, s_ref[mine, b * block:many], NEG)
            if b > 0:
                s = jnp.concatenate([s_ref[mine, :b * block], s], axis=1)
            top = jnp.max(s, axis=1, keepdims=True)
            e = jnp.exp(s - top)
            total = jnp.sum(e, axis=1, keepdims=True)
            e_ref[mine, :many] = e.astype(bf16)
            scales[k % 2, mine, :] = jnp.broadcast_to(1.0 / total, (strip, 128))
            at = pl.ds(b * block + r, strip)
            lse_ref[at, :] = jnp.where(lane == 2 * pair + h, top + jnp.log(total), lse_ref[at, :])

    def mix(k):
        b, h = jobs[k]
        many = (b + 1) * block
        o = lax.dot_general(e_refs[k % 2][:, :many], v_ref[:many, :], NN, preferred_element_type=f32) * scales[k % 2]
        rows = pl.ds(b * block, block)
        if h == 0:
            held[...] = o
        else:
            mixed_ref[rows, :] = jnp.where(first, held[...], o).astype(bf16)

    score(0)
    for k in range(len(jobs)):
        if k + 1 < len(jobs):
            score(k + 1)
        soften(k)
        mix(k)

def attn_fwd(lengths, projected, *, dim=64, block=256, strip=32):
    length, width3 = projected.shape
    width = width3 // 3
    docs = lengths.shape[1]
    pairs = width // 128
    col = lambda off: pl.BlockSpec((length, 128), lambda p: (0, p + off))
    return pl.pallas_call(
        functools.partial(attn_fwd_kernel, docs=docs, dim=dim, block=block, strip=strip),
        grid=(pairs,),
        in_specs=[pl.BlockSpec(memory_space=pltpu.SMEM), col(0), col(pairs), col(2 * pairs)],
        out_specs=[col(0), pl.BlockSpec((length, 128), lambda p: (0, 0))],
        out_shape=[jax.ShapeDtypeStruct((length, width), bf16), jax.ShapeDtypeStruct((length, 128), f32)],
        scratch_shapes=[pltpu.VMEM((length, 128), bf16), pltpu.VMEM((length, 128), bf16), pltpu.VMEM((length, 256), bf16),
                        pltpu.VMEM((block, length), f32), pltpu.VMEM((block, length), f32),
                        pltpu.VMEM((block, length), bf16), pltpu.VMEM((block, length), bf16),
                        pltpu.VMEM((2, block, 128), f32), pltpu.VMEM((block, 128), f32)],
        compiler_params=pltpu.CompilerParams(vmem_limit_bytes=LIMIT),
        cost_estimate=spend(12),
        name="attend",
    )(lengths, projected, projected, projected)

def attn_bwd_kernel(lengths_ref, q_ref, k_ref, v_ref, mixed_ref, gmix_ref, lse_ref, dq_ref, dk_ref, dv_ref,
                    aug_q, aug_k, kk, vv, qq, gg, kt, dqt, dk_acc, dv_acc, s_0, s_1, d_0, d_1, p_0, p_1, c_0, c_1,
                    *, docs, dim, block, first, strip):
    s_refs, d_refs, p_refs, c_refs = (s_0, s_1), (d_0, d_1), (p_0, p_1), (c_0, c_1)
    step = pl.program_id(0)
    pair = step + first
    length = q_ref.shape[0]
    blocks = length // block
    lane = lax.broadcasted_iota(jnp.int32, (1, 128), 1)

    @pl.when(step == 0)
    def _():
        hot = one_hot_docs(lengths_ref, docs, length)
        marks = lane < docs + 1
        aug_q[...] = jnp.where(hot & marks, 1.0, 0.0).astype(bf16)
        aug_k[...] = key_marks(hot, lane)

    kk[:, :128] = k_ref[...]
    kk[:, 128:] = aug_k[...]
    vv[:, :128] = v_ref[...]
    vv[:, 128:] = aug_k[...]
    kt[...] = jnp.transpose(k_ref[...])
    scale = 1.0 / math.sqrt(dim)
    low = lane < dim
    q2 = q_ref[...].astype(f32) * scale
    g2 = gmix_ref[...].astype(f32)
    dots = g2 * mixed_ref[...].astype(f32)
    lse_all = lse_ref[...]
    marks_q = aug_q[...].astype(f32)
    for h in range(2):
        mine = low if h == 0 else jnp.logical_not(low)
        lse = jnp.sum(jnp.where(lane == 2 * pair + h, lse_all, 0.0), axis=1, keepdims=True)
        qq[h, :, :128] = jnp.where(mine, q2, 0.0).astype(bf16)
        qq[h, :, 128:] = with_stat(marks_q, -lse, lane)
        delta = jnp.sum(jnp.where(mine, dots, 0.0), axis=1, keepdims=True)
        gg[h, :, :128] = jnp.where(mine, g2, 0.0).astype(bf16)
        gg[h, :, 128:] = with_stat(jnp.zeros_like(marks_q), -delta, lane)
    jobs = [(h, kb, qb) for kb in range(blocks) for h in range(2) for qb in range(kb, blocks)]

    def score(k):
        h, kb, qb = jobs[k]
        keys, queries = pl.ds(kb * block, block), pl.ds(qb * block, block)
        s_refs[k % 2][...] = lax.dot_general(kk[keys, :], qq[h, queries, :], NT, preferred_element_type=f32)
        d_refs[k % 2][...] = lax.dot_general(vv[keys, :], gg[h, queries, :], NT, preferred_element_type=f32)

    def bend(k):
        h, kb, qb = jobs[k]
        for r in range(0, block, strip):
            mine = pl.ds(r, strip)
            s = s_refs[k % 2][mine, :]
            if qb == kb:
                krow = lax.broadcasted_iota(jnp.int32, (strip, block), 0) + r
                qcol = lax.broadcasted_iota(jnp.int32, (strip, block), 1)
                s = jnp.where(qcol >= krow, s, NEG)
            p = jnp.exp(s)
            p_refs[k % 2][mine, :] = p.astype(bf16)
            c_refs[k % 2][mine, :] = (p * d_refs[k % 2][mine, :]).astype(bf16)

    def pull(k):
        h, kb, qb = jobs[k]
        keys, queries = pl.ds(kb * block, block), pl.ds(qb * block, block)
        p, ds = p_refs[k % 2][...], c_refs[k % 2][...]
        dv = lax.dot_general(p, gg[h, queries, :128], NN, preferred_element_type=f32)
        dk = lax.dot_general(ds, qq[h, queries, :128], NN, preferred_element_type=f32)
        dq = lax.dot_general(kt[h * dim:(h + 1) * dim, keys], ds, NN, preferred_element_type=f32)
        if h == 0 and qb == kb:
            dk_acc[keys, :] = dk
            dv_acc[keys, :] = dv
        else:
            dk_acc[keys, :] += dk
            dv_acc[keys, :] += dv
        if kb == 0:
            dqt[h * dim:(h + 1) * dim, queries] = dq
        else:
            dqt[h * dim:(h + 1) * dim, queries] += dq

    score(0)
    for k in range(len(jobs)):
        if k + 1 < len(jobs):
            score(k + 1)
        bend(k)
        pull(k)
    dk_ref[...] = dk_acc[...].astype(bf16)
    dv_ref[...] = dv_acc[...].astype(bf16)
    dq_ref[...] = (jnp.transpose(dqt[...]) * scale).astype(bf16)

def attn_bwd(lengths, projected, mixed, gmix, lse, *, first=0, count=4, dim=64, block=256, strip=32, us=25):
    length, width3 = projected.shape
    width = width3 // 3
    docs = lengths.shape[1]
    pairs = width // 128
    col = lambda off: pl.BlockSpec((length, 128), lambda p: (0, p + off))
    here = pl.BlockSpec((length, 128), lambda p: (0, p))
    one = jax.ShapeDtypeStruct((length, 128 * count), bf16)
    return pl.pallas_call(
        functools.partial(attn_bwd_kernel, docs=docs, dim=dim, block=block, first=first, strip=strip),
        grid=(count,),
        in_specs=[pl.BlockSpec(memory_space=pltpu.SMEM), col(first), col(first + pairs), col(first + 2 * pairs), col(first), col(first),
                  pl.BlockSpec((length, 128), lambda p: (0, 0))],
        out_specs=[here, here, here],
        out_shape=[one, one, one],
        scratch_shapes=[pltpu.VMEM((length, 128), bf16), pltpu.VMEM((length, 128), bf16),
                        pltpu.VMEM((length, 256), bf16), pltpu.VMEM((length, 256), bf16),
                        pltpu.VMEM((2, length, 256), bf16), pltpu.VMEM((2, length, 256), bf16),
                        pltpu.VMEM((128, length), bf16), pltpu.VMEM((128, length), f32),
                        pltpu.VMEM((length, 128), f32), pltpu.VMEM((length, 128), f32)]
        + [pltpu.VMEM((block, block), f32)] * 4 + [pltpu.VMEM((block, block), bf16)] * 4,
        compiler_params=pltpu.CompilerParams(vmem_limit_bytes=LIMIT),
        cost_estimate=spend(us),
        name="attend_back",
    )(lengths, projected, projected, projected, mixed, gmix, lse)


def place_tables(length, width):
    freq = np.exp(np.arange(width // 2, dtype=np.float64) * (-2.0 * math.log(10000.0) / width))
    angles = np.arange(length, dtype=np.float64)[:, None] * freq[None, :]
    return (np.concatenate([np.sin(angles), np.cos(angles)], axis=1).astype(np.float32),
            freq.astype(np.float32)[None, :])

def norm_stats(v):
    center = v - jnp.mean(v, axis=1, keepdims=True)
    inv = lax.rsqrt(jnp.mean(center * center, axis=1, keepdims=True) + 1e-5)
    return center * inv, inv

def front_kernel(lengths_ref, x_ref, table_ref, freq_ref, gain_ref, bias_ref, w_ref,
                 stream_ref, proj_ref, starts, turned, normed, *, docs):
    step = pl.program_id(0)
    rows, width = x_ref.shape
    half = width // 2
    begin, end, _ = doc_bounds(lengths_ref, docs)

    @pl.when(step == 0)
    def _():
        some = -(-(docs + 1) // 16) * 16
        at = jnp.transpose(jnp.broadcast_to(begin.astype(f32), (128, 128)))[:some, :1]
        angle = at * freq_ref[...]
        both = jnp.concatenate([jnp.sin(angle), jnp.cos(angle)], axis=1)
        hi = both.astype(bf16)
        mid = (both - hi.astype(f32)).astype(bf16)
        low = (both - hi.astype(f32) - mid.astype(f32)).astype(bf16)
        starts[...] = jnp.zeros_like(starts)
        for k, part in enumerate((hi, mid, low)):
            starts[k * 128:k * 128 + some, :] = part

    place = step * rows + lax.broadcasted_iota(jnp.int32, (rows, 128), 0)
    hot = jnp.where((place >= begin) & (place < end), 1.0, 0.0).astype(bf16)
    start = lax.dot_general(jnp.concatenate([hot, hot, hot], axis=1), starts[...], NN, preferred_element_type=f32)
    turned[...] = start
    for r in range(0, rows, 32):
        mine = pl.ds(r, 32)
        sin_b, cos_b = turned[mine, :half], turned[mine, half:]
        sin_t, cos_t = table_ref[mine, :half], table_ref[mine, half:]
        x = x_ref[mine, :].astype(f32)
        stream = jnp.concatenate([x[:, :half] + (sin_t * cos_b - cos_t * sin_b),
                                  x[:, half:] + (cos_t * cos_b + sin_t * sin_b)], axis=1)
        stream_ref[mine, :] = stream
        unit, _ = norm_stats(stream)
        normed[mine, :] = (unit * gain_ref[...] + bias_ref[...]).astype(bf16)
    proj_ref[...] = lax.dot_general(normed[...], w_ref[...], NN, preferred_element_type=f32).astype(bf16)

def front(lengths, x, gain, bias, w, *, rows=256):
    length, width = x.shape
    table, freq = place_tables(length, width)
    docs = lengths.shape[1]
    blk = pl.BlockSpec((rows, width), lambda i: (i, 0))
    whole = lambda a: pl.BlockSpec(a.shape, lambda i: (0,) * a.ndim)
    return pl.pallas_call(
        functools.partial(front_kernel, docs=docs),
        grid=(length // rows,),
        in_specs=[pl.BlockSpec(memory_space=pltpu.SMEM), blk, blk, whole(freq), whole(gain), whole(bias), whole(w)],
        out_specs=[blk, pl.BlockSpec((rows, w.shape[1]), lambda i: (i, 0))],
        out_shape=[jax.ShapeDtypeStruct((length, width), f32),
                   jax.ShapeDtypeStruct((length, w.shape[1]), bf16)],
        scratch_shapes=[pltpu.VMEM((384, width), bf16), pltpu.VMEM((rows, width), f32), pltpu.VMEM((rows, width), bf16)],
        compiler_params=pltpu.CompilerParams(vmem_limit_bytes=LIMIT),
        cost_estimate=spend(6),
        name="front",
    )(lengths, x, table, freq, gain, bias, w)

ERF = tuple(0.5 * v for v in (0.254829592, -0.284496736, 1.421413741, -1.453152027, 1.061405429))
ERF_P = 0.3275911

def gelu_both(h):
    bell = jnp.exp2(h * h * (-0.5 * LOG2E))
    d = 1.0 + jnp.abs(h) * (ERF_P / math.sqrt(2.0))
    t = pl.reciprocal(d, approx=True)
    t = t * (2.0 - d * t)
    poly = t * (ERF[0] + t * (ERF[1] + t * (ERF[2] + t * (ERF[3] + t * ERF[4]))))
    tail = poly * bell
    phi = jnp.where(h < 0.0, tail, 1.0 - tail)
    return h * phi, phi + h * bell * (1.0 / math.sqrt(2.0 * math.pi))

def ffn_kernel(stream_ref, mixed_ref, w_out_ref, b_out_ref, gain_ref, bias_ref, w_up_ref, b_up_ref, w_down_ref, b_down_ref,
               after_ref, normed_ref, act_ref, slope_ref, out_ref, h_0, h_1, *, chunk):
    rows = stream_ref.shape[0]
    wide = w_up_ref.shape[1]
    after_ref[...] = lax.dot_general(mixed_ref[...], w_out_ref[...], NN, preferred_element_type=f32)
    for r in range(0, rows, 32):
        mine = pl.ds(r, 32)
        after = stream_ref[mine, :] + after_ref[mine, :] + b_out_ref[...]
        after_ref[mine, :] = after
        unit, _ = norm_stats(after)
        normed_ref[mine, :] = (unit * gain_ref[...] + bias_ref[...]).astype(bf16)
    hs = (h_0, h_1)

    def up(c):
        hs[c % 2][...] = lax.dot_general(normed_ref[...], w_up_ref[:, c * chunk:(c + 1) * chunk], NN, preferred_element_type=f32)

    def bend(c):
        for r in range(0, rows, 32):
            for k in range(0, chunk, 256):
                mine, cols = pl.ds(r, 32), pl.ds(c * chunk + k, 256)
                act, slope = gelu_both(hs[c % 2][mine, k:k + 256] + b_up_ref[:, cols])
                act_ref[mine, cols] = act.astype(bf16)
                slope_ref[mine, cols] = slope.astype(bf16)

    up(0)
    for c in range(wide // chunk):
        if c + 1 < wide // chunk:
            up(c + 1)
        bend(c)
    out = lax.dot_general(act_ref[...], w_down_ref[...], NN, preferred_element_type=f32)
    out_ref[...] = (out + after_ref[...] + b_down_ref[...]).astype(bf16)

def ffn(stream, mixed, w_out, b_out, gain, bias, w_up, b_up, w_down, b_down, *, rows=256, chunk=512):
    length, width = stream.shape
    wide = w_up.shape[1]
    blk = pl.BlockSpec((rows, width), lambda i: (i, 0))
    big = pl.BlockSpec((rows, wide), lambda i: (i, 0))
    whole = lambda a: pl.BlockSpec(a.shape, lambda i: (0,) * a.ndim)
    args = (w_out, b_out, gain, bias, w_up, b_up, w_down, b_down)
    return pl.pallas_call(
        functools.partial(ffn_kernel, chunk=chunk),
        grid=(length // rows,),
        in_specs=[blk, blk] + [whole(a) for a in args],
        out_specs=[blk, blk, big, big, blk],
        out_shape=[jax.ShapeDtypeStruct((length, width), f32), jax.ShapeDtypeStruct((length, width), bf16),
                   jax.ShapeDtypeStruct((length, wide), bf16), jax.ShapeDtypeStruct((length, wide), bf16),
                   jax.ShapeDtypeStruct((length, width), bf16)],
        scratch_shapes=[pltpu.VMEM((rows, chunk), f32), pltpu.VMEM((rows, chunk), f32)],
        compiler_params=pltpu.CompilerParams(vmem_limit_bytes=LIMIT),
        cost_estimate=spend(16),
        name="ffn",
    )(stream, mixed, *args)

def norm_back(g, gain, unit, inv):
    gu = g * gain
    return inv * (gu - jnp.mean(gu, axis=1, keepdims=True) - unit * jnp.mean(gu * unit, axis=1, keepdims=True))

def colsum(x):
    return jnp.sum(x, axis=0, keepdims=True)


def arrange(dst, t, me_ref, ab):
    row8 = t.shape[0] // 8
    for a in range(8):
        r = lax.bitwise_xor(jnp.int32(a), me_ref[0] * 4 + me_ref[1 + ab])
        dst[pl.ds(pl.multiple_of(r * row8, row8), row8), :] = t[a * row8:(a + 1) * row8, :]

def ffn_back_kernel(me_ref, g_ref, act_ref, slope_ref, w_down_ref, w_up_ref, normed_ref, after_ref, gain_ref, mixed_ref, w_out_ref,
                    bdown_ref, send_ref, keep_ref, gafter_ref, gmix_ref, g_low, g_t, norm_t, gh_ref, bup, small):
    i = pl.program_id(0)
    steps = pl.num_programs(0)
    width = g_ref.shape[1]
    tile = slope_ref.shape[1]
    wide = steps * tile
    half = width // 2

    @pl.when(i == 0)
    def _():
        low = g_ref[...].astype(bf16)
        g_low[...] = low
        arrange(g_t, jnp.transpose(low), me_ref, 0)
        arrange(norm_t, jnp.transpose(normed_ref[...]), me_ref, 1)

    def put(at, grad, size):
        cols = pl.ds(pl.multiple_of(at, 128), size)
        keep_ref[:, cols] = grad[:half, :]
        send_ref[:, cols] = grad[half:, :]

    gh = lax.dot_general(g_low[...], w_down_ref[...], NT, preferred_element_type=f32) * slope_ref[...].astype(f32)
    bup[pl.ds(i, 1), :] = colsum(gh)
    gh = gh.astype(bf16)
    gh_ref[:, pl.ds(pl.multiple_of(i * tile, tile), tile)] = gh
    put(i * tile, lax.dot_general(g_t[...], act_ref[...], NN, preferred_element_type=f32).astype(bf16), tile)
    put(i * tile + wide + width, lax.dot_general(norm_t[...], gh, NN, preferred_element_type=f32).astype(bf16), tile)

    @pl.when(i == steps - 1)
    def _():
        gafter_ref[...] = lax.dot_general(gh_ref[...], w_up_ref[...], NT, preferred_element_type=f32)
        fold = lambda x: x[0:8] + x[8:16] + x[16:24] + x[24:32]
        sums = [jnp.zeros((8, width), f32)] * 3
        for r in range(0, g_ref.shape[0], 32):
            mine = pl.ds(r, 32)
            unit, inv = norm_stats(after_ref[mine, :])
            gn = gafter_ref[mine, :]
            ga = g_ref[mine, :] + norm_back(gn, gain_ref[...], unit, inv)
            gafter_ref[mine, :] = ga
            g_low[mine, :] = ga.astype(bf16)
            sums = [s + fold(x) for s, x in zip(sums, (gn * unit, gn, ga))]
        gmix_ref[...] = lax.dot_general(g_low[...], w_out_ref[...], NT, preferred_element_type=f32).astype(bf16)
        arrange(g_t, jnp.transpose(mixed_ref[...]), me_ref, 0)
        put(wide, lax.dot_general(g_t[...], g_low[...], NN, preferred_element_type=f32).astype(bf16), width)
        small[...] = jnp.zeros_like(small)
        small[0:1, :] = bdown_ref[...]
        for k in range(3):
            small[1 + k:2 + k, :] = colsum(sums[k])
        per = width // tile if tile < width else 1
        for k in range(wide // width):
            if tile >= width:
                many = tile // width
                small[4 + k:5 + k, :] = bup[k // many:k // many + 1, (k % many) * width:(k % many + 1) * width]
            else:
                for m in range(per):
                    small[4 + k:5 + k, m * tile:(m + 1) * tile] = bup[k * per + m:k * per + m + 1, :]
        arrange(norm_t.at[:, :128], jnp.transpose(small[...]).astype(bf16), me_ref, 1)
        put(2 * wide + width, norm_t[:, :128], 128)

def ffn_back(me, g, act, slope, w_down, w_up, normed, after, gain, mixed, w_out, bdown, *, tile=512):
    length, width = g.shape
    wide = slope.shape[1]
    steps = wide // tile
    whole = lambda a: pl.BlockSpec(a.shape, lambda i, m: (0,) * a.ndim)
    full = lambda s: pl.BlockSpec(s, lambda i, m: (0,) * len(s))
    sums = (width // 2, 2 * wide + width + 128)
    return pl.pallas_call(
        ffn_back_kernel,
        grid_spec=pltpu.PrefetchScalarGridSpec(
            num_scalar_prefetch=1, grid=(steps,),
            in_specs=[whole(g), pl.BlockSpec((length, tile), lambda i, m: (0, i)), pl.BlockSpec((length, tile), lambda i, m: (0, i)),
                      pl.BlockSpec((tile, width), lambda i, m: (i, 0)),
                      whole(w_up), whole(normed), whole(after), whole(gain), whole(mixed), whole(w_out), whole(bdown)],
            out_specs=[full(sums), full(sums), full((length, width)), full((length, width))],
            scratch_shapes=[pltpu.VMEM((length, width), bf16), pltpu.VMEM((width, length), bf16), pltpu.VMEM((width, length), bf16),
                            pltpu.VMEM((length, wide), bf16), pltpu.VMEM((steps, tile), f32), pltpu.VMEM((128, width), f32)]),
        out_shape=[jax.ShapeDtypeStruct(sums, bf16)] * 2
        + [jax.ShapeDtypeStruct((length, width), f32), jax.ShapeDtypeStruct((length, width), bf16)],
        compiler_params=pltpu.CompilerParams(vmem_limit_bytes=LIMIT),
        cost_estimate=spend(20),
        name="ffn_back",
    )(me, g, act, slope, w_down, w_up, normed, after, gain, mixed, w_out, bdown)

def window(refs, start, size):
    found, at = [], 0
    for ref in refs:
        low, high = max(start, at), min(start + size, at + ref.shape[1])
        if low < high:
            found.append(ref[:, low - at:high - at])
        at += ref.shape[1]
    return found[0] if len(found) == 1 else jnp.concatenate(found, axis=1)

def qkv_grad_kernel(me_ref, *refs, parts):
    gps, (stream_ref, gain_ref, bias_ref, w_ref, send_ref, keep_ref, unit_t, rows_t, unit_ref) = refs[:parts], refs[parts:]
    length, width = stream_ref.shape
    half = width // 2
    for r in range(0, length, 32):
        unit, _ = norm_stats(stream_ref[pl.ds(r, 32), :])
        unit_ref[pl.ds(r, 32), :] = unit.astype(bf16)
    t = jnp.transpose(unit_ref[...])
    column_of = lambda row: jnp.transpose(jnp.broadcast_to(row, (128, width)))
    gain, bias = column_of(gain_ref[...]), column_of(bias_ref[...])
    for ab in range(2):
        arrange(unit_t.at[ab], t, me_ref, ab)
    gains, biases, ws = [], [], []
    for ab in range(2):
        arrange(rows_t, gain, me_ref, ab)
        gains.append(rows_t[:, :1])
        arrange(rows_t, bias, me_ref, ab)
        biases.append(rows_t[:, :1])
    total = 3 * width
    cut = total // 2
    gain_grad = [jnp.zeros((width, 128), f32), jnp.zeros((width, 128), f32)]
    bias_grad = [jnp.zeros((width, 128), f32), jnp.zeros((width, 128), f32)]
    for at in range(0, total, 256):
        ab = 0 if at < cut else 1
        gp = window(gps, at, 256)
        m = lax.dot_general(unit_t[ab], gp, NN, preferred_element_type=f32)
        s = colsum(gp.astype(f32))
        grad = (m * gains[ab] + biases[ab] * s).astype(bf16)
        keep_ref[:, at:at + 256] = grad[:half, :]
        send_ref[:, at:at + 256] = grad[half:, :]
        arrange_w = []
        row8 = width // 8
        for r in range(8):
            a = lax.bitwise_xor(jnp.int32(r), me_ref[0] * 4 + me_ref[1 + ab])
            arrange_w.append(w_ref[pl.ds(pl.multiple_of(a * row8, row8), row8), at:at + 256])
        w = jnp.concatenate(arrange_w, axis=0).astype(f32)
        mw, ws = m * w, w * s
        gain_grad[ab] = gain_grad[ab] + mw[:, :128] + mw[:, 128:]
        bias_grad[ab] = bias_grad[ab] + ws[:, :128] + ws[:, 128:]
    row8 = width // 8
    lane = lax.broadcasted_iota(jnp.int32, (1, 128), 1)
    over = lambda v: jnp.sum(v, axis=1, keepdims=True)
    both = [jnp.where(lane == 0, over(gain_grad[ab]), jnp.where(lane == 1, over(bias_grad[ab]), 0.0)) for ab in range(2)]
    for r in range(8):
        to = lax.bitwise_xor(jnp.int32(r), lax.bitwise_xor(me_ref[1], me_ref[2]))
        rows_t[pl.ds(pl.multiple_of(to * row8, row8), row8), :] = both[0][r * row8:(r + 1) * row8, :]
    small = (rows_t[...] + both[1]).astype(bf16)
    keep_ref[:, total:] = small[:half, :]
    send_ref[:, total:] = small[half:, :]

def qkv_grad(me, gps, stream, gain, bias, w):
    length, width = stream.shape
    vm = pl.BlockSpec(memory_space=pltpu.VMEM)
    parts = len(gps)
    return pl.pallas_call(
        functools.partial(qkv_grad_kernel, parts=parts),
        in_specs=[pl.BlockSpec(memory_space=pltpu.SMEM)] + [vm] * (parts + 4),
        out_specs=[vm, vm],
        out_shape=[jax.ShapeDtypeStruct((width // 2, 3 * width + 128), bf16)] * 2,
        scratch_shapes=[pltpu.VMEM((2, width, length), bf16), pltpu.VMEM((width, 128), f32),
                        pltpu.VMEM((length, width), bf16)],
        compiler_params=pltpu.CompilerParams(vmem_limit_bytes=LIMIT),
        cost_estimate=spend(0.2),
        name="qkv_grad",
    )(me, *gps, stream, gain, bias, w)

def front_back_kernel(*refs, parts):
    gps, (w_ref, stream_ref, gafter_ref, gain_ref, out_ref, gn_ref) = refs[:parts], refs[parts:]
    gp = window(gps, 0, w_ref.shape[1])
    gn_ref[...] = lax.dot_general(gp, w_ref[...], NT, preferred_element_type=f32)
    for r in range(0, gn_ref.shape[0], 32):
        mine = pl.ds(r, 32)
        unit, inv = norm_stats(stream_ref[mine, :])
        out_ref[mine, :] = (gafter_ref[mine, :] + norm_back(gn_ref[mine, :], gain_ref[...], unit, inv)).astype(bf16)

def front_back(gps, w, stream, gafter, gain, *, rows=256):
    length, width = stream.shape
    blk = pl.BlockSpec((rows, width), lambda i: (i, 0))
    whole = lambda a: pl.BlockSpec(a.shape, lambda i: (0,) * a.ndim)
    return pl.pallas_call(
        functools.partial(front_back_kernel, parts=len(gps)),
        grid=(length // rows,),
        in_specs=[pl.BlockSpec((rows, gp.shape[1]), lambda i: (i, 0)) for gp in gps] + [whole(w), blk, blk, whole(gain)],
        out_specs=blk,
        out_shape=jax.ShapeDtypeStruct((length, width), bf16),
        scratch_shapes=[pltpu.VMEM((rows, width), f32)],
        compiler_params=pltpu.CompilerParams(vmem_limit_bytes=LIMIT),
        cost_estimate=spend(0.2),
        name="front_back",
    )(*gps, w, stream, gafter, gain)


def finish_kernel(me_ref, own_a, own_b, got_a, got_b, *refs, plan, n):
    outs, whole = refs[:-1], refs[-1]
    rows, cut = own_a.shape
    chunk = rows // (4 * n)

    def lay(dst, at, size):
        ab = 0 if at < cut else 1
        at -= ab * cut
        for near, ref in ((0, (own_a, own_b)[ab]), (1, (got_a, got_b)[ab])):
            core = lax.bitwise_xor(jnp.int32(near), me_ref[0])
            for pq in range(4):
                for z in range(n):
                    to = core * 4 + lax.bitwise_xor(jnp.int32(pq), me_ref[1 + ab])
                    to = to * n + lax.bitwise_xor(jnp.int32(z), me_ref[3])
                    r = (pq * n + z) * chunk
                    dst[pl.ds(pl.multiple_of(to * chunk, chunk), chunk), :] = ref[r:r + chunk, at:at + size].astype(f32)

    for at, size, out, col, turned in plan:
        if out < 0:
            lay(whole.at[:, :size], at, size)
            flat = jnp.transpose(whole[:, :size])
            done = 0
            for v in outs[out:]:
                width = flat.shape[1]
                for k in range(v.shape[1] // width):
                    v[:, k * width:(k + 1) * width] = flat[done:done + 1, :]
                    done += 1
        elif not turned:
            lay(outs[out].at[:, col:col + size], at, size)
        else:
            lay(whole.at[:, :size], at, size)
            flat = jnp.transpose(whole[:, :size])
            outs[out][col:col + size, :] = flat[:outs[out].shape[0] - col, :]

def finish(me, pieces, shapes, plan, *, n, us):
    rows = pieces[0].shape[0]
    room = 8 * 2 ** 20 + sum(p.size * 2 for p in pieces) + sum(4 * a * b for a, b in shapes)
    vm = pl.BlockSpec(memory_space=pltpu.VMEM)
    return pl.pallas_call(
        functools.partial(finish_kernel, plan=plan, n=n),
        in_specs=[pl.BlockSpec(memory_space=pltpu.SMEM)] + [vm] * 4,
        out_specs=[vm] * len(shapes),
        out_shape=[jax.ShapeDtypeStruct(s, f32) for s in shapes],
        scratch_shapes=[pltpu.VMEM((2 * rows, 256), f32)],
        compiler_params=pltpu.CompilerParams(vmem_limit_bytes=room),
        cost_estimate=spend(us),
        name="finish",
    )(me, *pieces)

class Links:
    def __init__(self, mesh):
        self.sizes = dict(mesh.shape)
        self.n = self.sizes["rows"] // 2
        self.fine = self.n == 4
        self.zi = lax.axis_index("rows") // 2

    def swap(self, x, axis, bit):
        return lax.ppermute(x, axis, [(a, a ^ bit) for a in range(self.sizes[axis])])

    def core(self, x):
        return self.swap(x, "bank", 1)

    def near(self, x):
        return self.swap(x, "bank", 2)

    def side(self, x):
        return self.swap(x, "rows", 1)

def plus(*terms):
    out = terms[0].astype(f32)
    for t in terms[1:]:
        out = out + t.astype(f32)
    return out.astype(bf16)

def stacked(pieces):
    rows = sum(p.shape[0] for p in pieces)
    out, at = None, 0
    for p in pieces:
        term = lax.pad(p, jnp.zeros((), p.dtype), [(at, rows - at - p.shape[0], 0), (0, 0, 0)])
        out = term if out is None else out + term
        at += p.shape[0]
    return out

def chain(links, send, keep, cut):
    n = links.n
    got, = yield [(links.core, send)]
    half = keep.shape[0] // 2
    sa, sb = plus(keep[half:, :cut], got[half:, :cut]), plus(keep[half:, cut:], got[half:, cut:])
    a, b = plus(keep[:half, :cut], got[:half, :cut]), plus(keep[:half, cut:], got[:half, cut:])
    ra, rb = yield [(links.near, sa), (links.side, sb)]
    half //= 2
    sa, sb = plus(a[half:], ra[half:]), plus(b[half:], rb[half:])
    a, b = plus(a[:half], ra[:half]), plus(b[:half], rb[:half])
    ra, rb = yield [(links.side, sa), (links.near, sb)]
    z = jnp.concatenate([plus(a, ra), plus(b, rb)], axis=1)
    chunk = half // n
    if links.fine:
        piece = lambda k: lax.dynamic_slice(z, ((links.zi ^ k) * chunk, 0), (chunk, z.shape[1]))
        hops = [functools.partial(links.swap, axis="rows", bit=2 * k) for k in range(1, n)]
        got = yield [(hop, piece(k + 1)) for k, hop in enumerate(hops)]
        mine = plus(piece(0), *got)
        got = yield [(hop, mine) for hop in hops]
        a = stacked([v[:, :cut] for v in (mine, *got)])
        b = stacked([v[:, cut:] for v in (mine, *got)])
    else:
        groups = [[r for r in range(2 * n) if r % 2 == y] for y in range(2)]
        z, = yield [(lambda v: lax.psum(v, "rows", axis_index_groups=groups), z)]
        yield []
        a, b = z[:, :cut], z[:, cut:]
    ra, rb = yield [(links.side, a), (links.near, b)]
    a, b = stacked([a, ra]), stacked([b, rb])
    ra, rb = yield [(links.near, a), (links.side, b)]
    a, b = stacked([a, ra]), stacked([b, rb])
    ga, gb = yield [(links.core, a), (links.core, b)]
    yield (a, b, ga, gb)

class Step:
    def __init__(self, *args):
        self.run = chain(*args)
        self.sends = next(self.run)

    def go(self):
        self.got = [how(what) for how, what in self.sends]

    def take(self):
        self.sends = self.run.send(self.got)

def tie(steps, *extra):
    flat = [what for s in steps for _, what in s.sends] + list(extra)
    flat = list(lax.optimization_barrier(tuple(flat)))
    for s in steps:
        s.sends = [(how, flat.pop(0)) for how, _ in s.sends]
    return flat

def tiles_of(start, width, out, turned):
    plan, at = [], 0
    while at < width:
        size = min(256, width - at)
        plan.append((start + at, size, out, at, turned))
        at += size
    return plan

def body(mesh, hidden_in, lengths, ln1_gain, ln1_bias, w_qkv, w_out, b_out, ln2_gain, ln2_bias, w_up, b_up, w_down, b_down,
         bank, bank_labels, target_slots, gold_ids):
    links = Links(mesh)
    row = lambda v: v.reshape(1, -1)
    width = hidden_in.shape[1]
    wide = w_up.shape[1]
    ib, ir = lax.axis_index("bank"), lax.axis_index("rows")
    core, x, y = ib % 2, ib // 2, ir % 2
    me = jnp.stack([core, x * 2 + y, y * 2 + x, links.zi if links.fine else 0, ib]).astype(jnp.int32)
    own = with_labels(bank, bank_labels)
    other = links.core(own)
    near = links.near(own)
    stream, projected = front(lengths, hidden_in, row(ln1_gain), row(ln1_bias), w_qkv)
    mixed, lse = attn_fwd(lengths, projected)
    after, normed_c, act, slope, block_out = ffn(stream, mixed, w_out, row(b_out), row(ln2_gain), row(ln2_bias), w_up, row(b_up),
                                                 w_down, row(b_down), chunk=256)
    e, hist, sums = bank_first(me, block_out, gold_ids, target_slots, own, other)
    near, e = lax.optimization_barrier((near, e))
    far = links.core(near)
    g, loss, bdown = bank_last(me, lengths, block_out, gold_ids, target_slots, e, hist, sums, own, other, near, far)
    send, keep, gafter, gmix = ffn_back(me, g, act, slope, w_down, w_up, normed_c, after, row(ln2_gain), mixed, w_out, bdown)
    cut = wide + width
    n = links.n if links.fine else 1
    one = Step(links, send, keep, cut)
    one.go()
    parts = []
    back = lambda first, count: parts.append(attn_bwd(lengths, projected, mixed, gmix, lse, first=first, count=count, us=0.2 * count))
    for first, count in ((0, 1), (1, 2), (3, 1)):
        back(first, count)
        one.take()
        gmix, *parts[-1] = tie([one], gmix, *parts[-1])
        one.go()
    gps = [p[k] for k in range(3) for p in parts]
    send, keep = qkv_grad(me, gps, stream, row(ln1_gain), row(ln1_bias), w_qkv)
    cut2 = 3 * width // 2
    two = Step(links, send, keep, cut2)
    two.go()
    one.take()
    two.take()
    tie([one, two])
    one.go()
    two.go()
    two.take()
    tie([two])
    two.go()
    one.take()
    two.take()
    tie([one, two])
    one.go()
    two.go()
    one.take()
    two.take()
    gafter, = tie([one, two], gafter)
    one.go()
    two.go()
    input_grad = front_back(gps, w_qkv, stream, gafter, row(ln1_gain))
    one.take()
    two.take()
    input_grad, = tie([one, two], input_grad)
    one.go()
    two.go()
    one.take()
    vector = (1, width)
    two.take()
    pieces = tie([two], *one.sends)
    two.go()
    w_down_grad, w_out_grad, w_up_grad, *small = finish(
        me, pieces, [(wide, width), (width, width), (width, wide)] + [vector] * 4 + [(1, wide)],
        tiles_of(0, wide, 0, True) + tiles_of(wide, width, 1, False) + tiles_of(cut, wide, 2, False) + tiles_of(cut + wide, 128, -5, True),
        n=n, us=0.2)
    two.take()
    w_down_grad, = tie([two], w_down_grad)
    two.go()
    two.take()
    w_qkv_grad, *small1 = finish(me, two.sends, [(width, 3 * width), vector, vector],
                                 tiles_of(0, 3 * width, 0, False) + tiles_of(3 * width, 128, -2, True), n=n, us=0.2)
    flat = lambda v: v.reshape(-1)
    return (block_out, flat(loss), input_grad, flat(small1[0]), flat(small1[1]), w_qkv_grad, w_out_grad, flat(small[3]),
            flat(small[1]), flat(small[2]), w_up_grad, flat(small[4]), w_down_grad, flat(small[0]))

def solution(mesh):
    in_specs = (
        P(("rows", "bank"), None),
        P(("rows", "bank"), None),
        P(),
        P(),
        P(),
        P(),
        P(),
        P(),
        P(),
        P(),
        P(),
        P(),
        P(),
        P("bank", None),
        P("bank"),
        P(("rows", "bank")),
        P(("rows", "bank")),
    )
    out_specs = (
        P(("rows", "bank"), None),
        P(("rows", "bank")),
        P(("rows", "bank"), None),
        P(),
        P(),
        P(),
        P(),
        P(),
        P(),
        P(),
        P(),
        P(),
        P(),
        P(),
    )
    return jax.shard_map(functools.partial(body, mesh), mesh=mesh, in_specs=in_specs, out_specs=out_specs, check_vma=False)
```
